32 devices in a mesh: narrow: 4 (over y, x), wide: 8 (over z, core).
Axes of the slice: x: 2, y: 2, z: 4, core: 2. Of those that a mesh axis runs over, the one named last changes fastest.
Arguments:
- tokens: bfloat16 [8, 2048, 768], P('wide', 'narrow'), may hold values from -6 to 6
- condition: bfloat16 [8, 2, 128], P('wide'), may hold values from -6 to 6
- docs_per_row: int32 [8], P('wide'), may hold values from 1 to 2, as said below
- w_ada: bfloat16 [128, 4608], replicated, may hold values from -0.5 to 0.5
- b_ada: bfloat16 [4608], replicated, may hold values from -3 to 3
- gain_one: bfloat16 [768], replicated, may hold values from 0.25 to 1.75
- w_qkv: bfloat16 [768, 2304], replicated, may hold values from -0.21875 to 0.21875
- w_out: bfloat16 [768, 768], replicated, may hold values from -1.75 to 1.75
- gain_two: bfloat16 [768], replicated, may hold values from 0.25 to 1.75
- w_up: bfloat16 [768, 3072], replicated, may hold values from -0.21875 to 0.21875
- b_up: bfloat16 [3072], replicated, may hold values from -3 to 3
- w_down: bfloat16 [3072, 768], replicated, may hold values from -0.109375 to 0.109375
- b_down: bfloat16 [768], replicated, may hold values from -3 to 3
- cotangent: bfloat16 [8, 2048, 768], P('wide', 'narrow'), may hold values from -6 to 6
Outputs:
- output: bfloat16 [8, 2048, 768], P('wide', 'narrow')
- grad_tokens: float32 [8, 2048, 768], P('wide', 'narrow')
- grad_condition: float32 [8, 2, 128], P('wide')
- grad_w_ada: float32 [128, 4608], P(None, 'wide')
- grad_b_ada: float32 [4608], P('wide')
- grad_gain_one: float32 [768], P('wide')
- grad_w_qkv: float32 [768, 2304], P('wide')
- grad_w_out: float32 [768, 768], P('wide')
- grad_gain_two: float32 [768], P('wide')
- grad_w_up: float32 [768, 3072], P('wide')
- grad_b_up: float32 [3072], P('wide')
- grad_w_down: float32 [3072, 768], P('wide')
- grad_b_down: float32 [768], P('wide')
The draws below stay inside these ranges and needn't reach their ends.
Inputs may be any that keep to these rules, and one draw needn't show every extreme that they name: `docs_per_row`: each entry is 1 (the row is one sequence of 2048 tokens) or 2 (the row holds 2 sequences of 1024 tokens). In every draw the rows of some index of wide are all of the first kind and those of another index all of the second.
All inputs are finite; a program needn't handle non-finite values.
Results may differ from the reference program's by a relative error of at most 0.014.
The reference program's roundings to bfloat16 on the way count: a program that leaves them out, or rounds other values in their place, can miss the bound.
Values may be sent and summed in bfloat16 or wider, within the bound.
A program may use at most 192 MiB of HBM per device.

```python
import jax
import jax.numpy as jnp
from jax import lax

D = 768
HEADS = 12
HEAD_DIM = 64
FF = 3072
COND = 128
ROW_LEN = 2048
ROWS_DEV = 1
DOCS = 2
ROWS = 8


def draw_docs_per_row(key, part):
    key = jax.random.fold_in(key, 11)
    first, second, third = jax.random.split(key, 3)
    count = ROWS // ROWS_DEV
    kinds = jax.random.randint(first, (ROWS,), 0, 2)
    owner = jax.random.randint(second, (), 0, count)
    other = (owner + 1 + jax.random.randint(third, (), 0, count - 1)) % count
    holder = jnp.arange(ROWS, dtype=jnp.int32) // ROWS_DEV
    kinds = jnp.where(holder == owner, 0, kinds)
    kinds = jnp.where(holder == other, 1, kinds)
    return jnp.where(kinds == 1, DOCS, 1).astype(jnp.int32)


def steps_of(key, shape, shards, smallest, top_value):
    factor_of, own = 1.0, jax.random.fold_in(key, 6)
    for dim, shards_of in shards:
        draws = jnp.exp(jax.random.uniform(jax.random.fold_in(own, dim), (shards_of,), jnp.float32, smallest / len(shards), top_value / len(shards)))
        factor_of = factor_of * jnp.repeat(draws, shape[dim] // shards_of).reshape([-1 if axis == dim else 1 for axis in range(len(shape))])
    return factor_of


def normal_values(key, dims, scale, most, cuts=(), kind=jnp.bfloat16):
    result = scale * jax.random.normal(key, dims, jnp.float32)
    if cuts:
        result = result * steps_of(key, dims, cuts, -0.22, 0.18)
    return jnp.clip(result, -most, most).astype(kind)


def setup_inputs(seed: int = 0) -> dict:
    seeds = jax.random.split(jax.random.key(seed), 15)
    tokens = normal_values(seeds[0], (ROWS, ROW_LEN, D), 1.0, 6.0, ((0, 8), (1, 4)))
    condition = normal_values(seeds[1], (ROWS, DOCS, COND), 1.0, 6.0, ((0, 8),))
    docs_per_row = draw_docs_per_row(jax.random.fold_in(seeds[14], 71), 0)
    w_ada = normal_values(seeds[3], (COND, 6 * D), COND ** -0.5, 0.5)
    b_ada = normal_values(seeds[4], (6 * D,), 0.5, 3.0)
    gain_one = jnp.clip(1.0 + 0.15 * jax.random.normal(seeds[5], (D,), jnp.float32), 0.25, 1.75).astype(jnp.bfloat16)
    w_qkv = normal_values(seeds[6], (D, 3 * D), D ** -0.5, 0.21875)
    w_out = normal_values(seeds[7], (D, D), (max(D // 64, 1)) ** -0.5, 1.75)
    gain_two = jnp.clip(1.0 + 0.15 * jax.random.normal(seeds[8], (D,), jnp.float32), 0.25, 1.75).astype(jnp.bfloat16)
    w_up = normal_values(seeds[9], (D, FF), D ** -0.5, 0.21875)
    b_up = normal_values(seeds[10], (FF,), 0.5, 3.0)
    w_down = normal_values(seeds[11], (FF, D), FF ** -0.5, 0.109375)
    b_down = normal_values(seeds[12], (D,), 0.5, 3.0)
    cotangent = normal_values(seeds[13], (ROWS, ROW_LEN, D), 1.0, 6.0, ((0, 8), (1, 4)))
    return {"tokens": tokens, "condition": condition, "docs_per_row": docs_per_row, "w_ada": w_ada, "b_ada": b_ada, "gain_one": gain_one, "w_qkv": w_qkv, "w_out": w_out, "gain_two": gain_two, "w_up": w_up, "b_up": b_up, "w_down": w_down, "b_down": b_down, "cotangent": cotangent}


EPS = 1e-05
HIGH = lax.Precision.HIGHEST

@jax.custom_vjp
def low(v):
    return lax.optimization_barrier(v.astype(jnp.bfloat16)).astype(jnp.float32)

@jax.custom_vjp
def low_back(v):
    return v

def low_keep(v):
    return (low(v), None)

def low_pass(kept, grad):
    return (grad,)

def back_keep(v):
    return (v, None)

def back_low(kept, grad):
    return (low(grad),)
low.defvjp(low_keep, low_pass)
low_back.defvjp(back_keep, back_low)

def normalize(values):
    mean = lax.optimization_barrier(jnp.mean(values, axis=-1, keepdims=True))
    centred = values - mean
    spread = lax.optimization_barrier(jnp.mean(centred * centred, axis=-1, keepdims=True))
    return centred * lax.rsqrt(spread + EPS)

def modulated(values, gain, shift, scale):
    return normalize(values) * gain * (1.0 + scale) + shift

def gelu_tanh(values):
    return 0.5 * values * (1.0 + jnp.tanh(0.7978845608028654 * (values + 0.044715 * values * values * values)))

def rotate(values, cosine, sine):
    half = values.shape[-1] // 2
    turned = jnp.concatenate([-values[..., half:], values[..., :half]], axis=-1)
    return values * cosine + turned * sine

def angles(position, head_dim):
    freq = 10000.0 ** (-jnp.arange(head_dim // 2, dtype=jnp.float32) * 2.0 / head_dim)
    angle = position.astype(jnp.float32)[..., None] * freq
    angle = jnp.concatenate([angle, angle], axis=-1)
    return (jnp.cos(angle), jnp.sin(angle))

def head_attention(query, keys, values, same):
    scores = low_back(jnp.dot(query, keys.T, precision=HIGH) * HEAD_DIM ** (-0.5))
    scores = jnp.where(same, scores, -1e+30)
    probs = jax.nn.softmax(scores, axis=-1)
    return jnp.dot(low(probs), values, precision=HIGH)

def one_row(params, item):
    w_ada, b_ada, gain_one, w_qkv, w_out, gain_two, w_up, b_up, w_down, b_down = params
    tokens, condition, docs = item
    index = jnp.arange(ROW_LEN, dtype=jnp.int32)
    segment = index % docs
    position = index // docs
    cosine, sine = angles(position, HEAD_DIM)
    cosine = cosine[:, None, :]
    sine = sine[:, None, :]
    onehot = (segment[:, None] == jnp.arange(DOCS, dtype=jnp.int32)[None, :]).astype(jnp.float32)
    mods = jnp.dot(condition, w_ada, precision=HIGH) + b_ada
    per_token = jnp.dot(onehot, mods, precision=HIGH)
    shift_one, scale_one, gate_one, shift_two, scale_two, gate_two = jnp.split(per_token, 6, axis=-1)
    first = low(modulated(tokens, gain_one, shift_one, scale_one))
    projected = low_back(jnp.dot(first, w_qkv, precision=HIGH)).reshape(ROW_LEN, 3, HEADS, HEAD_DIM)
    query = low(low_back(rotate(projected[:, 0], cosine, sine)))
    keys = low(low_back(rotate(projected[:, 1], cosine, sine)))
    values = low(low_back(projected[:, 2]))
    same = segment[:, None] == segment[None, :]
    mixed = lax.map(lambda trio: head_attention(trio[0], trio[1], trio[2], same), (query.transpose(1, 0, 2), keys.transpose(1, 0, 2), values.transpose(1, 0, 2)))
    attended = low(low_back(mixed.transpose(1, 0, 2).reshape(ROW_LEN, D)))
    branch = low_back(jnp.dot(attended, w_out, precision=HIGH))
    middle = tokens + gate_one * branch
    second = low(modulated(middle, gain_two, shift_two, scale_two))
    hidden = low_back(jnp.dot(second, w_up, precision=HIGH) + b_up)
    active = low(gelu_tanh(hidden))
    down = low_back(jnp.dot(active, w_down, precision=HIGH) + b_down)
    return middle + gate_two * down

def layer(params, tokens, condition, docs):
    saved = jax.checkpoint(one_row)
    return lax.map(lambda item: saved(params, item), (tokens, condition, docs))

def reference(tokens, condition, docs_per_row, w_ada, b_ada, gain_one, w_qkv, w_out, gain_two, w_up, b_up, w_down, b_down, cotangent):
    params = tuple((weight.astype(jnp.float32) for weight in (w_ada, b_ada, gain_one, w_qkv, w_out, gain_two, w_up, b_up, w_down, b_down)))

    def run(weights, inputs, conds):
        return layer(weights, inputs, conds, docs_per_row)
    output, pullback = jax.vjp(run, params, tokens.astype(jnp.float32), condition.astype(jnp.float32))
    grad_params, grad_tokens, grad_condition = pullback(cotangent.astype(jnp.float32))
    return (output.astype(jnp.bfloat16), grad_tokens, grad_condition, grad_params[0], grad_params[1], grad_params[2], grad_params[3], grad_params[4], grad_params[5], grad_params[6], grad_params[7], grad_params[8], grad_params[9])
```

```python
import functools

import jax
import jax.numpy as jnp
import numpy as np
from jax import lax
from jax.experimental import pallas as pl
from jax.experimental.pallas import tpu as pltpu
from jax.sharding import PartitionSpec as P

D = 768
HEADS = 12
HEAD_DIM = 64
FF = 3072
DOCS = 2
EPS = 1e-05
LOG2E = 1.4426950408889634
BIG = 1e30
OWN = 3
WCOLS = 640
ROWS_G = 432
COLS_G = 384
MESH = pl.DeviceIdType.MESH
F32 = jnp.float32
BF16 = jnp.bfloat16
NN = (((1,), (0,)), ((), ()))
NT = (((1,), (1,)), ((), ()))
TN = (((0,), (0,)), ((), ()))
VMEM = pltpu.VMEM
ANY = pl.ANY


def dg(a, b, dims):
    return lax.dot_general(a, b, dims, preferred_element_type=F32)


def place():
    n = lax.axis_index("narrow")
    w = lax.axis_index("wide")
    return n, n // 2, lax.rem(n, 2), w // 2, lax.rem(w, 2)


def sibling(n, z, c):
    return (n, 2 * z + 1 - c)


def plane_barrier(n, z, c):
    barrier = pltpu.get_barrier_semaphore()
    me = n * 2 + c
    for step in range(1, 8):
        other = lax.rem(me + step, 8)
        pl.semaphore_signal(
            barrier, inc=1, device_id=(other // 2, 2 * z + lax.rem(other, 2)), device_id_type=MESH
        )
    pl.semaphore_wait(barrier, 7)


def remote(src, dst, send, recv, device):
    return pltpu.make_async_remote_copy(
        src_ref=src, dst_ref=dst, send_sem=send, recv_sem=recv, device_id=device, device_id_type=MESH
    )


def send_or_keep(is_self, src, dst, send, recv, device):
    @pl.when(is_self)
    def _():
        pltpu.make_async_copy(src, dst, recv).start()

    @pl.when(jnp.logical_not(is_self))
    def _():
        remote(src, dst, send, recv, device).start()


def wait_send_unless(is_self, src, dst, send, recv, device):
    @pl.when(jnp.logical_not(is_self))
    def _():
        remote(src, dst, send, recv, device).wait_send()


def wait_bytes(ref, sem):
    pltpu.make_async_copy(ref, ref, sem).wait()


def lane(shape):
    return lax.broadcasted_iota(jnp.int32, shape, len(shape) - 1)


def by8(values):
    return values.reshape(values.shape[0] // 8, 8, values.shape[1])


def flat8(values):
    return values.reshape(values.shape[0] * 8, values.shape[2])


def sum8(values):
    return jnp.sum(by8(values), axis=0)


def norm_stats(values):
    mean = jnp.mean(values, axis=-1, keepdims=True)
    centred = values - mean
    spread = jnp.mean(centred * centred, axis=-1, keepdims=True)
    inv = lax.rsqrt(spread + EPS)
    return centred * inv, inv


def halves_turn(values):
    where = lax.rem(lane(values.shape), 64) < 32
    return jnp.where(where, pltpu.roll(values, 96, 1), pltpu.roll(values, 32, 1))


def cos_sin(table):
    lanes = lane(table.shape)
    other = pltpu.roll(table, 64, 1)
    cosine = jnp.where(lanes < 64, table, other)
    sine = jnp.where(lanes < 64, other, table)
    return cosine, jnp.where(lax.rem(lanes, 64) < 32, -sine, sine)


def split3(column):
    high = column.astype(BF16).astype(F32)
    rest = column - high
    middle = rest.astype(BF16).astype(F32)
    low = (rest - middle).astype(BF16).astype(F32)
    return high, middle, low


def forward_kernel(
    docs_ref,
    tokens_ref,
    cond_ref,
    w_ada_ref,
    b_ada_ref,
    gain_ref,
    w_qkv_hbm,
    table_hbm,
    att_ref,
    all_ref,
    q_ref,
    k_ref,
    v_ref,
    pat_ref,
    own_ref,
    tab_ref,
    mine,
    gathered,
    w_qkv,
    tables,
    osend,
    oland,
    docs_mine,
    docs_other,
    load_sem,
    docs_sem,
    a_send,
    a_recv,
    f_send,
    f_recv,
    o_send,
    o_recv,
    all_sem,
):
    n, ny, nx, z, c = place()
    local = tokens_ref.shape[0]
    half = local // 2
    length = local * 4
    loads = [
        pltpu.make_async_copy(w_qkv_hbm, w_qkv, load_sem.at[0]),
        pltpu.make_async_copy(table_hbm, tables, load_sem.at[1]),
    ]
    for load in loads:
        load.start()
    docs_mine[...] = jnp.full(docs_mine.shape, docs_ref[0], jnp.int32).astype(F32)
    plane_barrier(n, z, c)
    docs_copy = remote(docs_mine, docs_other, docs_sem.at[0], docs_sem.at[1], sibling(n, z, c))
    docs_copy.start()

    two = docs_ref[0] == DOCS
    parity = lax.rem(lax.broadcasted_iota(jnp.int32, (16, 128), 0), 2)
    odd = jnp.logical_and(parity == 1, two)
    cond = cond_ref[...].astype(F32)
    cond16 = jnp.where(odd, cond[1:2, :], cond[0:1, :]).astype(BF16)
    pat_ref[...] = dg(cond16, w_ada_ref[...], NN)[:8] + b_ada_ref[...].astype(F32)

    shift = pat_ref[:, 0:D]
    amp = gain_ref[...].astype(F32) * (1.0 + pat_ref[:, D : 2 * D])

    def a_copy(my, hh):
        target = 2 * my + c
        is_self = jnp.logical_and(target == n, c == hh)
        return (
            is_self,
            mine.at[pl.ds(hh * half, half)],
            gathered.at[pl.ds(pl.multiple_of(n * local + hh * half, half), half)],
            a_send.at[my * 2 + hh],
            a_recv.at[n],
            (target, 2 * z + hh),
        )

    for hh in range(2):
        normed, _ = norm_stats(tokens_ref[hh * half : (hh + 1) * half, :].astype(F32))
        mine[hh * half : (hh + 1) * half, :] = flat8(by8(normed) * amp[None] + shift[None]).astype(
            BF16
        )
        for my in range(2):
            send_or_keep(*a_copy(my, hh))

    for load in loads:
        load.wait()
    group = 2 * ny + c
    lanes_w = lane((D, 128))

    def columns(part, j, at):
        col = part * HEADS + group * OWN + j
        block = w_qkv[:, pl.ds(pl.multiple_of((col // 2) * 128, 128), 128)].astype(F32)
        return pltpu.roll(block, lax.rem(col + at, 2) * 64, 1)

    for j in range(OWN):
        own_ref[:, j * 128 : (j + 1) * 128] = jnp.where(
            lanes_w < 64, columns(1, j, 0), columns(2, j, 1)
        ).astype(BF16)
    own_ref[:, 384:512] = jnp.where(lanes_w < 64, columns(0, 0, 0), columns(0, 1, 1)).astype(BF16)
    own_ref[:, 512:640] = jnp.where(lanes_w < 64, columns(0, 2, 0), 0.0).astype(BF16)

    docs_copy.wait()
    docs_heads = jnp.where(nx == c, docs_mine[...], docs_other[...])
    tab_ref[...] = jnp.where(docs_heads[0:1] == DOCS, tables[1], tables[0])

    lanes = lane((8, 128))
    odd8 = jnp.logical_and(parity[:8] == 1, docs_heads == DOCS)
    tail_q = jnp.where(lanes == 64, jnp.where(odd8, 0.0, 1.0), 0.0)
    tail_q = jnp.where(lanes == 65, jnp.where(odd8, 1.0, 0.0), tail_q)
    tail_k = jnp.where(lanes == 64, jnp.where(odd8, -BIG, 0.0), 0.0)
    tail_k = jnp.where(lanes == 65, jnp.where(odd8, 0.0, -BIG), tail_k)
    tail_k = jnp.where(jnp.logical_and(lanes >= 66, lanes < 69), 1.0, tail_k)

    def with_tail(values, tail):
        shaped = by8(values)
        return flat8(jnp.where(lane(shaped.shape) < 64, shaped, tail[None])).astype(BF16)

    def project(source):
        def step(i, carry):
            rows = pl.ds(pl.multiple_of(source * local + i * half, half), half)
            wide = dg(gathered[rows, :], own_ref[...], NN)
            cosine, sine = cos_sin(tab_ref[rows, :])

            def rot(values):
                return values * cosine + halves_turn(values) * sine

            for j in range(OWN):
                block = wide[:, j * 128 : (j + 1) * 128]
                k_ref[j, rows, :] = with_tail(rot(block), tail_k)
                v_ref[j, rows, :] = jnp.where(
                    lane(block.shape) < 64, pltpu.roll(block, 64, 1), 1.0
                ).astype(BF16)
            first = rot(wide[:, 384:512]) * HEAD_DIM**-0.5
            q_ref[0, rows, :] = with_tail(first, tail_q)
            q_ref[1, rows, :] = with_tail(pltpu.roll(first, 64, 1), tail_q)
            q_ref[2, rows, :] = with_tail(rot(wide[:, 512:640]) * HEAD_DIM**-0.5, tail_q)
            return carry

        lax.fori_loop(0, 2, step, 0)

    def part(source, hh):
        return gathered.at[pl.ds(pl.multiple_of(source * local + hh * half, half), half)]

    def forward(source):
        wait_bytes(part(source, c), a_recv.at[source])
        remote(
            part(source, c), part(source, c), f_send.at[source], f_recv.at[source], sibling(n, z, c)
        ).start()

    sources = [n, lax.rem(n + 2, 4), n + 1 - 2 * nx, lax.rem(n + 3 - 2 * nx, 4)]

    def arrive(source):
        wait_bytes(part(source, 1 - c), f_recv.at[source])
        project(source)

    forward(sources[0])
    forward(sources[1])
    arrive(sources[0])
    forward(sources[2])
    arrive(sources[1])
    forward(sources[3])
    arrive(sources[2])
    arrive(sources[3])
    keep = pltpu.make_async_copy(gathered, all_ref, all_sem)
    keep.start()

    def o_copy(j, quarter):
        is_self = jnp.logical_and(quarter == n, nx == c)
        return (
            is_self,
            osend.at[j, quarter],
            oland.at[group * OWN + j],
            o_send.at[j, quarter],
            o_recv.at[group * OWN + j],
            (quarter, 2 * z + nx),
        )

    def attend(index, carry):
        j = index // 4
        quarter = lax.rem(n + 3 - lax.rem(index, 4), 4)
        start = quarter * local
        scores = []
        for u in range(2):
            rows = pl.ds(pl.multiple_of(start + u * half, half), half)
            scores.append(dg(q_ref[j, rows, :], k_ref[j], NT))
        outs = []
        for u in range(2):
            rows = pl.ds(pl.multiple_of(start + u * half, half), half)
            top = jnp.max(scores[u], axis=1, keepdims=True)
            weights = jnp.exp2((scores[u] - top) * LOG2E)
            total = jnp.sum(weights, axis=1, keepdims=True)
            mixed = dg((weights * (1.0 / total)).astype(BF16), v_ref[j], NN)
            high, middle, low = split3(top + jnp.log(total))
            query = q_ref[j, rows, :].astype(F32)
            lanes_q = lane(query.shape)
            query = jnp.where(lanes_q == 66, -high, query)
            query = jnp.where(lanes_q == 67, -middle, query)
            q_ref[j, rows, :] = jnp.where(lanes_q == 68, -low, query).astype(BF16)
            outs.append(mixed)
        osend[j, quarter] = jnp.where(
            lane(outs[0].shape) < 64, outs[0], pltpu.roll(outs[1], 64, 1)
        ).astype(BF16)
        send_or_keep(*o_copy(j, quarter))
        return carry

    lax.fori_loop(0, OWN * 4, attend, 0)

    for head in range(HEADS):
        wait_bytes(oland.at[head], o_recv.at[head])
    for pair in range(HEADS // 2):
        even = oland[2 * pair].astype(F32)
        odd_head = oland[2 * pair + 1].astype(F32)
        low = lane(even.shape) < 64
        cols = slice(pair * 128, (pair + 1) * 128)
        att_ref[0:half, cols] = jnp.where(low, even, pltpu.roll(odd_head, 64, 1)).astype(BF16)
        att_ref[half:local, cols] = jnp.where(low, pltpu.roll(even, 64, 1), odd_head).astype(BF16)

    for hh in range(2):
        for my in range(2):
            wait_send_unless(*a_copy(my, hh))
    for source in range(4):
        remote(
            part(source, c), part(source, c), f_send.at[source], f_recv.at[source], sibling(n, z, c)
        ).wait_send()

    def drain(index, carry):
        wait_send_unless(*o_copy(index // 4, lax.rem(index, 4)))
        return carry

    lax.fori_loop(0, OWN * 4, drain, 0)
    keep.wait()


def vm():
    return pl.BlockSpec(memory_space=VMEM)


def hbm():
    return pl.BlockSpec(memory_space=ANY)


def smem():
    return pl.BlockSpec(memory_space=pltpu.SMEM)


def params(collective_id, limit=56):
    return pltpu.CompilerParams(
        collective_id=collective_id, has_side_effects=True, vmem_limit_bytes=limit * 2**20
    )


def dma(*shape):
    return pltpu.SemaphoreType.DMA(shape)


def call_forward(docs, tokens, cond, w_ada, b_ada, gain, w_qkv, table):
    local = tokens.shape[0]
    length = 4 * local
    half = local // 2
    sds = jax.ShapeDtypeStruct
    return pl.pallas_call(
        forward_kernel,
        out_shape=(
            sds((local, D), BF16),
            sds((length, D), BF16),
            sds((OWN, length, 128), BF16),
            sds((OWN, length, 128), BF16),
            sds((OWN, length, 128), BF16),
            sds((8, 6 * D), F32),
            sds((D, WCOLS), BF16),
            sds((length, 128), F32),
        ),
        in_specs=[smem(), vm(), vm(), vm(), vm(), vm(), hbm(), hbm()],
        out_specs=(vm(), hbm(), vm(), vm(), vm(), vm(), vm(), vm()),
        scratch_shapes=[
            VMEM((local, D), BF16),
            VMEM((length, D), BF16),
            VMEM((D, 3 * D), BF16),
            VMEM((2, length, 128), F32),
            VMEM((OWN, 4, half, 128), BF16),
            VMEM((HEADS, half, 128), BF16),
            VMEM((8, 128), F32),
            VMEM((8, 128), F32),
            dma(2),
            dma(2),
            dma(4),
            dma(4),
            dma(4),
            dma(4),
            dma(OWN, 4),
            dma(HEADS),
            pltpu.SemaphoreType.DMA,
        ],
        compiler_params=params(0),
        cost_estimate=pl.CostEstimate(flops=10**10, bytes_accessed=2 * 10**7, transcendentals=10**7),
    )(docs, tokens, cond, w_ada, b_ada, gain, w_qkv, table)


def rotary_table(length):
    freq = 10000.0 ** (-np.arange(HEAD_DIM // 2, dtype=np.float64) * 2.0 / HEAD_DIM)
    tables = []
    for docs in (1, DOCS):
        angle = (np.arange(length) // docs)[:, None] * freq[None, :]
        cosine, sine = np.cos(angle), np.sin(angle)
        tables.append(np.concatenate([cosine, cosine, sine, sine], axis=1))
    return np.stack(tables).astype(np.float32)


SMALL = 4 * D + FF + D


def middle_kernel(
    tokens_ref,
    cot_ref,
    att_ref,
    pat_ref,
    gain_ref,
    w_out_ref,
    w_up_ref,
    b_up_ref,
    w_down_ref,
    b_down_ref,
    out_ref,
    gmid_ref,
    g_ref,
    small_ref,
    do_ref,
    second_ref,
    active_ref,
    slope_ref,
    down_ref,
    gsecond_ref,
    middle_ref,
    branch_ref,
    lhs_t,
    gdown_ref,
    dsend,
    dland,
    d_send,
    d_recv,
):
    n, ny, nx, z, c = place()
    group = 2 * ny + c
    local = tokens_ref.shape[0]
    half = local // 2
    tile = 768
    plane_barrier(n, z, c)

    def piece(index):
        return pat_ref[:, index * D : (index + 1) * D]

    def spread(values, pattern):
        return flat8(by8(values) * pattern[None])

    branch_ref[...] = dg(att_ref[...], w_out_ref[...], NN)
    middle = tokens_ref[...].astype(F32) + spread(branch_ref[...], piece(2))
    middle_ref[...] = middle
    amp = gain_ref[...].astype(F32) * (1.0 + piece(4))
    normed, _ = norm_stats(middle)
    second = flat8(by8(normed) * amp[None] + piece(3)[None]).astype(BF16)
    second_ref[...] = second
    down_ref[...] = jnp.broadcast_to(b_down_ref[...].astype(F32), down_ref.shape)

    def up(t, carry):
        cols = pl.ds(pl.multiple_of(t * tile, tile), tile)
        hidden = dg(second_ref[...], w_up_ref[:, cols], NN) + b_up_ref[:, cols].astype(F32)
        square = hidden * hidden
        bend = jnp.tanh(0.7978845608028654 * hidden * (1.0 + 0.044715 * square))
        part = 0.5 * (1.0 + bend)
        active_ref[:, cols] = (hidden * part).astype(BF16)
        slope_ref[:, cols] = part + (0.5 * 0.7978845608028654) * hidden * (1.0 - bend * bend) * (
            1.0 + 3.0 * 0.044715 * square
        )
        down_ref[...] += dg(active_ref[:, cols], w_down_ref[cols, :], NN)
        return carry

    lax.fori_loop(0, FF // tile, up, 0)

    cot = cot_ref[...].astype(F32)
    down = down_ref[...]
    out_ref[...] = (middle_ref[...] + spread(down, piece(5))).astype(BF16)
    small_ref[:, 3 * D : 4 * D] = sum8(cot * down)
    gdown = spread(cot, piece(5)).astype(BF16)
    gdown_ref[...] = gdown
    small_ref[:, 4 * D + FF :] = sum8(gdown.astype(F32))
    lhs_t[0] = second_ref[...].T
    lhs_t[1] = gdown.T
    gsecond_ref[...] = jnp.zeros_like(gsecond_ref)

    def back(t, carry):
        cols = pl.ds(pl.multiple_of(t * tile, tile), tile)
        ghidden = dg(gdown_ref[...], w_down_ref[cols, :], NT) * slope_ref[:, cols]
        low = ghidden.astype(BF16)
        small_ref[:, pl.ds(pl.multiple_of(4 * D + t * tile, tile), tile)] = sum8(low.astype(F32))
        gsecond_ref[...] += dg(low, w_up_ref[:, cols], NT)
        gup = dg(lhs_t[0], low, NN).astype(BF16)
        for hh in range(2):
            g_ref[:, t, hh * 96 : (hh + 1) * 96, :] = gup[:, hh * 384 : (hh + 1) * 384].reshape(
                8, 96, 384
            )
        gdw = dg(lhs_t[1], active_ref[:, cols], NN).astype(BF16)
        for hh in range(2):
            g_ref[2 * t + hh, :, 192:384, :] = gdw[:, hh * 384 : (hh + 1) * 384].reshape(4, 192, 384)
        return carry

    lax.fori_loop(0, FF // tile, back, 0)

    normed, inv = norm_stats(middle_ref[...])
    gsecond = gsecond_ref[...]
    small_ref[:, D : 2 * D] = sum8(gsecond)
    small_ref[:, 2 * D : 3 * D] = sum8(gsecond * normed)
    amp = gain_ref[...].astype(F32) * (1.0 + piece(4))
    grad = spread(gsecond, amp)
    mean = jnp.mean(grad, axis=-1, keepdims=True)
    along = jnp.mean(grad * normed, axis=-1, keepdims=True)
    gmid = cot_ref[...].astype(F32) + (grad - mean - normed * along) * inv
    gmid_ref[...] = gmid
    small_ref[:, 0:D] = sum8(gmid * branch_ref[...])
    gbranch = spread(gmid, piece(2)).astype(BF16)
    gatt = dg(gbranch, w_out_ref[...], NT)

    def d_copy(quarter_x, pick_y, cc, j):
        target = 2 * pick_y + c
        head = (2 * pick_y + cc) * OWN + j
        is_self = jnp.logical_and(target == n, c == cc)
        return (
            is_self,
            dsend.at[head],
            dland.at[j, n],
            d_send.at[head],
            d_recv.at[j, n],
            (target, 2 * z + cc),
        )

    copies = []
    for pair in range(HEADS // 2):
        top = gatt[0:half, pair * 128 : (pair + 1) * 128]
        bottom = gatt[half:local, pair * 128 : (pair + 1) * 128]
        low = lane(top.shape) < 64
        dsend[2 * pair] = jnp.where(low, top, pltpu.roll(bottom, 64, 1)).astype(BF16)
        dsend[2 * pair + 1] = jnp.where(low, pltpu.roll(top, 64, 1), bottom).astype(BF16)
    for head in range(HEADS):
        copies.append(d_copy(None, head // OWN // 2, (head // OWN) % 2, head % OWN))
        send_or_keep(*copies[-1])

    for hh in range(2):
        gout = dg(att_ref[...], gbranch[:, hh * 384 : (hh + 1) * 384], TN).astype(BF16)
        shaped = gout.reshape(8, 2, 48, 384)
        for rh in range(2):
            g_ref[:, rh * 2 + hh, 384:432, :] = shaped[:, rh]

    for j in range(OWN):
        for quarter in range(4):
            wait_bytes(dland.at[j, quarter], d_recv.at[j, quarter])
    do_ref[...] = dland[...]
    for copy in copies:
        wait_send_unless(*copy)


def call_middle(tokens, cot, att, pat, gain, w_out, w_up, b_up, w_down, b_down):
    local = tokens.shape[0]
    half = local // 2
    sds = jax.ShapeDtypeStruct
    return pl.pallas_call(
        middle_kernel,
        out_shape=(
            sds((local, D), BF16),
            sds((local, D), F32),
            sds((8, 4, ROWS_G, COLS_G), BF16),
            sds((8, SMALL), F32),
            sds((OWN, 4, half, 128), BF16),
        ),
        in_specs=[vm()] * 10,
        out_specs=(vm(),) * 5,
        scratch_shapes=[
            VMEM((local, D), BF16),
            VMEM((local, FF), BF16),
            VMEM((local, FF), F32),
            VMEM((local, D), F32),
            VMEM((local, D), F32),
            VMEM((local, D), F32),
            VMEM((local, D), F32),
            VMEM((2, D, local), BF16),
            VMEM((local, D), BF16),
            VMEM((HEADS, half, 128), BF16),
            VMEM((OWN, 4, half, 128), BF16),
            dma(HEADS),
            dma(OWN, 4),
        ],
        compiler_params=params(1, 60),
        cost_estimate=pl.CostEstimate(flops=2 * 10**10, bytes_accessed=3 * 10**7, transcendentals=10**7),
    )(tokens, cot, att, pat, gain, w_out, w_up, b_up, w_down, b_down)


def backward_kernel(
    tokens_ref,
    pat_ref,
    gain_ref,
    gmid_ref,
    do_ref,
    q_ref,
    k_ref,
    v_ref,
    all_ref,
    own_ref,
    tab_ref,
    gtok_ref,
    gq_ref,
    small_ref,
    packed,
    acc_k,
    acc_v,
    acc_w,
    kept,
    csend,
    cland,
    rsend,
    rland,
    c_send,
    c_recv,
    r_send,
    r_recv,
):
    n, ny, nx, z, c = place()
    local = tokens_ref.shape[0]
    half = local // 2
    length = 4 * local
    plane_barrier(n, z, c)
    lanes = lane((local, 128))

    def turned(values, rows):
        cosine, sine = cos_sin(tab_ref[rows, :])
        return values * cosine - halves_turn(values) * sine

    def rounded(values):
        return values.astype(BF16).astype(F32)

    for j in range(OWN):
        acc_k[...] = jnp.zeros_like(acc_k)
        acc_v[...] = jnp.zeros_like(acc_v)

        def quarter_step(i, carry):
            rows = pl.ds(pl.multiple_of(i * local, local), local)
            block = do_ref[j, i].astype(F32)
            grad = jnp.concatenate([block, pltpu.roll(block, 64, 1)], axis=0)
            grad = jnp.where(lanes < 64, grad, 0.0).astype(BF16)
            query = q_ref[j, rows, :]
            probs = jnp.exp2(dg(query, k_ref[j], NT) * LOG2E)
            gprobs = probs * dg(grad, v_ref[j], NT)
            scores = (gprobs - probs * jnp.sum(gprobs, axis=1, keepdims=True)).astype(BF16)
            probs = probs.astype(BF16)
            gquery = rounded(dg(scores, k_ref[j], NN) * HEAD_DIM**-0.5)
            at = 384 + 64 * j
            packed[rows, at : at + 64] = turned(gquery, rows)[:, :64].astype(BF16)
            acc_v[...] += dg(grad.T[:64], probs, NN)
            acc_k[...] += dg(query.T[:64], scores, NN)
            return carry

        lax.fori_loop(0, 4, quarter_step, 0)

        def finish(i, carry):
            rows = pl.ds(pl.multiple_of(i * local, local), local)
            both = jnp.concatenate([acc_k[:, rows], acc_v[:, rows]], axis=0).T
            both = rounded(both)
            packed[rows, j * 128 : (j + 1) * 128] = jnp.where(
                lanes < 64, turned(both, rows), both
            ).astype(BF16)
            return carry

        lax.fori_loop(0, 4, finish, 0)
    packed[:, 576:640] = jnp.zeros((length, 64), BF16)

    def rows_of(quarter, hh):
        return pl.ds(pl.multiple_of(quarter * local + hh * half, half), half)

    def c_copy(quarter):
        return remote(
            csend.at[quarter], cland.at[quarter], c_send.at[quarter], c_recv.at[quarter],
            sibling(n, z, c),
        )

    def r_copy(quarter):
        is_self = jnp.logical_and(quarter == n, nx == c)
        return (
            is_self,
            rsend.at[quarter],
            rland.at[ny, pl.ds(pl.multiple_of(c * half, half), half)],
            r_send.at[quarter],
            r_recv.at[ny, c],
            (quarter, 2 * z + nx),
        )

    def order(i):
        return lax.rem(n + 3 - i, 4)

    def give(i, carry):
        quarter = order(i)
        csend[quarter] = dg(packed[rows_of(quarter, 1 - c), :], own_ref[...], NT).astype(BF16)
        c_copy(quarter).start()
        return carry

    lax.fori_loop(0, 4, give, 0)

    def keep(i, carry):
        quarter = order(i)
        kept[quarter] = dg(packed[rows_of(quarter, c), :], own_ref[...], NT)
        return carry

    lax.fori_loop(0, 4, keep, 0)

    def add(i, carry):
        quarter = order(i)
        wait_bytes(cland.at[quarter], c_recv.at[quarter])
        rsend[quarter] = (kept[quarter] + cland[quarter].astype(F32)).astype(BF16)
        send_or_keep(*r_copy(quarter))
        return carry

    lax.fori_loop(0, 4, add, 0)

    acc_w[...] = jnp.zeros_like(acc_w)

    def weights(i, carry):
        rows = pl.ds(pl.multiple_of(i * local, local), local)
        acc_w[...] += dg(all_ref[rows, :], packed[rows, :], TN)
        return carry

    lax.fori_loop(0, 4, weights, 0)
    gq_ref[...] = acc_w[...].astype(BF16).reshape(gq_ref.shape)

    normed, inv = norm_stats(tokens_ref[...].astype(F32))
    for y in range(2):
        for hh in range(2):
            wait_bytes(rland.at[y, pl.ds(hh * half, half)], r_recv.at[y, hh])
    gfirst = rland[0].astype(F32) + rland[1].astype(F32)
    small_ref[:, 0:D] = sum8(gfirst)
    small_ref[:, D : 2 * D] = sum8(gfirst * normed)
    amp = gain_ref[...].astype(F32) * (1.0 + pat_ref[:, D : 2 * D])
    grad = flat8(by8(gfirst) * amp[None])
    mean = jnp.mean(grad, axis=-1, keepdims=True)
    along = jnp.mean(grad * normed, axis=-1, keepdims=True)
    gtok_ref[...] = gmid_ref[...] + (grad - mean - normed * along) * inv

    def drain(quarter, carry):
        c_copy(quarter).wait_send()
        wait_send_unless(*r_copy(quarter))
        return carry

    lax.fori_loop(0, 4, drain, 0)


def call_backward(tokens, pat, gain, gmid, do, q, k, v, everything, own, tab):
    local = tokens.shape[0]
    half = local // 2
    length = 4 * local
    sds = jax.ShapeDtypeStruct
    return pl.pallas_call(
        backward_kernel,
        out_shape=(
            sds((local, D), F32),
            sds((8, 96, WCOLS), BF16),
            sds((8, 2 * D), F32),
        ),
        in_specs=[vm()] * 11,
        out_specs=(vm(),) * 3,
        scratch_shapes=[
            VMEM((length, WCOLS), BF16),
            VMEM((64, length), F32),
            VMEM((64, length), F32),
            VMEM((D, WCOLS), F32),
            VMEM((4, half, D), F32),
            VMEM((4, half, D), BF16),
            VMEM((4, half, D), BF16),
            VMEM((4, half, D), BF16),
            VMEM((2, local, D), BF16),
            dma(4),
            dma(4),
            dma(4),
            dma(2, 2),
        ],
        compiler_params=params(2, 60),
        cost_estimate=pl.CostEstimate(flops=2 * 10**10, bytes_accessed=3 * 10**7, transcendentals=10**7),
    )(tokens, pat, gain, gmid, do, q, k, v, everything, own, tab)


def plain_sums(g, gq, own_ids):
    n, z, c = own_ids
    up = g[:, :, :192].reshape(8, 4, 2, 96, 384).transpose(0, 3, 1, 2, 4).reshape(D, FF)
    down = g[:, :, 192:384].reshape(8, D, 384).transpose(0, 2, 1).reshape(FF, D)
    out = g[:, :, 384:].reshape(8, 2, 2, 48, 384).transpose(0, 1, 3, 2, 4).reshape(D, D)
    flat = gq.reshape(D, WCOLS)
    pieces = [flat[:, 384:576]]
    pieces.append(jnp.concatenate([flat[:, j * 128 : j * 128 + 64] for j in range(OWN)], axis=1))
    pieces.append(jnp.concatenate([flat[:, j * 128 + 64 : j * 128 + 128] for j in range(OWN)], axis=1))
    group = 2 * (n // 2) + c
    whole = jnp.zeros((D, 3, 4, OWN * HEAD_DIM), F32)
    for part in range(3):
        whole = lax.dynamic_update_slice(
            whole, pieces[part].astype(F32)[:, None, None, :], (0, part, group, 0)
        )
    whole = whole.reshape(D, 3 * D)

    def total(values):
        share = lax.psum_scatter(values.astype(F32), "wide", scatter_dimension=0, tiled=True)
        return lax.psum(share, "narrow")

    return total(whole), total(out), total(up), total(down)


def body(
    tokens,
    condition,
    docs_per_row,
    w_ada,
    b_ada,
    gain_one,
    w_qkv,
    w_out,
    gain_two,
    w_up,
    b_up,
    w_down,
    b_down,
    cotangent,
):
    local = tokens.shape[1]
    x = tokens.reshape(local, D)
    cot = cotangent.reshape(local, D)
    cond = condition.reshape(DOCS, -1)
    table = jnp.asarray(rotary_table(4 * local))

    def line(vector):
        return vector.reshape(1, -1)

    att, everything, q, k, v, pat, own, tab = call_forward(
        docs_per_row, x, cond, w_ada, line(b_ada), line(gain_one), w_qkv, table
    )
    output, gmid, g, small_two, do = call_middle(
        x, cot, att, pat, line(gain_two), w_out, w_up, line(b_up), w_down, line(b_down)
    )
    gtok, gq, small_one = call_backward(
        x, pat, line(gain_one), gmid, do, q, k, v, everything, own, tab
    )
    n, w = lax.axis_index("narrow"), lax.axis_index("wide")
    sum_qkv, sum_out, sum_up, sum_down = plain_sums(g, gq, (n, w // 2, w % 2))

    small = jnp.concatenate([small_one, small_two], axis=1).reshape(4, 2, -1).sum(0)
    small = lax.psum(small, "narrow")
    shift_one, raw_one, gate_one, shift_two, raw_two, gate_two = jnp.split(small[:, : 6 * D], 6, axis=1)
    scales = pat[:2].reshape(2, 6, D)
    sum_gain_one = jnp.sum(raw_one * (1.0 + scales[:, 1]), axis=0)
    sum_gain_two = jnp.sum(raw_two * (1.0 + scales[:, 4]), axis=0)
    grads = jnp.concatenate(
        [
            shift_one,
            raw_one * gain_one.astype(F32),
            gate_one,
            shift_two,
            raw_two * gain_two.astype(F32),
            gate_two,
        ],
        axis=1,
    )
    two = docs_per_row[0] == DOCS
    grad_mods = jnp.stack(
        [jnp.where(two, grads[0], grads[0] + grads[1]), jnp.where(two, grads[1], 0.0)]
    )
    high = lax.Precision.HIGHEST
    grad_condition = jnp.einsum("sm,cm->sc", grad_mods, w_ada.astype(F32), precision=high)[None]
    part_ada = jnp.einsum("sm,sc->mc", grad_mods, cond.astype(F32), precision=high)

    def share(values):
        return lax.psum_scatter(values, "wide", scatter_dimension=0, tiled=True)

    sum_b_up = jnp.sum(small[:, 6 * D : 6 * D + FF], axis=0)
    sum_b_down = jnp.sum(small[:, 6 * D + FF :], axis=0)
    return (
        output[None],
        gtok[None],
        grad_condition,
        share(part_ada).T,
        share(jnp.sum(grad_mods, axis=0)),
        share(sum_gain_one),
        sum_qkv,
        sum_out,
        share(sum_gain_two),
        sum_up,
        share(sum_b_up),
        sum_down,
        share(sum_b_down),
    )


def solution(mesh):
    in_specs = (
        P("wide", "narrow", None),
        P("wide", None, None),
        P("wide"),
        P(),
        P(),
        P(),
        P(),
        P(),
        P(),
        P(),
        P(),
        P(),
        P(),
        P("wide", "narrow", None),
    )
    out_specs = (
        P("wide", "narrow", None),
        P("wide", "narrow", None),
        P("wide", None, None),
        P(None, "wide"),
        P("wide"),
        P("wide"),
        P("wide", None),
        P("wide", None),
        P("wide"),
        P("wide", None),
        P("wide"),
        P("wide", None),
        P("wide"),
    )
    return jax.shard_map(body, mesh=mesh, in_specs=in_specs, out_specs=out_specs, check_vma=False)
```

```python
import functools

import jax
import jax.numpy as jnp
import numpy as np
from jax import lax
from jax.experimental import pallas as pl
from jax.experimental.pallas import tpu as pltpu
from jax.sharding import PartitionSpec as P

D = 768
HEADS = 12
HEAD_DIM = 64
FF = 3072
DOCS = 2
EPS = 1e-05
LOG2E = 1.4426950408889634
BIG = 1e30
OWN = 3
WCOLS = 640
ROWS_G = 432
COLS_G = 384
MESH = pl.DeviceIdType.MESH
F32 = jnp.float32
BF16 = jnp.bfloat16
NN = (((1,), (0,)), ((), ()))
NT = (((1,), (1,)), ((), ()))
TN = (((0,), (0,)), ((), ()))
VMEM = pltpu.VMEM
ANY = pl.ANY


def dg(a, b, dims):
    return lax.dot_general(a, b, dims, preferred_element_type=F32)


def place():
    n = lax.axis_index("narrow")
    w = lax.axis_index("wide")
    return n, n // 2, lax.rem(n, 2), w // 2, lax.rem(w, 2)


def sibling(n, z, c):
    return (n, 2 * z + 1 - c)


def plane_barrier(n, z, c):
    barrier = pltpu.get_barrier_semaphore()
    me = n * 2 + c
    for step in range(1, 8):
        other = lax.rem(me + step, 8)
        pl.semaphore_signal(
            barrier, inc=1, device_id=(other // 2, 2 * z + lax.rem(other, 2)), device_id_type=MESH
        )
    pl.semaphore_wait(barrier, 7)


def remote(src, dst, send, recv, device):
    return pltpu.make_async_remote_copy(
        src_ref=src, dst_ref=dst, send_sem=send, recv_sem=recv, device_id=device, device_id_type=MESH
    )


def send_or_keep(is_self, src, dst, send, recv, device):
    @pl.when(is_self)
    def _():
        pltpu.make_async_copy(src, dst, recv).start()

    @pl.when(jnp.logical_not(is_self))
    def _():
        remote(src, dst, send, recv, device).start()


def wait_send_unless(is_self, src, dst, send, recv, device):
    @pl.when(jnp.logical_not(is_self))
    def _():
        remote(src, dst, send, recv, device).wait_send()


def wait_bytes(ref, sem):
    pltpu.make_async_copy(ref, ref, sem).wait()


def lane(shape):
    return lax.broadcasted_iota(jnp.int32, shape, len(shape) - 1)


def by8(values):
    return values.reshape(values.shape[0] // 8, 8, values.shape[1])


def flat8(values):
    return values.reshape(values.shape[0] * 8, values.shape[2])


def sum8(values):
    return jnp.sum(by8(values), axis=0)


def norm_stats(values):
    mean = jnp.mean(values, axis=-1, keepdims=True)
    centred = values - mean
    spread = jnp.mean(centred * centred, axis=-1, keepdims=True)
    inv = lax.rsqrt(spread + EPS)
    return centred * inv, inv


def halves_turn(values):
    where = lax.rem(lane(values.shape), 64) < 32
    return jnp.where(where, pltpu.roll(values, 96, 1), pltpu.roll(values, 32, 1))


def cos_sin(table):
    lanes = lane(table.shape)
    other = pltpu.roll(table, 64, 1)
    cosine = jnp.where(lanes < 64, table, other)
    sine = jnp.where(lanes < 64, other, table)
    return cosine, jnp.where(lax.rem(lanes, 64) < 32, -sine, sine)


def split3(column):
    high = column.astype(BF16).astype(F32)
    rest = column - high
    middle = rest.astype(BF16).astype(F32)
    low = (rest - middle).astype(BF16).astype(F32)
    return high, middle, low


def forward_kernel(
    docs_ref,
    tokens_ref,
    cond_ref,
    w_ada_ref,
    b_ada_ref,
    gain_ref,
    w_qkv_hbm,
    table_hbm,
    att_ref,
    all_ref,
    q_ref,
    k_ref,
    v_ref,
    pat_ref,
    own_ref,
    tab_ref,
    mine,
    gathered,
    w_qkv,
    tables,
    osend,
    oland,
    docs_mine,
    docs_other,
    load_sem,
    docs_sem,
    a_send,
    a_recv,
    f_send,
    f_recv,
    o_send,
    o_recv,
    all_sem,
):
    n, ny, nx, z, c = place()
    local = tokens_ref.shape[0]
    half = local // 2
    length = local * 4
    loads = [
        pltpu.make_async_copy(w_qkv_hbm, w_qkv, load_sem.at[0]),
        pltpu.make_async_copy(table_hbm, tables, load_sem.at[1]),
    ]
    for load in loads:
        load.start()
    docs_mine[...] = jnp.full(docs_mine.shape, docs_ref[0], jnp.int32).astype(F32)
    plane_barrier(n, z, c)
    docs_copy = remote(docs_mine, docs_other, docs_sem.at[0], docs_sem.at[1], sibling(n, z, c))
    docs_copy.start()

    two = docs_ref[0] == DOCS
    parity = lax.rem(lax.broadcasted_iota(jnp.int32, (16, 128), 0), 2)
    odd = jnp.logical_and(parity == 1, two)
    cond = cond_ref[...].astype(F32)
    cond16 = jnp.where(odd, cond[1:2, :], cond[0:1, :]).astype(BF16)
    pat_ref[...] = dg(cond16, w_ada_ref[...], NN)[:8] + b_ada_ref[...].astype(F32)

    shift = pat_ref[:, 0:D]
    amp = gain_ref[...].astype(F32) * (1.0 + pat_ref[:, D : 2 * D])

    def a_copy(my, hh):
        target = 2 * my + c
        is_self = jnp.logical_and(target == n, c == hh)
        return (
            is_self,
            mine.at[pl.ds(hh * half, half)],
            gathered.at[pl.ds(pl.multiple_of(n * local + hh * half, half), half)],
            a_send.at[my * 2 + hh],
            a_recv.at[n],
            (target, 2 * z + hh),
        )

    for hh in range(2):
        normed, _ = norm_stats(tokens_ref[hh * half : (hh + 1) * half, :].astype(F32))
        mine[hh * half : (hh + 1) * half, :] = flat8(by8(normed) * amp[None] + shift[None]).astype(
            BF16
        )
        for my in range(2):
            send_or_keep(*a_copy(my, hh))

    for load in loads:
        load.wait()
    group = 2 * ny + c
    lanes_w = lane((D, 128))

    def columns(part, j, at):
        col = part * HEADS + group * OWN + j
        block = w_qkv[:, pl.ds(pl.multiple_of((col // 2) * 128, 128), 128)].astype(F32)
        return pltpu.roll(block, lax.rem(col + at, 2) * 64, 1)

    for j in range(OWN):
        own_ref[:, j * 128 : (j + 1) * 128] = jnp.where(
            lanes_w < 64, columns(1, j, 0), columns(2, j, 1)
        ).astype(BF16)
    own_ref[:, 384:512] = jnp.where(lanes_w < 64, columns(0, 0, 0), columns(0, 1, 1)).astype(BF16)
    own_ref[:, 512:640] = jnp.where(lanes_w < 64, columns(0, 2, 0), 0.0).astype(BF16)

    docs_copy.wait()
    docs_heads = jnp.where(nx == c, docs_mine[...], docs_other[...])
    tab_ref[...] = jnp.where(docs_heads[0:1] == DOCS, tables[1], tables[0])

    lanes = lane((8, 128))
    odd8 = jnp.logical_and(parity[:8] == 1, docs_heads == DOCS)
    tail_q = jnp.where(lanes == 64, jnp.where(odd8, 0.0, 1.0), 0.0)
    tail_q = jnp.where(lanes == 65, jnp.where(odd8, 1.0, 0.0), tail_q)
    tail_k = jnp.where(lanes == 64, jnp.where(odd8, -BIG, 0.0), 0.0)
    tail_k = jnp.where(lanes == 65, jnp.where(odd8, 0.0, -BIG), tail_k)
    tail_k = jnp.where(jnp.logical_and(lanes >= 66, lanes < 69), 1.0, tail_k)

    def with_tail(values, tail):
        shaped = by8(values)
        return flat8(jnp.where(lane(shaped.shape) < 64, shaped, tail[None])).astype(BF16)

    def project(source):
        def step(i, carry):
            rows = pl.ds(pl.multiple_of(source * local + i * half, half), half)
            wide = dg(gathered[rows, :], own_ref[...], NN)
            cosine, sine = cos_sin(tab_ref[rows, :])

            def rot(values):
                return values * cosine + halves_turn(values) * sine

            for j in range(OWN):
                block = wide[:, j * 128 : (j + 1) * 128]
                k_ref[j, rows, :] = with_tail(rot(block), tail_k)
                v_ref[j, rows, :] = jnp.where(
                    lane(block.shape) < 64, pltpu.roll(block, 64, 1), 1.0
                ).astype(BF16)
            first = rot(wide[:, 384:512]) * HEAD_DIM**-0.5
            q_ref[0, rows, :] = with_tail(first, tail_q)
            q_ref[1, rows, :] = with_tail(pltpu.roll(first, 64, 1), tail_q)
            q_ref[2, rows, :] = with_tail(rot(wide[:, 512:640]) * HEAD_DIM**-0.5, tail_q)
            return carry

        lax.fori_loop(0, 2, step, 0)

    def part(source, hh):
        return gathered.at[pl.ds(pl.multiple_of(source * local + hh * half, half), half)]

    def forward(source):
        wait_bytes(part(source, c), a_recv.at[source])
        remote(
            part(source, c), part(source, c), f_send.at[source], f_recv.at[source], sibling(n, z, c)
        ).start()

    sources = [n, lax.rem(n + 2, 4), n + 1 - 2 * nx, lax.rem(n + 3 - 2 * nx, 4)]

    def arrive(source):
        wait_bytes(part(source, 1 - c), f_recv.at[source])
        project(source)

    forward(sources[0])
    forward(sources[1])
    arrive(sources[0])
    forward(sources[2])
    arrive(sources[1])
    forward(sources[3])
    arrive(sources[2])
    arrive(sources[3])
    keep = pltpu.make_async_copy(gathered, all_ref, all_sem)
    keep.start()

    def o_copy(j, quarter):
        is_self = jnp.logical_and(quarter == n, nx == c)
        return (
            is_self,
            osend.at[j, quarter],
            oland.at[group * OWN + j],
            o_send.at[j, quarter],
            o_recv.at[group * OWN + j],
            (quarter, 2 * z + nx),
        )

    def attend(index, carry):
        j = index // 4
        quarter = lax.rem(n + 3 - lax.rem(index, 4), 4)
        start = quarter * local
        scores = []
        for u in range(2):
            rows = pl.ds(pl.multiple_of(start + u * half, half), half)
            scores.append(dg(q_ref[j, rows, :], k_ref[j], NT))
        outs = []
        for u in range(2):
            rows = pl.ds(pl.multiple_of(start + u * half, half), half)
            top = jnp.max(scores[u], axis=1, keepdims=True)
            weights = jnp.exp2((scores[u] - top) * LOG2E)
            total = jnp.sum(weights, axis=1, keepdims=True)
            mixed = dg((weights * (1.0 / total)).astype(BF16), v_ref[j], NN)
            high, middle, low = split3(top + jnp.log(total))
            query = q_ref[j, rows, :].astype(F32)
            lanes_q = lane(query.shape)
            query = jnp.where(lanes_q == 66, -high, query)
            query = jnp.where(lanes_q == 67, -middle, query)
            q_ref[j, rows, :] = jnp.where(lanes_q == 68, -low, query).astype(BF16)
            outs.append(mixed)
        osend[j, quarter] = jnp.where(
            lane(outs[0].shape) < 64, outs[0], pltpu.roll(outs[1], 64, 1)
        ).astype(BF16)
        send_or_keep(*o_copy(j, quarter))
        return carry

    lax.fori_loop(0, OWN * 4, attend, 0)

    for head in range(HEADS):
        wait_bytes(oland.at[head], o_recv.at[head])
    for pair in range(HEADS // 2):
        even = oland[2 * pair].astype(F32)
        odd_head = oland[2 * pair + 1].astype(F32)
        low = lane(even.shape) < 64
        cols = slice(pair * 128, (pair + 1) * 128)
        att_ref[0:half, cols] = jnp.where(low, even, pltpu.roll(odd_head, 64, 1)).astype(BF16)
        att_ref[half:local, cols] = jnp.where(low, pltpu.roll(even, 64, 1), odd_head).astype(BF16)

    for hh in range(2):
        for my in range(2):
            wait_send_unless(*a_copy(my, hh))
    for source in range(4):
        remote(
            part(source, c), part(source, c), f_send.at[source], f_recv.at[source], sibling(n, z, c)
        ).wait_send()

    def drain(index, carry):
        wait_send_unless(*o_copy(index // 4, lax.rem(index, 4)))
        return carry

    lax.fori_loop(0, OWN * 4, drain, 0)
    keep.wait()


def vm():
    return pl.BlockSpec(memory_space=VMEM)


def hbm():
    return pl.BlockSpec(memory_space=ANY)


def smem():
    return pl.BlockSpec(memory_space=pltpu.SMEM)


def params(collective_id, limit=56):
    return pltpu.CompilerParams(
        collective_id=collective_id, has_side_effects=True, vmem_limit_bytes=limit * 2**20
    )


def dma(*shape):
    return pltpu.SemaphoreType.DMA(shape)


def call_forward(docs, tokens, cond, w_ada, b_ada, gain, w_qkv, table):
    local = tokens.shape[0]
    length = 4 * local
    half = local // 2
    sds = jax.ShapeDtypeStruct
    return pl.pallas_call(
        forward_kernel,
        out_shape=(
            sds((local, D), BF16),
            sds((length, D), BF16),
            sds((OWN, length, 128), BF16),
            sds((OWN, length, 128), BF16),
            sds((OWN, length, 128), BF16),
            sds((8, 6 * D), F32),
            sds((D, WCOLS), BF16),
            sds((length, 128), F32),
        ),
        in_specs=[smem(), vm(), vm(), vm(), vm(), vm(), hbm(), hbm()],
        out_specs=(vm(), hbm(), vm(), vm(), vm(), vm(), vm(), vm()),
        scratch_shapes=[
            VMEM((local, D), BF16),
            VMEM((length, D), BF16),
            VMEM((D, 3 * D), BF16),
            VMEM((2, length, 128), F32),
            VMEM((OWN, 4, half, 128), BF16),
            VMEM((HEADS, half, 128), BF16),
            VMEM((8, 128), F32),
            VMEM((8, 128), F32),
            dma(2),
            dma(2),
            dma(4),
            dma(4),
            dma(4),
            dma(4),
            dma(OWN, 4),
            dma(HEADS),
            pltpu.SemaphoreType.DMA,
        ],
        compiler_params=params(0),
        cost_estimate=pl.CostEstimate(flops=10**10, bytes_accessed=2 * 10**7, transcendentals=10**7),
    )(docs, tokens, cond, w_ada, b_ada, gain, w_qkv, table)


def rotary_table(length):
    freq = 10000.0 ** (-np.arange(HEAD_DIM // 2, dtype=np.float64) * 2.0 / HEAD_DIM)
    tables = []
    for docs in (1, DOCS):
        angle = (np.arange(length) // docs)[:, None] * freq[None, :]
        cosine, sine = np.cos(angle), np.sin(angle)
        tables.append(np.concatenate([cosine, cosine, sine, sine], axis=1))
    return np.stack(tables).astype(np.float32)


SMALL = 4 * D + FF + D


def middle_kernel(
    tokens_ref,
    cot_ref,
    att_ref,
    pat_ref,
    gain_ref,
    w_out_ref,
    w_up_ref,
    b_up_ref,
    w_down_ref,
    b_down_ref,
    out_ref,
    gmid_ref,
    g_ref,
    small_ref,
    do_ref,
    second_ref,
    active_ref,
    slope_ref,
    down_ref,
    gsecond_ref,
    middle_ref,
    branch_ref,
    lhs_t,
    gdown_ref,
    dsend,
    dland,
    d_send,
    d_recv,
):
    n, ny, nx, z, c = place()
    group = 2 * ny + c
    local = tokens_ref.shape[0]
    half = local // 2
    tile = 768
    plane_barrier(n, z, c)

    def piece(index):
        return pat_ref[:, index * D : (index + 1) * D]

    def spread(values, pattern):
        return flat8(by8(values) * pattern[None])

    branch_ref[...] = dg(att_ref[...], w_out_ref[...], NN)
    middle = tokens_ref[...].astype(F32) + spread(branch_ref[...], piece(2))
    middle_ref[...] = middle
    amp = gain_ref[...].astype(F32) * (1.0 + piece(4))
    normed, _ = norm_stats(middle)
    second = flat8(by8(normed) * amp[None] + piece(3)[None]).astype(BF16)
    second_ref[...] = second
    down_ref[...] = jnp.broadcast_to(b_down_ref[...].astype(F32), down_ref.shape)

    def up(t, carry):
        cols = pl.ds(pl.multiple_of(t * tile, tile), tile)
        hidden = dg(second_ref[...], w_up_ref[:, cols], NN) + b_up_ref[:, cols].astype(F32)
        square = hidden * hidden
        bend = jnp.tanh(0.7978845608028654 * hidden * (1.0 + 0.044715 * square))
        part = 0.5 * (1.0 + bend)
        active_ref[:, cols] = (hidden * part).astype(BF16)
        slope_ref[:, cols] = part + (0.5 * 0.7978845608028654) * hidden * (1.0 - bend * bend) * (
            1.0 + 3.0 * 0.044715 * square
        )
        down_ref[...] += dg(active_ref[:, cols], w_down_ref[cols, :], NN)
        return carry

    lax.fori_loop(0, FF // tile, up, 0)

    cot = cot_ref[...].astype(F32)
    down = down_ref[...]
    out_ref[...] = (middle_ref[...] + spread(down, piece(5))).astype(BF16)
    small_ref[:, 3 * D : 4 * D] = sum8(cot * down)
    gdown = spread(cot, piece(5)).astype(BF16)
    gdown_ref[...] = gdown
    small_ref[:, 4 * D + FF :] = sum8(gdown.astype(F32))
    lhs_t[0] = second_ref[...].T
    lhs_t[1] = gdown.T
    gsecond_ref[...] = jnp.zeros_like(gsecond_ref)

    def back(t, carry):
        cols = pl.ds(pl.multiple_of(t * tile, tile), tile)
        ghidden = dg(gdown_ref[...], w_down_ref[cols, :], NT) * slope_ref[:, cols]
        low = ghidden.astype(BF16)
        small_ref[:, pl.ds(pl.multiple_of(4 * D + t * tile, tile), tile)] = sum8(low.astype(F32))
        gsecond_ref[...] += dg(low, w_up_ref[:, cols], NT)
        gup = dg(lhs_t[0], low, NN).astype(BF16)
        for hh in range(2):
            g_ref[:, t, hh * 96 : (hh + 1) * 96, :] = gup[:, hh * 384 : (hh + 1) * 384].reshape(
                8, 96, 384
            )
        gdw = dg(lhs_t[1], active_ref[:, cols], NN).astype(BF16)
        for hh in range(2):
            g_ref[2 * t + hh, :, 192:384, :] = gdw[:, hh * 384 : (hh + 1) * 384].reshape(4, 192, 384)
        return carry

    lax.fori_loop(0, FF // tile, back, 0)

    normed, inv = norm_stats(middle_ref[...])
    gsecond = gsecond_ref[...]
    small_ref[:, D : 2 * D] = sum8(gsecond)
    small_ref[:, 2 * D : 3 * D] = sum8(gsecond * normed)
    amp = gain_ref[...].astype(F32) * (1.0 + piece(4))
    grad = spread(gsecond, amp)
    mean = jnp.mean(grad, axis=-1, keepdims=True)
    along = jnp.mean(grad * normed, axis=-1, keepdims=True)
    gmid = cot_ref[...].astype(F32) + (grad - mean - normed * along) * inv
    gmid_ref[...] = gmid
    small_ref[:, 0:D] = sum8(gmid * branch_ref[...])
    gbranch = spread(gmid, piece(2)).astype(BF16)
    gatt = dg(gbranch, w_out_ref[...], NT)

    def d_copy(quarter_x, pick_y, cc, j):
        target = 2 * pick_y + c
        head = (2 * pick_y + cc) * OWN + j
        is_self = jnp.logical_and(target == n, c == cc)
        return (
            is_self,
            dsend.at[head],
            dland.at[j, n],
            d_send.at[head],
            d_recv.at[j, n],
            (target, 2 * z + cc),
        )

    copies = []
    for pair in range(HEADS // 2):
        top = gatt[0:half, pair * 128 : (pair + 1) * 128]
        bottom = gatt[half:local, pair * 128 : (pair + 1) * 128]
        low = lane(top.shape) < 64
        dsend[2 * pair] = jnp.where(low, top, pltpu.roll(bottom, 64, 1)).astype(BF16)
        dsend[2 * pair + 1] = jnp.where(low, pltpu.roll(top, 64, 1), bottom).astype(BF16)
    for head in range(HEADS):
        copies.append(d_copy(None, head // OWN // 2, (head // OWN) % 2, head % OWN))
        send_or_keep(*copies[-1])

    for hh in range(2):
        gout = dg(att_ref[...], gbranch[:, hh * 384 : (hh + 1) * 384], TN).astype(BF16)
        shaped = gout.reshape(8, 2, 48, 384)
        for rh in range(2):
            g_ref[:, rh * 2 + hh, 384:432, :] = shaped[:, rh]

    for j in range(OWN):
        for quarter in range(4):
            wait_bytes(dland.at[j, quarter], d_recv.at[j, quarter])
    do_ref[...] = dland[...]
    for copy in copies:
        wait_send_unless(*copy)


def call_middle(tokens, cot, att, pat, gain, w_out, w_up, b_up, w_down, b_down):
    local = tokens.shape[0]
    half = local // 2
    sds = jax.ShapeDtypeStruct
    return pl.pallas_call(
        middle_kernel,
        out_shape=(
            sds((local, D), BF16),
            sds((local, D), F32),
            sds((8, 4, ROWS_G, COLS_G), BF16),
            sds((8, SMALL), F32),
            sds((OWN, 4, half, 128), BF16),
        ),
        in_specs=[vm()] * 10,
        out_specs=(vm(),) * 5,
        scratch_shapes=[
            VMEM((local, D), BF16),
            VMEM((local, FF), BF16),
            VMEM((local, FF), F32),
            VMEM((local, D), F32),
            VMEM((local, D), F32),
            VMEM((local, D), F32),
            VMEM((local, D), F32),
            VMEM((2, D, local), BF16),
            VMEM((local, D), BF16),
            VMEM((HEADS, half, 128), BF16),
            VMEM((OWN, 4, half, 128), BF16),
            dma(HEADS),
            dma(OWN, 4),
        ],
        compiler_params=params(1, 60),
        cost_estimate=pl.CostEstimate(flops=2 * 10**10, bytes_accessed=3 * 10**7, transcendentals=10**7),
    )(tokens, cot, att, pat, gain, w_out, w_up, b_up, w_down, b_down)


CUT = 288
CHUNK = 24


def slot_of(other, me):
    return lax.rem(other - me + 3, 4)


def backward_kernel(
    docs_ref,
    tokens_ref,
    cond_ref,
    w_ada_ref,
    pat_ref,
    gain_ref,
    gain_two_ref,
    gmid_ref,
    do_ref,
    q_ref,
    k_ref,
    v_ref,
    all_ref,
    own_ref,
    tab_ref,
    small_two_ref,
    g_hbm,
    gtok_ref,
    blocks_ref,
    qkv_ref,
    packet_ref,
    gcond_ref,
    packed,
    acc_k,
    acc_v,
    acc_w,
    kept,
    csend,
    cland,
    rsend,
    rland,
    small_one,
    g_own,
    g_sum,
    land_a1,
    land_b1,
    sum_a,
    sum_b,
    land_a2,
    land_b2,
    block,
    land_block,
    gq,
    land_q0,
    sum_q,
    land_q1,
    done_q,
    land_q2,
    pack,
    land_s1,
    pack_sum,
    land_s2,
    gc_mine,
    land_gc,
    c_send,
    c_recv,
    r_send,
    r_recv,
    g_load,
    g_send,
    g_recv,
    a1_send,
    a1_recv,
    b1_send,
    b1_recv,
    a2_send,
    a2_recv,
    b2_send,
    b2_recv,
    ag_send,
    ag_recv,
    q0_sem,
    q1_send,
    q1_recv,
    q2_send,
    q2_recv,
    s1_send,
    s1_recv,
    s2_send,
    s2_recv,
    gc_send,
    gc_recv,
):
    n, ny, nx, z, c = place()
    w = 2 * z + c
    local = tokens_ref.shape[0]
    half = local // 2
    length = 4 * local
    group = 2 * ny + c

    barrier = pltpu.get_barrier_semaphore()

    def greet(device):
        pl.semaphore_signal(barrier, inc=1, device_id=device, device_id_type=MESH)

    me = n * 2 + c
    for step in range(1, 8):
        other = lax.rem(me + step, 8)
        greet((other // 2, 2 * z + lax.rem(other, 2)))
    for step in range(1, 4):
        greet((n, 2 * lax.rem(z + step, 4) + c))
    for row in range(8):

        @pl.when(jnp.logical_not(jnp.logical_and(z == n, row == w)))
        def _():
            greet((z, row))

    pl.semaphore_wait(barrier, jnp.where(z == n, 17, 18))


    def others(base):
        return [lax.rem(base + step, 4) for step in (1, 2, 3)]

    def g_copy(chip):
        return remote(
            g_hbm.at[chip, 1 - c], g_sum.at[chip], g_send.at[chip], g_recv.at[chip],
            sibling(n, z, c),
        )

    def g_fetch(chip):
        return pltpu.make_async_copy(g_hbm.at[chip, c], g_own.at[chip % 2], g_load.at[chip % 2])

    def a1_copy(other):
        slot = slot_of(other, n)
        return remote(
            g_sum.at[:, other, pl.ds(0, CUT)], land_a1.at[slot], a1_send.at[slot], a1_recv.at[slot],
            (other, w),
        )

    def b1_copy(chip):
        slot = slot_of(chip, z)
        return remote(
            g_sum.at[chip, :, pl.ds(CUT, ROWS_G - CUT)], land_b1.at[slot], b1_send.at[slot],
            b1_recv.at[slot], (n, 2 * chip + c),
        )

    def a2_copy(chip):
        slot = slot_of(chip, z)
        return remote(
            sum_a.at[chip], land_a2.at[slot], a2_send.at[slot], a2_recv.at[slot], (n, 2 * chip + c)
        )

    def b2_copy(other):
        slot = slot_of(other, n)
        return remote(
            sum_b.at[other], land_b2.at[slot], b2_send.at[slot], b2_recv.at[slot], (other, w)
        )

    def ag_copy(other):
        return remote(block, land_block.at[n], ag_send.at[slot_of(other, n)], ag_recv.at[n], (other, w))

    def core_start():
        for chip in range(4):
            g_copy(chip).start()
        g_fetch(0).start()

    def core_finish():
        for chip in range(4):
            if chip < 3:
                g_fetch(chip + 1).start()
            g_fetch(chip).wait()
            wait_bytes(g_sum.at[chip], g_recv.at[chip])
            for part in range(4):
                g_sum[chip, part] = (
                    g_sum[chip, part].astype(F32) + g_own[chip % 2, part].astype(F32)
                ).astype(BF16)
        for i in range(3):
            a1_copy(others(n)[i]).start()
            b1_copy(others(z)[i]).start()

    def second_a():
        for slot in range(3):
            wait_bytes(land_a1.at[slot], a1_recv.at[slot])
        for chip in range(4):
            total = g_sum[chip, n, 0:CUT].astype(F32)
            for slot in range(3):
                total = total + land_a1[slot, chip].astype(F32)
            sum_a[chip] = total.astype(BF16)
        for chip in others(z):
            a2_copy(chip).start()

    def second_b():
        for slot in range(3):
            wait_bytes(land_b1.at[slot], b1_recv.at[slot])
        for part in range(4):
            total = g_sum[z, part, CUT:ROWS_G].astype(F32)
            for slot in range(3):
                total = total + land_b1[slot, part].astype(F32)
            sum_b[part] = total.astype(BF16)
        for other in others(n):
            b2_copy(other).start()

    def last():
        for slot in range(3):
            wait_bytes(land_a2.at[slot], a2_recv.at[slot])
            wait_bytes(land_b2.at[slot], b2_recv.at[slot])
        top = sum_a[z].astype(F32)
        bottom = sum_b[n].astype(F32)
        for slot in range(3):
            top = top + land_a2[slot].astype(F32)
            bottom = bottom + land_b2[slot].astype(F32)
        block[0:CUT] = top.astype(BF16)
        block[CUT:ROWS_G] = bottom.astype(BF16)
        for other in others(n):
            ag_copy(other).start()


    core_start()
    lanes = lane((local, 128))

    def turned(values, rows):
        cosine, sine = cos_sin(tab_ref[rows, :])
        return values * cosine - halves_turn(values) * sine

    def rounded(values):
        return values.astype(BF16).astype(F32)

    for j in range(OWN):
        acc_k[...] = jnp.zeros_like(acc_k)
        acc_v[...] = jnp.zeros_like(acc_v)

        def quarter_step(i, carry):
            if j == 0:
                pl.when(i == 3)(core_finish)
            rows = pl.ds(pl.multiple_of(i * local, local), local)
            packed_grad = do_ref[j, i].astype(F32)
            grad = jnp.concatenate([packed_grad, pltpu.roll(packed_grad, 64, 1)], axis=0)
            grad = jnp.where(lanes < 64, grad, 0.0).astype(BF16)
            query = q_ref[j, rows, :]
            probs = jnp.exp2(dg(query, k_ref[j], NT) * LOG2E)
            gprobs = probs * dg(grad, v_ref[j], NT)
            scores = (gprobs - probs * jnp.sum(gprobs, axis=1, keepdims=True)).astype(BF16)
            probs = probs.astype(BF16)
            gquery = rounded(dg(scores, k_ref[j], NN) * HEAD_DIM**-0.5)
            at = 384 + 64 * j
            packed[rows, at : at + 64] = turned(gquery, rows)[:, :64].astype(BF16)
            acc_v[...] += dg(grad.T[:64], probs, NN)
            acc_k[...] += dg(query.T[:64], scores, NN)
            return carry

        lax.fori_loop(0, 4, quarter_step, 0)

        def finish(i, carry):
            rows = pl.ds(pl.multiple_of(i * local, local), local)
            both = rounded(jnp.concatenate([acc_k[:, rows], acc_v[:, rows]], axis=0).T)
            packed[rows, j * 128 : (j + 1) * 128] = jnp.where(
                lanes < 64, turned(both, rows), both
            ).astype(BF16)
            return carry

        lax.fori_loop(0, 4, finish, 0)
    packed[:, 576:640] = jnp.zeros((length, 64), BF16)


    def rows_of(quarter, hh):
        return pl.ds(pl.multiple_of(quarter * local + hh * half, half), half)

    def c_copy(quarter):
        return remote(
            csend.at[quarter], cland.at[quarter], c_send.at[quarter], c_recv.at[quarter],
            sibling(n, z, c),
        )

    def r_copy(quarter):
        is_self = jnp.logical_and(quarter == n, nx == c)
        return (
            is_self,
            rsend.at[quarter],
            rland.at[ny, pl.ds(pl.multiple_of(c * half, half), half)],
            r_send.at[quarter],
            r_recv.at[ny, c],
            (quarter, 2 * z + nx),
        )

    def order(i):
        return lax.rem(n + 3 - i, 4)

    def give(i, carry):
        quarter = order(i)
        csend[quarter] = dg(packed[rows_of(quarter, 1 - c), :], own_ref[...], NT).astype(BF16)
        c_copy(quarter).start()
        return carry

    lax.fori_loop(0, 4, give, 0)

    def keep(i, carry):
        quarter = order(i)
        kept[quarter] = dg(packed[rows_of(quarter, c), :], own_ref[...], NT)
        return carry

    lax.fori_loop(0, 4, keep, 0)

    def add(i, carry):
        quarter = order(i)
        wait_bytes(cland.at[quarter], c_recv.at[quarter])
        rsend[quarter] = (kept[quarter] + cland[quarter].astype(F32)).astype(BF16)
        send_or_keep(*r_copy(quarter))
        return carry

    lax.fori_loop(0, 4, add, 0)


    acc_w[...] = jnp.zeros_like(acc_w)

    def weights(i, carry):
        rows = pl.ds(pl.multiple_of(i * local, local), local)
        acc_w[...] += dg(all_ref[rows, :], packed[rows, :], TN)
        return carry

    lax.fori_loop(0, 4, weights, 0)
    gq[...] = acc_w[...].astype(BF16).reshape(gq.shape)
    q0_copy = remote(
        gq.at[:, 1 - nx], land_q0, q0_sem.at[0], q0_sem.at[1], (n + 1 - 2 * nx, w)
    )
    q0_copy.start()

    def q1_copy(chip):
        slot = slot_of(chip, z)
        return remote(
            sum_q.at[chip], land_q1.at[slot], q1_send.at[slot], q1_recv.at[slot], (n, 2 * chip + c)
        )

    def q2_copy(other):
        is_self = jnp.logical_and(other == n, nx == c)
        return (
            is_self, done_q, land_q2.at[group], q2_send.at[other], q2_recv.at[group],
            (other, 2 * z + nx),
        )

    second_a()
    second_b()
    normed, inv = norm_stats(tokens_ref[...].astype(F32))
    q0_copy.wait()
    for chip in range(4):
        sum_q[chip] = (gq[chip, nx].astype(F32) + land_q0[chip].astype(F32)).astype(BF16)
    for chip in others(z):
        q1_copy(chip).start()

    for y in range(2):
        for hh in range(2):
            wait_bytes(rland.at[y, pl.ds(hh * half, half)], r_recv.at[y, hh])
    gfirst = rland[0].astype(F32) + rland[1].astype(F32)
    small_one[:, 0:D] = sum8(gfirst)
    small_one[:, D : 2 * D] = sum8(gfirst * normed)
    amp = gain_ref[...].astype(F32) * (1.0 + pat_ref[:, D : 2 * D])
    grad = flat8(by8(gfirst) * amp[None])
    mean = jnp.mean(grad, axis=-1, keepdims=True)
    along = jnp.mean(grad * normed, axis=-1, keepdims=True)
    gtok_ref[...] = gmid_ref[...] + (grad - mean - normed * along) * inv


    two = docs_ref[0] == DOCS
    even_rows = lax.rem(lax.broadcasted_iota(jnp.int32, (8, D), 0), 2) == 0

    def even_odd(values):
        even = jnp.sum(jnp.where(even_rows, values, 0.0), axis=0, keepdims=True)
        return even, jnp.sum(jnp.where(even_rows, 0.0, values), axis=0, keepdims=True)

    pack[...] = jnp.zeros_like(pack)
    gc_mine[...] = jnp.zeros_like(gc_mine)

    def put(chunk, row, values, s):
        pack[chunk, row : row + 1, 0:96] = values[:, 96 * s : 96 * s + 96]

    raws = [
        small_one[:, 0:D],
        small_one[:, D : 2 * D],
        small_two_ref[:, 0:D],
        small_two_ref[:, D : 2 * D],
        small_two_ref[:, 2 * D : 3 * D],
        small_two_ref[:, 3 * D : 4 * D],
    ]
    gains = {1: gain_ref, 4: gain_two_ref}
    for piece in range(6):
        even, odd = even_odd(raws[piece])
        if piece in gains:
            scale = pat_ref[:, piece * D : (piece + 1) * D]
            gain_sum = even * (1.0 + scale[0:1]) + odd * (1.0 + scale[1:2])
            for s in range(8):
                put(s, 12 if piece == 1 else 13, gain_sum, s)
            gain = gains[piece][...].astype(F32)
            even, odd = even * gain, odd * gain
        first_doc = jnp.where(two, even, even + odd)
        second_doc = jnp.where(two, odd, 0.0)
        for s in range(8):
            at = 8 * piece + s
            put(at // 6, at % 6, first_doc, s)
            put(at // 6, 6 + at % 6, second_doc, s)
        pieces = [*split3(first_doc), *split3(second_doc)]
        stacked = jnp.concatenate([*pieces, jnp.zeros((10, D), F32)], axis=0).astype(BF16)
        part = dg(stacked, w_ada_ref[:, piece * D : (piece + 1) * D], NT)
        gc_mine[0:1] += part[0:1] + part[1:2] + part[2:3]
        gc_mine[1:2] += part[3:4] + part[4:5] + part[5:6]
    for s in range(32):
        col = 4 * D + 96 * s
        row = jnp.sum(small_two_ref[:, col : col + 96], axis=0, keepdims=True)
        pack[s // 4, 14 + s % 4 : 15 + s % 4, 0:96] = row
    for s in range(8):
        col = 4 * D + FF + 96 * s
        pack[s, 18:19, 0:96] = jnp.sum(small_two_ref[:, col : col + 96], axis=0, keepdims=True)

    def s1_copy(other):
        return remote(
            pack.at[pl.ds(2 * other, 2)], land_s1.at[n], s1_send.at[slot_of(other, n)],
            s1_recv.at[n], (other, w),
        )

    def gc_copy(other):
        return remote(
            gc_mine, land_gc.at[n], gc_send.at[slot_of(other, n)], gc_recv.at[n], (other, w)
        )

    for other in others(n):
        s1_copy(other).start()
        gc_copy(other).start()
    land_gc[n] = gc_mine[...]
    land_s1[n] = pack[pl.ds(2 * n, 2)]
    for other in others(n):
        wait_bytes(land_s1.at[other], s1_recv.at[other])
    total = land_s1[0] + land_s1[1] + land_s1[2] + land_s1[3]
    pack_sum[...] = total
    cond = cond_ref[...].astype(F32)
    for i in range(2):
        pack_sum[i, 19:21, :] = cond

    def s2_copy(index):
        i, other = index // 4, lax.rem(index, 4)
        is_self = jnp.logical_and(other == n, w == 2 * n + i)
        return (
            is_self, pack_sum.at[i], land_s2.at[w], s2_send.at[index], s2_recv.at[w],
            (other, 2 * n + i),
        )

    for index in range(8):
        send_or_keep(*s2_copy(index))

    for slot in range(3):
        wait_bytes(land_q1.at[slot], q1_recv.at[slot])
    total = sum_q[z].astype(F32)
    for slot in range(3):
        total = total + land_q1[slot].astype(F32)
    done_q[...] = total.astype(BF16)
    for other in range(4):
        send_or_keep(*q2_copy(other))

    last()

    for other in others(n):
        wait_bytes(land_gc.at[other], gc_recv.at[other])
    gcond_ref[...] = land_gc[0] + land_gc[1] + land_gc[2] + land_gc[3]
    for row in range(8):
        wait_bytes(land_s2.at[row], s2_recv.at[row])
    packet_ref[...] = land_s2[...]
    for g in range(4):
        wait_bytes(land_q2.at[g], q2_recv.at[g])
    qkv_ref[...] = land_q2[...]
    land_block[n] = block[...]
    for other in others(n):
        wait_bytes(land_block.at[other], ag_recv.at[other])
    blocks_ref[...] = land_block[...]


    def drain(quarter, carry):
        c_copy(quarter).wait_send()
        wait_send_unless(*r_copy(quarter))
        g_copy(quarter).wait_send()
        wait_send_unless(*q2_copy(quarter))
        return carry

    lax.fori_loop(0, 4, drain, 0)
    for i in range(3):
        other, chip = others(n)[i], others(z)[i]
        a1_copy(other).wait_send()
        b1_copy(chip).wait_send()
        a2_copy(chip).wait_send()
        b2_copy(other).wait_send()
        ag_copy(other).wait_send()
        q1_copy(chip).wait_send()
        s1_copy(other).wait_send()
        gc_copy(other).wait_send()
    for index in range(8):
        wait_send_unless(*s2_copy(index))


def call_backward(
    docs, tokens, cond, w_ada, pat, gain, gain_two, gmid, do, q, k, v, everything, own, tab, small_two, g
):
    local = tokens.shape[0]
    half = local // 2
    length = 4 * local
    sds = jax.ShapeDtypeStruct
    rest = ROWS_G - CUT
    return pl.pallas_call(
        backward_kernel,
        out_shape=(
            sds((local, D), F32),
            sds((4, ROWS_G, COLS_G), BF16),
            sds((4, 96, WCOLS), BF16),
            sds((8, CHUNK, 128), F32),
            sds((8, 128), F32),
        ),
        in_specs=[smem()] + [vm()] * 15 + [hbm()],
        out_specs=(vm(),) * 5,
        scratch_shapes=[
            VMEM((length, WCOLS), BF16),
            VMEM((64, length), F32),
            VMEM((64, length), F32),
            VMEM((D, WCOLS), F32),
            VMEM((4, half, D), F32),
            VMEM((4, half, D), BF16),
            VMEM((4, half, D), BF16),
            VMEM((4, half, D), BF16),
            VMEM((2, local, D), BF16),
            VMEM((8, 2 * D), F32),
            VMEM((2, 4, ROWS_G, COLS_G), BF16),
            VMEM((4, 4, ROWS_G, COLS_G), BF16),
            VMEM((3, 4, CUT, COLS_G), BF16),
            VMEM((3, 4, rest, COLS_G), BF16),
            VMEM((4, CUT, COLS_G), BF16),
            VMEM((4, rest, COLS_G), BF16),
            VMEM((3, CUT, COLS_G), BF16),
            VMEM((3, rest, COLS_G), BF16),
            VMEM((ROWS_G, COLS_G), BF16),
            VMEM((4, ROWS_G, COLS_G), BF16),
            VMEM((4, 2, 96, WCOLS), BF16),
            VMEM((4, 96, WCOLS), BF16),
            VMEM((4, 96, WCOLS), BF16),
            VMEM((3, 96, WCOLS), BF16),
            VMEM((96, WCOLS), BF16),
            VMEM((4, 96, WCOLS), BF16),
            VMEM((8, CHUNK, 128), F32),
            VMEM((4, 2, CHUNK, 128), F32),
            VMEM((2, CHUNK, 128), F32),
            VMEM((8, CHUNK, 128), F32),
            VMEM((8, 128), F32),
            VMEM((4, 8, 128), F32),
        ]
        + [
            dma(k)
            for k in (4, 4, 4)
        ]
        + [dma(2, 2), dma(2), dma(4), dma(4)]
        + [dma(3)] * 8
        + [dma(3), dma(4), dma(2), dma(3), dma(3), dma(4), dma(4), dma(3), dma(4), dma(8), dma(8)]
        + [dma(3), dma(4)],
        compiler_params=params(2, 62),
        cost_estimate=pl.CostEstimate(flops=2 * 10**10, bytes_accessed=3 * 10**7, transcendentals=10**7),
    )(
        docs, tokens, cond, w_ada, pat, gain, gain_two, gmid, do, q, k, v, everything, own, tab,
        small_two, g,
    )


def finish_kernel(
    output_in, gtok_in, blocks, qkv, packet, output_out, gtok_out, gqkv, gout, gup, gdown, gada, gvec
):
    output_out[...] = output_in[...]
    gtok_out[...] = gtok_in[...]
    for part in range(4):
        for hh in range(2):
            at = part * 768 + hh * 384
            gup[:, at : at + 384] = blocks[part, hh * 96 : (hh + 1) * 96, :].astype(F32)
        rh, ch = part // 2, part % 2
        gout[rh * 48 : (rh + 1) * 48, ch * 384 : (ch + 1) * 384] = blocks[part, 384:432, :].astype(F32)
    for pair in range(2):
        both = jnp.concatenate(
            [blocks[2 * pair, 192:384, :], blocks[2 * pair + 1, 192:384, :]], axis=0
        ).astype(F32)
        gdown[:, pair * 384 : (pair + 1) * 384] = both.T

    def head_block(part, head):
        g, j = head // OWN, head % OWN
        if part == 0:
            at, upper = 384 + 128 * (j // 2), j % 2
        else:
            at, upper = 128 * j, part - 1
        return qkv[g, :, at : at + 128].astype(F32), upper

    for part in range(3):
        for pair in range(HEADS // 2):
            even, up = head_block(part, 2 * pair)
            even = pltpu.roll(even, 64, 1) if up else even
            odd, up = head_block(part, 2 * pair + 1)
            odd = odd if up else pltpu.roll(odd, 64, 1)
            at = part * D + pair * 128
            gqkv[:, at : at + 128] = jnp.where(lane(even.shape) < 64, even, odd)

    conds = [packet[:, 19, :], packet[:, 20, :]]
    lhs = jnp.concatenate([conds[0]] * 3 + [conds[1]] * 3, axis=0).astype(BF16)
    for k in range(6):
        first, second = packet[:, k, :], packet[:, 6 + k, :]
        rhs = jnp.concatenate([*split3(first), *split3(second)], axis=0).astype(BF16)
        gada[:, 96 * k : 96 * k + 96] = dg(lhs, rhs, TN)[:, :96]
        gvec[0:1, 96 * k : 96 * k + 96] = jnp.sum(first + second, axis=0, keepdims=True)[:, :96]
    for row, at, k in ((1, 0, 12), (2, 0, 13), (3, 0, 14), (3, 1, 15), (3, 2, 16), (3, 3, 17), (4, 0, 18)):
        gvec[row : row + 1, 96 * at : 96 * at + 96] = jnp.sum(packet[:, k, :], axis=0, keepdims=True)[
            :, :96
        ]


def call_finish(output, gtok, blocks, qkv, packet):
    local = output.shape[0]
    sds = jax.ShapeDtypeStruct
    return pl.pallas_call(
        finish_kernel,
        out_shape=(
            sds((local, D), BF16),
            sds((local, D), F32),
            sds((96, 3 * D), F32),
            sds((96, D), F32),
            sds((96, FF), F32),
            sds((384, D), F32),
            sds((128, 576), F32),
            sds((8, 576), F32),
        ),
        in_specs=[vm()] * 5,
        out_specs=(vm(),) * 8,
        compiler_params=pltpu.CompilerParams(vmem_limit_bytes=40 * 2**20),
        cost_estimate=pl.CostEstimate(flops=10**7, bytes_accessed=10**7, transcendentals=0),
    )(output, gtok, blocks, qkv, packet)


def plain_backward_kernel(
    tokens_ref,
    pat_ref,
    gain_ref,
    gmid_ref,
    do_ref,
    q_ref,
    k_ref,
    v_ref,
    all_ref,
    own_ref,
    tab_ref,
    gtok_ref,
    gq_ref,
    small_ref,
    packed,
    acc_k,
    acc_v,
    acc_w,
    kept,
    csend,
    cland,
    rsend,
    rland,
    c_send,
    c_recv,
    r_send,
    r_recv,
):
    n, ny, nx, z, c = place()
    local = tokens_ref.shape[0]
    half = local // 2
    length = 4 * local
    plane_barrier(n, z, c)
    lanes = lane((local, 128))

    def turned(values, rows):
        cosine, sine = cos_sin(tab_ref[rows, :])
        return values * cosine - halves_turn(values) * sine

    def rounded(values):
        return values.astype(BF16).astype(F32)

    for j in range(OWN):
        acc_k[...] = jnp.zeros_like(acc_k)
        acc_v[...] = jnp.zeros_like(acc_v)

        def quarter_step(i, carry):
            rows = pl.ds(pl.multiple_of(i * local, local), local)
            block = do_ref[j, i].astype(F32)
            grad = jnp.concatenate([block, pltpu.roll(block, 64, 1)], axis=0)
            grad = jnp.where(lanes < 64, grad, 0.0).astype(BF16)
            query = q_ref[j, rows, :]
            probs = jnp.exp2(dg(query, k_ref[j], NT) * LOG2E)
            gprobs = probs * dg(grad, v_ref[j], NT)
            scores = (gprobs - probs * jnp.sum(gprobs, axis=1, keepdims=True)).astype(BF16)
            probs = probs.astype(BF16)
            gquery = rounded(dg(scores, k_ref[j], NN) * HEAD_DIM**-0.5)
            at = 384 + 64 * j
            packed[rows, at : at + 64] = turned(gquery, rows)[:, :64].astype(BF16)
            acc_v[...] += dg(grad.T[:64], probs, NN)
            acc_k[...] += dg(query.T[:64], scores, NN)
            return carry

        lax.fori_loop(0, 4, quarter_step, 0)

        def finish(i, carry):
            rows = pl.ds(pl.multiple_of(i * local, local), local)
            both = jnp.concatenate([acc_k[:, rows], acc_v[:, rows]], axis=0).T
            both = rounded(both)
            packed[rows, j * 128 : (j + 1) * 128] = jnp.where(
                lanes < 64, turned(both, rows), both
            ).astype(BF16)
            return carry

        lax.fori_loop(0, 4, finish, 0)
    packed[:, 576:640] = jnp.zeros((length, 64), BF16)

    def rows_of(quarter, hh):
        return pl.ds(pl.multiple_of(quarter * local + hh * half, half), half)

    def c_copy(quarter):
        return remote(
            csend.at[quarter], cland.at[quarter], c_send.at[quarter], c_recv.at[quarter],
            sibling(n, z, c),
        )

    def r_copy(quarter):
        is_self = jnp.logical_and(quarter == n, nx == c)
        return (
            is_self,
            rsend.at[quarter],
            rland.at[ny, pl.ds(pl.multiple_of(c * half, half), half)],
            r_send.at[quarter],
            r_recv.at[ny, c],
            (quarter, 2 * z + nx),
        )

    def order(i):
        return lax.rem(n + 3 - i, 4)

    def give(i, carry):
        quarter = order(i)
        csend[quarter] = dg(packed[rows_of(quarter, 1 - c), :], own_ref[...], NT).astype(BF16)
        c_copy(quarter).start()
        return carry

    lax.fori_loop(0, 4, give, 0)

    def keep(i, carry):
        quarter = order(i)
        kept[quarter] = dg(packed[rows_of(quarter, c), :], own_ref[...], NT)
        return carry

    lax.fori_loop(0, 4, keep, 0)

    def add(i, carry):
        quarter = order(i)
        wait_bytes(cland.at[quarter], c_recv.at[quarter])
        rsend[quarter] = (kept[quarter] + cland[quarter].astype(F32)).astype(BF16)
        send_or_keep(*r_copy(quarter))
        return carry

    lax.fori_loop(0, 4, add, 0)

    acc_w[...] = jnp.zeros_like(acc_w)

    def weights(i, carry):
        rows = pl.ds(pl.multiple_of(i * local, local), local)
        acc_w[...] += dg(all_ref[rows, :], packed[rows, :], TN)
        return carry

    lax.fori_loop(0, 4, weights, 0)
    gq_ref[...] = acc_w[...].astype(BF16).reshape(gq_ref.shape)

    normed, inv = norm_stats(tokens_ref[...].astype(F32))
    for y in range(2):
        for hh in range(2):
            wait_bytes(rland.at[y, pl.ds(hh * half, half)], r_recv.at[y, hh])
    gfirst = rland[0].astype(F32) + rland[1].astype(F32)
    small_ref[:, 0:D] = sum8(gfirst)
    small_ref[:, D : 2 * D] = sum8(gfirst * normed)
    amp = gain_ref[...].astype(F32) * (1.0 + pat_ref[:, D : 2 * D])
    grad = flat8(by8(gfirst) * amp[None])
    mean = jnp.mean(grad, axis=-1, keepdims=True)
    along = jnp.mean(grad * normed, axis=-1, keepdims=True)
    gtok_ref[...] = gmid_ref[...] + (grad - mean - normed * along) * inv

    def drain(quarter, carry):
        c_copy(quarter).wait_send()
        wait_send_unless(*r_copy(quarter))
        return carry

    lax.fori_loop(0, 4, drain, 0)


def call_plain_backward(tokens, pat, gain, gmid, do, q, k, v, everything, own, tab):
    local = tokens.shape[0]
    half = local // 2
    length = 4 * local
    sds = jax.ShapeDtypeStruct
    return pl.pallas_call(
        plain_backward_kernel,
        out_shape=(
            sds((local, D), F32),
            sds((8, 96, WCOLS), BF16),
            sds((8, 2 * D), F32),
        ),
        in_specs=[vm()] * 11,
        out_specs=(vm(),) * 3,
        scratch_shapes=[
            VMEM((length, WCOLS), BF16),
            VMEM((64, length), F32),
            VMEM((64, length), F32),
            VMEM((D, WCOLS), F32),
            VMEM((4, half, D), F32),
            VMEM((4, half, D), BF16),
            VMEM((4, half, D), BF16),
            VMEM((4, half, D), BF16),
            VMEM((2, local, D), BF16),
            dma(4),
            dma(4),
            dma(4),
            dma(2, 2),
        ],
        compiler_params=params(2, 60),
        cost_estimate=pl.CostEstimate(flops=2 * 10**10, bytes_accessed=3 * 10**7, transcendentals=10**7),
    )(tokens, pat, gain, gmid, do, q, k, v, everything, own, tab)


def plain_sums(g, gq, own_ids):
    n, z, c = own_ids
    up = g[:, :, :192].reshape(8, 4, 2, 96, 384).transpose(0, 3, 1, 2, 4).reshape(D, FF)
    down = g[:, :, 192:384].reshape(8, D, 384).transpose(0, 2, 1).reshape(FF, D)
    out = g[:, :, 384:].reshape(8, 2, 2, 48, 384).transpose(0, 1, 3, 2, 4).reshape(D, D)
    flat = gq.reshape(D, WCOLS)
    pieces = [flat[:, 384:576]]
    pieces.append(jnp.concatenate([flat[:, j * 128 : j * 128 + 64] for j in range(OWN)], axis=1))
    pieces.append(jnp.concatenate([flat[:, j * 128 + 64 : j * 128 + 128] for j in range(OWN)], axis=1))
    group = 2 * (n // 2) + c
    whole = jnp.zeros((D, 3, 4, OWN * HEAD_DIM), F32)
    for part in range(3):
        whole = lax.dynamic_update_slice(
            whole, pieces[part].astype(F32)[:, None, None, :], (0, part, group, 0)
        )
    whole = whole.reshape(D, 3 * D)

    def total(values):
        share = lax.psum_scatter(values.astype(F32), "wide", scatter_dimension=0, tiled=True)
        return lax.psum(share, "narrow")

    return total(whole), total(out), total(up), total(down)


def body(
    tokens,
    condition,
    docs_per_row,
    w_ada,
    b_ada,
    gain_one,
    w_qkv,
    w_out,
    gain_two,
    w_up,
    b_up,
    w_down,
    b_down,
    cotangent,
):
    local = tokens.shape[1]
    x = tokens.reshape(local, D)
    cot = cotangent.reshape(local, D)
    cond = condition.reshape(DOCS, -1)
    table = jnp.asarray(rotary_table(4 * local))

    def line(vector):
        return vector.reshape(1, -1)

    att, everything, q, k, v, pat, own, tab = call_forward(
        docs_per_row, x, cond, w_ada, line(b_ada), line(gain_one), w_qkv, table
    )
    output, gmid, g, small_two, do = call_middle(
        x, cot, att, pat, line(gain_two), w_out, w_up, line(b_up), w_down, line(b_down)
    )
    if (lax.axis_size("narrow"), lax.axis_size("wide")) == (4, 8):
        gtok, blocks, qkv, packet, gcond = call_backward(
            docs_per_row, x, cond, w_ada, pat, line(gain_one), line(gain_two), gmid, do, q, k, v,
            everything, own, tab, small_two, g.reshape(4, 2, 4, ROWS_G, COLS_G),
        )
        output, gtok, gqkv, gout, gup, gdown, gada, gvec = call_finish(
            output, gtok, blocks, qkv, packet
        )
        return (
            output[None],
            gtok[None],
            gcond[None, :DOCS],
            gada,
            gvec[0],
            gvec[1, :96],
            gqkv,
            gout,
            gvec[2, :96],
            gup,
            gvec[3, :384],
            gdown,
            gvec[4, :96],
        )

    gtok, gq, small_one = call_plain_backward(
        x, pat, line(gain_one), gmid, do, q, k, v, everything, own, tab
    )
    n, w = lax.axis_index("narrow"), lax.axis_index("wide")
    sum_qkv, sum_out, sum_up, sum_down = plain_sums(g, gq, (n, w // 2, w % 2))

    small = jnp.concatenate([small_one, small_two], axis=1).reshape(4, 2, -1).sum(0)
    small = lax.psum(small, "narrow")
    shift_one, raw_one, gate_one, shift_two, raw_two, gate_two = jnp.split(small[:, : 6 * D], 6, axis=1)
    scales = pat[:2].reshape(2, 6, D)
    sum_gain_one = jnp.sum(raw_one * (1.0 + scales[:, 1]), axis=0)
    sum_gain_two = jnp.sum(raw_two * (1.0 + scales[:, 4]), axis=0)
    grads = jnp.concatenate(
        [
            shift_one,
            raw_one * gain_one.astype(F32),
            gate_one,
            shift_two,
            raw_two * gain_two.astype(F32),
            gate_two,
        ],
        axis=1,
    )
    two = docs_per_row[0] == DOCS
    grad_mods = jnp.stack(
        [jnp.where(two, grads[0], grads[0] + grads[1]), jnp.where(two, grads[1], 0.0)]
    )
    high = lax.Precision.HIGHEST
    grad_condition = jnp.einsum("sm,cm->sc", grad_mods, w_ada.astype(F32), precision=high)[None]
    part_ada = jnp.einsum("sm,sc->mc", grad_mods, cond.astype(F32), precision=high)

    def share(values):
        return lax.psum_scatter(values, "wide", scatter_dimension=0, tiled=True)

    sum_b_up = jnp.sum(small[:, 6 * D : 6 * D + FF], axis=0)
    sum_b_down = jnp.sum(small[:, 6 * D + FF :], axis=0)
    return (
        output[None],
        gtok[None],
        grad_condition,
        share(part_ada).T,
        share(jnp.sum(grad_mods, axis=0)),
        share(sum_gain_one),
        sum_qkv,
        sum_out,
        share(sum_gain_two),
        sum_up,
        share(sum_b_up),
        sum_down,
        share(sum_b_down),
    )


def solution(mesh):
    in_specs = (
        P("wide", "narrow", None),
        P("wide", None, None),
        P("wide"),
        P(),
        P(),
        P(),
        P(),
        P(),
        P(),
        P(),
        P(),
        P(),
        P(),
        P("wide", "narrow", None),
    )
    out_specs = (
        P("wide", "narrow", None),
        P("wide", "narrow", None),
        P("wide", None, None),
        P(None, "wide"),
        P("wide"),
        P("wide"),
        P("wide", None),
        P("wide", None),
        P("wide"),
        P("wide", None),
        P("wide"),
        P("wide", None),
        P("wide"),
    )
    return jax.shard_map(body, mesh=mesh, in_specs=in_specs, out_specs=out_specs, check_vma=False)
```

```python
import functools

import jax
import jax.numpy as jnp
import numpy as np
from jax import lax
from jax.experimental import pallas as pl
from jax.experimental.pallas import tpu as pltpu
from jax.sharding import PartitionSpec as P

D = 768
HEADS = 12
HEAD_DIM = 64
FF = 3072
DOCS = 2
EPS = 1e-05
LOG2E = 1.4426950408889634
BIG = 1e30
OWN = 3
WCOLS = 640
KV_AT = (0, 128, 384)
Q_AT = (256, 320, 512)
ROWS_G = 432
COLS_G = 384
MESH = pl.DeviceIdType.MESH
F32 = jnp.float32
BF16 = jnp.bfloat16
NN = (((1,), (0,)), ((), ()))
NT = (((1,), (1,)), ((), ()))
TN = (((0,), (0,)), ((), ()))
VMEM = pltpu.VMEM
ANY = pl.ANY


def dg(a, b, dims):
    return lax.dot_general(a, b, dims, preferred_element_type=F32)


def place():
    n = lax.axis_index("narrow")
    w = lax.axis_index("wide")
    return n, n // 2, lax.rem(n, 2), w // 2, lax.rem(w, 2)


def sibling(n, z, c):
    return (n, 2 * z + 1 - c)


def plane_barrier(n, z, c):
    barrier = pltpu.get_barrier_semaphore()
    me = n * 2 + c
    for step in range(1, 8):
        other = lax.rem(me + step, 8)
        pl.semaphore_signal(
            barrier, inc=1, device_id=(other // 2, 2 * z + lax.rem(other, 2)), device_id_type=MESH
        )
    pl.semaphore_wait(barrier, 7)


def remote(src, dst, send, recv, device):
    return pltpu.make_async_remote_copy(
        src_ref=src, dst_ref=dst, send_sem=send, recv_sem=recv, device_id=device, device_id_type=MESH
    )


def send_or_keep(is_self, src, dst, send, recv, device):
    @pl.when(is_self)
    def _():
        pltpu.make_async_copy(src, dst, recv).start()

    @pl.when(jnp.logical_not(is_self))
    def _():
        remote(src, dst, send, recv, device).start()


def wait_send_unless(is_self, src, dst, send, recv, device):
    @pl.when(jnp.logical_not(is_self))
    def _():
        remote(src, dst, send, recv, device).wait_send()


def wait_bytes(ref, sem):
    pltpu.make_async_copy(ref, ref, sem).wait()


def lane(shape):
    return lax.broadcasted_iota(jnp.int32, shape, len(shape) - 1)


def by8(values):
    return values.reshape(values.shape[0] // 8, 8, values.shape[1])


def flat8(values):
    return values.reshape(values.shape[0] * 8, values.shape[2])


def sum8(values):
    return jnp.sum(by8(values), axis=0)


def norm_stats(values):
    mean = jnp.mean(values, axis=-1, keepdims=True)
    centred = values - mean
    spread = jnp.mean(centred * centred, axis=-1, keepdims=True)
    inv = lax.rsqrt(spread + EPS)
    return centred * inv, inv


def halves_turn(values):
    where = lax.rem(lane(values.shape), 64) < 32
    return jnp.where(where, pltpu.roll(values, 96, 1), pltpu.roll(values, 32, 1))


def cos_sin(table):
    lanes = lane(table.shape)
    other = pltpu.roll(table, 64, 1)
    cosine = jnp.where(lanes < 64, table, other)
    sine = jnp.where(lanes < 64, other, table)
    return cosine, jnp.where(lax.rem(lanes, 64) < 32, -sine, sine)


def split3(column):
    high = column.astype(BF16).astype(F32)
    rest = column - high
    middle = rest.astype(BF16).astype(F32)
    low = (rest - middle).astype(BF16).astype(F32)
    return high, middle, low


def forward_kernel(
    docs_ref,
    tokens_ref,
    cond_ref,
    w_ada_ref,
    b_ada_ref,
    gain_ref,
    w_qkv_hbm,
    table_hbm,
    att_ref,
    all_ref,
    q_ref,
    k_ref,
    v_ref,
    pat_ref,
    own_ref,
    tab_ref,
    mine,
    gathered,
    w_qkv,
    tables,
    osend,
    oland,
    docs_mine,
    docs_other,
    load_sem,
    docs_sem,
    a_send,
    a_recv,
    f_send,
    f_recv,
    o_send,
    o_recv,
    all_sem,
):
    n, ny, nx, z, c = place()
    local = tokens_ref.shape[0]
    half = local // 2
    length = local * 4
    loads = [
        pltpu.make_async_copy(w_qkv_hbm, w_qkv, load_sem.at[0]),
        pltpu.make_async_copy(table_hbm, tables, load_sem.at[1]),
    ]
    for load in loads:
        load.start()
    docs_mine[...] = jnp.full(docs_mine.shape, docs_ref[0], jnp.int32).astype(F32)
    plane_barrier(n, z, c)
    docs_copy = remote(docs_mine, docs_other, docs_sem.at[0], docs_sem.at[1], sibling(n, z, c))
    docs_copy.start()

    two = docs_ref[0] == DOCS
    parity = lax.rem(lax.broadcasted_iota(jnp.int32, (16, 128), 0), 2)
    odd = jnp.logical_and(parity == 1, two)
    cond = cond_ref[...].astype(F32)
    cond16 = jnp.where(odd, cond[1:2, :], cond[0:1, :]).astype(BF16)
    pat_ref[...] = dg(cond16, w_ada_ref[...], NN)[:8] + b_ada_ref[...].astype(F32)

    shift = pat_ref[:, 0:D]
    amp = gain_ref[...].astype(F32) * (1.0 + pat_ref[:, D : 2 * D])

    def a_copy(my, hh):
        target = 2 * my + c
        is_self = jnp.logical_and(target == n, c == hh)
        return (
            is_self,
            mine.at[pl.ds(hh * half, half)],
            gathered.at[pl.ds(pl.multiple_of(n * local + hh * half, half), half)],
            a_send.at[my * 2 + hh],
            a_recv.at[n],
            (target, 2 * z + hh),
        )

    for hh in range(2):
        normed, _ = norm_stats(tokens_ref[hh * half : (hh + 1) * half, :].astype(F32))
        mine[hh * half : (hh + 1) * half, :] = flat8(by8(normed) * amp[None] + shift[None]).astype(
            BF16
        )
        for my in range(2):
            send_or_keep(*a_copy(my, hh))

    for load in loads:
        load.wait()
    group = 2 * ny + c
    lanes_w = lane((D, 128))

    def columns(part, j, at):
        col = part * HEADS + group * OWN + j
        block = w_qkv[:, pl.ds(pl.multiple_of((col // 2) * 128, 128), 128)].astype(F32)
        return pltpu.roll(block, lax.rem(col + at, 2) * 64, 1)

    for j in range(OWN):
        own_ref[:, KV_AT[j] : KV_AT[j] + 128] = jnp.where(
            lanes_w < 64, columns(1, j, 0), columns(2, j, 1)
        ).astype(BF16)
    own_ref[:, 256:384] = jnp.where(lanes_w < 64, columns(0, 0, 0), columns(0, 1, 1)).astype(BF16)
    own_ref[:, 512:640] = jnp.where(lanes_w < 64, columns(0, 2, 0), 0.0).astype(BF16)

    docs_copy.wait()
    docs_heads = jnp.where(nx == c, docs_mine[...], docs_other[...])
    tab_ref[...] = jnp.where(docs_heads[0:1] == DOCS, tables[1], tables[0])

    lanes = lane((8, 128))
    odd8 = jnp.logical_and(parity[:8] == 1, docs_heads == DOCS)
    tail_q = jnp.where(lanes == 64, jnp.where(odd8, 0.0, 1.0), 0.0)
    tail_q = jnp.where(lanes == 65, jnp.where(odd8, 1.0, 0.0), tail_q)
    tail_k = jnp.where(lanes == 64, jnp.where(odd8, -BIG, 0.0), 0.0)
    tail_k = jnp.where(lanes == 65, jnp.where(odd8, 0.0, -BIG), tail_k)
    tail_k = jnp.where(jnp.logical_and(lanes >= 66, lanes < 69), 1.0, tail_k)

    def with_tail(values, tail):
        shaped = by8(values)
        return flat8(jnp.where(lane(shaped.shape) < 64, shaped, tail[None])).astype(BF16)

    def project(source):
        def step(i, carry):
            rows = pl.ds(pl.multiple_of(source * local + i * half, half), half)
            wide = dg(gathered[rows, :], own_ref[...], NN)
            cosine, sine = cos_sin(tab_ref[rows, :])

            def rot(values):
                return values * cosine + halves_turn(values) * sine

            for j in range(OWN):
                block = wide[:, KV_AT[j] : KV_AT[j] + 128]
                k_ref[j, rows, :] = with_tail(rot(block), tail_k)
                v_ref[j, rows, :] = jnp.where(
                    lane(block.shape) < 64, pltpu.roll(block, 64, 1), 1.0
                ).astype(BF16)
            first = rot(wide[:, 256:384]) * HEAD_DIM**-0.5
            q_ref[0, rows, :] = with_tail(first, tail_q)
            q_ref[1, rows, :] = with_tail(pltpu.roll(first, 64, 1), tail_q)
            q_ref[2, rows, :] = with_tail(rot(wide[:, 512:640]) * HEAD_DIM**-0.5, tail_q)
            return carry

        lax.fori_loop(0, 2, step, 0)

    def part(source, hh):
        return gathered.at[pl.ds(pl.multiple_of(source * local + hh * half, half), half)]

    def forward(source):
        wait_bytes(part(source, c), a_recv.at[source])
        remote(
            part(source, c), part(source, c), f_send.at[source], f_recv.at[source], sibling(n, z, c)
        ).start()

    sources = [n, lax.rem(n + 2, 4), n + 1 - 2 * nx, lax.rem(n + 3 - 2 * nx, 4)]

    def arrive(source):
        wait_bytes(part(source, 1 - c), f_recv.at[source])
        project(source)

    forward(sources[0])
    forward(sources[1])
    arrive(sources[0])
    forward(sources[2])
    arrive(sources[1])
    forward(sources[3])
    arrive(sources[2])
    arrive(sources[3])
    keep = pltpu.make_async_copy(gathered, all_ref, all_sem)
    keep.start()

    def o_copy(j, quarter):
        is_self = jnp.logical_and(quarter == n, nx == c)
        return (
            is_self,
            osend.at[j, quarter],
            oland.at[group * OWN + j],
            o_send.at[j, quarter],
            o_recv.at[group * OWN + j],
            (quarter, 2 * z + nx),
        )

    def attend(index, carry):
        j = index // 4
        quarter = lax.rem(n + 3 - lax.rem(index, 4), 4)
        start = quarter * local
        scores = []
        for u in range(2):
            rows = pl.ds(pl.multiple_of(start + u * half, half), half)
            scores.append(dg(q_ref[j, rows, :], k_ref[j], NT))
        outs = []
        for u in range(2):
            rows = pl.ds(pl.multiple_of(start + u * half, half), half)
            top = jnp.max(scores[u], axis=1, keepdims=True)
            weights = jnp.exp2((scores[u] - top) * LOG2E)
            total = jnp.sum(weights, axis=1, keepdims=True)
            mixed = dg((weights * (1.0 / total)).astype(BF16), v_ref[j], NN)
            high, middle, low = split3(top + jnp.log(total))
            query = q_ref[j, rows, :].astype(F32)
            lanes_q = lane(query.shape)
            query = jnp.where(lanes_q == 66, -high, query)
            query = jnp.where(lanes_q == 67, -middle, query)
            q_ref[j, rows, :] = jnp.where(lanes_q == 68, -low, query).astype(BF16)
            outs.append(mixed)
        osend[j, quarter] = jnp.where(
            lane(outs[0].shape) < 64, outs[0], pltpu.roll(outs[1], 64, 1)
        ).astype(BF16)
        send_or_keep(*o_copy(j, quarter))
        return carry

    lax.fori_loop(0, OWN * 4, attend, 0)

    for head in range(HEADS):
        wait_bytes(oland.at[head], o_recv.at[head])
    for pair in range(HEADS // 2):
        even = oland[2 * pair].astype(F32)
        odd_head = oland[2 * pair + 1].astype(F32)
        low = lane(even.shape) < 64
        cols = slice(pair * 128, (pair + 1) * 128)
        att_ref[0:half, cols] = jnp.where(low, even, pltpu.roll(odd_head, 64, 1)).astype(BF16)
        att_ref[half:local, cols] = jnp.where(low, pltpu.roll(even, 64, 1), odd_head).astype(BF16)

    for hh in range(2):
        for my in range(2):
            wait_send_unless(*a_copy(my, hh))
    for source in range(4):
        remote(
            part(source, c), part(source, c), f_send.at[source], f_recv.at[source], sibling(n, z, c)
        ).wait_send()

    def drain(index, carry):
        wait_send_unless(*o_copy(index // 4, lax.rem(index, 4)))
        return carry

    lax.fori_loop(0, OWN * 4, drain, 0)
    keep.wait()


def vm():
    return pl.BlockSpec(memory_space=VMEM)


def hbm():
    return pl.BlockSpec(memory_space=ANY)


def smem():
    return pl.BlockSpec(memory_space=pltpu.SMEM)


def params(collective_id, limit=56):
    return pltpu.CompilerParams(
        collective_id=collective_id, has_side_effects=True, vmem_limit_bytes=limit * 2**20
    )


def dma(*shape):
    return pltpu.SemaphoreType.DMA(shape)


def call_forward(docs, tokens, cond, w_ada, b_ada, gain, w_qkv, table):
    local = tokens.shape[0]
    length = 4 * local
    half = local // 2
    sds = jax.ShapeDtypeStruct
    return pl.pallas_call(
        forward_kernel,
        out_shape=(
            sds((local, D), BF16),
            sds((length, D), BF16),
            sds((OWN, length, 128), BF16),
            sds((OWN, length, 128), BF16),
            sds((OWN, length, 128), BF16),
            sds((8, 6 * D), F32),
            sds((D, WCOLS), BF16),
            sds((length, 128), F32),
        ),
        in_specs=[smem(), vm(), vm(), vm(), vm(), vm(), hbm(), hbm()],
        out_specs=(vm(), hbm(), vm(), vm(), vm(), vm(), vm(), vm()),
        scratch_shapes=[
            VMEM((local, D), BF16),
            VMEM((length, D), BF16),
            VMEM((D, 3 * D), BF16),
            VMEM((2, length, 128), F32),
            VMEM((OWN, 4, half, 128), BF16),
            VMEM((HEADS, half, 128), BF16),
            VMEM((8, 128), F32),
            VMEM((8, 128), F32),
            dma(2),
            dma(2),
            dma(4),
            dma(4),
            dma(4),
            dma(4),
            dma(OWN, 4),
            dma(HEADS),
            pltpu.SemaphoreType.DMA,
        ],
        compiler_params=params(0),
        cost_estimate=pl.CostEstimate(flops=10**10, bytes_accessed=2 * 10**7, transcendentals=10**7),
    )(docs, tokens, cond, w_ada, b_ada, gain, w_qkv, table)


def rotary_table(length):
    freq = 10000.0 ** (-np.arange(HEAD_DIM // 2, dtype=np.float64) * 2.0 / HEAD_DIM)
    tables = []
    for docs in (1, DOCS):
        angle = (np.arange(length) // docs)[:, None] * freq[None, :]
        cosine, sine = np.cos(angle), np.sin(angle)
        tables.append(np.concatenate([cosine, cosine, sine, sine], axis=1))
    return np.stack(tables).astype(np.float32)


SMALL = 4 * D + FF + D


def middle_kernel(
    tokens_ref,
    cot_ref,
    att_ref,
    pat_ref,
    gain_ref,
    w_out_ref,
    w_up_ref,
    b_up_ref,
    w_down_ref,
    b_down_ref,
    out_ref,
    gmid_ref,
    g_ref,
    small_ref,
    do_ref,
    second_ref,
    active_ref,
    slope_ref,
    down_ref,
    gsecond_ref,
    middle_ref,
    branch_ref,
    lhs_t,
    gdown_ref,
    dsend,
    dland,
    d_send,
    d_recv,
):
    n, ny, nx, z, c = place()
    group = 2 * ny + c
    local = tokens_ref.shape[0]
    half = local // 2
    tile = 768
    plane_barrier(n, z, c)

    def piece(index):
        return pat_ref[:, index * D : (index + 1) * D]

    def spread(values, pattern):
        return flat8(by8(values) * pattern[None])

    branch_ref[...] = dg(att_ref[...], w_out_ref[...], NN)
    middle = tokens_ref[...].astype(F32) + spread(branch_ref[...], piece(2))
    middle_ref[...] = middle
    amp = gain_ref[...].astype(F32) * (1.0 + piece(4))
    normed, _ = norm_stats(middle)
    second = flat8(by8(normed) * amp[None] + piece(3)[None]).astype(BF16)
    second_ref[...] = second
    down_ref[...] = jnp.broadcast_to(b_down_ref[...].astype(F32), down_ref.shape)

    def up(t, carry):
        cols = pl.ds(pl.multiple_of(t * tile, tile), tile)
        hidden = dg(second_ref[...], w_up_ref[:, cols], NN) + b_up_ref[:, cols].astype(F32)
        square = hidden * hidden
        bend = jnp.tanh(0.7978845608028654 * hidden * (1.0 + 0.044715 * square))
        part = 0.5 * (1.0 + bend)
        active_ref[:, cols] = (hidden * part).astype(BF16)
        slope_ref[:, cols] = part + (0.5 * 0.7978845608028654) * hidden * (1.0 - bend * bend) * (
            1.0 + 3.0 * 0.044715 * square
        )
        down_ref[...] += dg(active_ref[:, cols], w_down_ref[cols, :], NN)
        return carry

    lax.fori_loop(0, FF // tile, up, 0)

    cot = cot_ref[...].astype(F32)
    down = down_ref[...]
    out_ref[...] = (middle_ref[...] + spread(down, piece(5))).astype(BF16)
    small_ref[:, 3 * D : 4 * D] = sum8(cot * down)
    gdown = spread(cot, piece(5)).astype(BF16)
    gdown_ref[...] = gdown
    small_ref[:, 4 * D + FF :] = sum8(gdown.astype(F32))
    lhs_t[0] = second_ref[...].T
    lhs_t[1] = gdown.T
    gsecond_ref[...] = jnp.zeros_like(gsecond_ref)

    def back(t, carry):
        cols = pl.ds(pl.multiple_of(t * tile, tile), tile)
        ghidden = dg(gdown_ref[...], w_down_ref[cols, :], NT) * slope_ref[:, cols]
        low = ghidden.astype(BF16)
        small_ref[:, pl.ds(pl.multiple_of(4 * D + t * tile, tile), tile)] = sum8(low.astype(F32))
        gsecond_ref[...] += dg(low, w_up_ref[:, cols], NT)
        gup = dg(lhs_t[0], low, NN).astype(BF16)
        for hh in range(2):
            g_ref[:, t, hh * 96 : (hh + 1) * 96, :] = gup[:, hh * 384 : (hh + 1) * 384].reshape(
                8, 96, 384
            )
        gdw = dg(lhs_t[1], active_ref[:, cols], NN).astype(BF16)
        for hh in range(2):
            g_ref[2 * t + hh, :, 192:384, :] = gdw[:, hh * 384 : (hh + 1) * 384].reshape(4, 192, 384)
        return carry

    lax.fori_loop(0, FF // tile, back, 0)

    normed, inv = norm_stats(middle_ref[...])
    gsecond = gsecond_ref[...]
    small_ref[:, D : 2 * D] = sum8(gsecond)
    small_ref[:, 2 * D : 3 * D] = sum8(gsecond * normed)
    amp = gain_ref[...].astype(F32) * (1.0 + piece(4))
    grad = spread(gsecond, amp)
    mean = jnp.mean(grad, axis=-1, keepdims=True)
    along = jnp.mean(grad * normed, axis=-1, keepdims=True)
    gmid = cot_ref[...].astype(F32) + (grad - mean - normed * along) * inv
    gmid_ref[...] = gmid
    small_ref[:, 0:D] = sum8(gmid * branch_ref[...])
    gbranch = spread(gmid, piece(2)).astype(BF16)
    gatt = dg(gbranch, w_out_ref[...], NT)

    def d_copy(quarter_x, pick_y, cc, j):
        target = 2 * pick_y + c
        head = (2 * pick_y + cc) * OWN + j
        is_self = jnp.logical_and(target == n, c == cc)
        return (
            is_self,
            dsend.at[head],
            dland.at[j, n],
            d_send.at[head],
            d_recv.at[j, n],
            (target, 2 * z + cc),
        )

    copies = []
    for pair in range(HEADS // 2):
        top = gatt[0:half, pair * 128 : (pair + 1) * 128]
        bottom = gatt[half:local, pair * 128 : (pair + 1) * 128]
        low = lane(top.shape) < 64
        dsend[2 * pair] = jnp.where(low, top, pltpu.roll(bottom, 64, 1)).astype(BF16)
        dsend[2 * pair + 1] = jnp.where(low, pltpu.roll(top, 64, 1), bottom).astype(BF16)
    for head in range(HEADS):
        copies.append(d_copy(None, head // OWN // 2, (head // OWN) % 2, head % OWN))
        send_or_keep(*copies[-1])

    for hh in range(2):
        gout = dg(att_ref[...], gbranch[:, hh * 384 : (hh + 1) * 384], TN).astype(BF16)
        shaped = gout.reshape(8, 2, 48, 384)
        for rh in range(2):
            g_ref[:, rh * 2 + hh, 384:432, :] = shaped[:, rh]

    for j in range(OWN):
        for quarter in range(4):
            wait_bytes(dland.at[j, quarter], d_recv.at[j, quarter])
    do_ref[...] = dland[...]
    for copy in copies:
        wait_send_unless(*copy)


def call_middle(tokens, cot, att, pat, gain, w_out, w_up, b_up, w_down, b_down):
    local = tokens.shape[0]
    half = local // 2
    sds = jax.ShapeDtypeStruct
    return pl.pallas_call(
        middle_kernel,
        out_shape=(
            sds((local, D), BF16),
            sds((local, D), F32),
            sds((8, 4, ROWS_G, COLS_G), BF16),
            sds((8, SMALL), F32),
            sds((OWN, 4, half, 128), BF16),
        ),
        in_specs=[vm()] * 10,
        out_specs=(vm(),) * 5,
        scratch_shapes=[
            VMEM((local, D), BF16),
            VMEM((local, FF), BF16),
            VMEM((local, FF), F32),
            VMEM((local, D), F32),
            VMEM((local, D), F32),
            VMEM((local, D), F32),
            VMEM((local, D), F32),
            VMEM((2, D, local), BF16),
            VMEM((local, D), BF16),
            VMEM((HEADS, half, 128), BF16),
            VMEM((OWN, 4, half, 128), BF16),
            dma(HEADS),
            dma(OWN, 4),
        ],
        compiler_params=params(1, 60),
        cost_estimate=pl.CostEstimate(flops=2 * 10**10, bytes_accessed=3 * 10**7, transcendentals=10**7),
    )(tokens, cot, att, pat, gain, w_out, w_up, b_up, w_down, b_down)


CUT = 320
CHUNK = 24
PARTS_Q = ((0, 384), (384, 256))


def slot_of(other, me):
    return lax.rem(other - me + 3, 4)


def fused_kernel(
    docs_ref,
    tokens_ref,
    cot_ref,
    att_ref,
    cond_ref,
    pat_ref,
    gain_one_ref,
    gain_ref,
    b_up_ref,
    b_down_ref,
    w_ada_hbm,
    w_out_hbm,
    w_up_hbm,
    w_down_hbm,
    q_hbm,
    k_hbm,
    v_hbm,
    all_hbm,
    own_hbm,
    tab_hbm,
    out_ref,
    gtok_ref,
    blocks_ref,
    qkv_a_ref,
    qkv_b_ref,
    packet_ref,
    gcond_ref,
    small_ref,
    small_one,
    dsend,
    dland,
    g_own,
    g_land,
    land_x1,
    land_y1,
    land_x2,
    land_y2,
    land_b1,
    land_a2,
    land_b2,
    block,
    land_block,
    cland,
    rland,
    gq_a,
    gq_b,
    land_qx_a,
    land_qx_b,
    land_qz_a,
    land_qz_b,
    land_q_a,
    land_q_b,
    pack,
    land_s1,
    pack_sum,
    land_s2,
    gc_mine,
    land_gc,
    load_sem,
    d_send,
    d_recv,
    g_send,
    g_recv,
    one_sem,
    two_sem,
    b1_send,
    b1_recv,
    a2_send,
    a2_recv,
    b2_send,
    b2_recv,
    ag_send,
    ag_recv,
    c_send,
    c_recv,
    r_send,
    r_recv,
    qx_sem,
    qz_send,
    qz_recv,
    qp_send,
    qp_recv,
    s1_send,
    s1_recv,
    s2_send,
    s2_recv,
    gc_send,
    gc_recv,
):
    n, ny, nx, z, c = place()
    w = 2 * z + c
    local = tokens_ref.shape[0]
    half = local // 2
    length = local * 4
    group = 2 * ny + c
    tile = 768
    across = n + 1 - 2 * nx
    along_y = lax.rem(n + 2, 4)

    barrier = pltpu.get_barrier_semaphore()

    def greet(device):
        pl.semaphore_signal(barrier, inc=1, device_id=device, device_id_type=MESH)

    me = n * 2 + c
    for step in range(1, 8):
        other = lax.rem(me + step, 8)
        greet((other // 2, 2 * z + lax.rem(other, 2)))
    for step in range(1, 4):
        greet((n, 2 * lax.rem(z + step, 4) + c))
    for row in range(8):

        @pl.when(jnp.logical_not(jnp.logical_and(z == n, row == w)))
        def _():
            greet((z, row))

    def others(base):
        return [lax.rem(base + step, 4) for step in (1, 2, 3)]

    def piece(index):
        return pat_ref[:, index * D : (index + 1) * D]

    def spread(values, pattern):
        return flat8(by8(values) * pattern[None])


    def core_up(g_give, t):
        return remote(
            g_give.at[:, t // 2, t % 2, pl.ds(0, 192)],
            g_land.at[:, t // 2, t % 2, pl.ds(0, 192)],
            g_send.at[t],
            g_recv.at[t],
            sibling(n, z, c),
        )

    def core_down(g_give, t):
        return remote(
            g_give.at[t, :, :, pl.ds(192, 192)],
            g_land.at[t, :, :, pl.ds(192, 192)],
            g_send.at[4 + t],
            g_recv.at[4 + t],
            sibling(n, z, c),
        )

    def core_out(g_give):
        return remote(
            g_give.at[:, :, :, pl.ds(384, 48)],
            g_land.at[:, :, :, pl.ds(384, 48)],
            g_send.at[8],
            g_recv.at[8],
            sibling(n, z, c),
        )

    def d_copy(head):
        pick_y, cc, j = head // OWN // 2, head // OWN % 2, head % OWN
        target = 2 * pick_y + c
        is_self = jnp.logical_and(target == n, c == cc)
        return (
            is_self,
            dsend.at[head],
            dland.at[j, n],
            d_send.at[head],
            d_recv.at[j, n],
            (target, 2 * z + cc),
        )


    def middle(
        w_out, w_up, w_down, active, slope, acc, branch_ref, lhs_t, low_ref, g_give
    ):
        loads = [
            pltpu.make_async_copy(src, dst, load_sem.at[i])
            for i, (src, dst) in enumerate(((w_out_hbm, w_out), (w_up_hbm, w_up), (w_down_hbm, w_down)))
        ]
        for load in loads:
            load.start()
        loads[0].wait()
        branch_ref[...] = dg(att_ref[...], w_out[...], NN)

        def middle_values():
            return tokens_ref[...].astype(F32) + spread(branch_ref[...], piece(2))

        normed, _ = norm_stats(middle_values())
        amp = gain_ref[...].astype(F32) * (1.0 + piece(4))
        low_ref[...] = flat8(by8(normed) * amp[None] + piece(3)[None]).astype(BF16)
        acc[...] = jnp.broadcast_to(b_down_ref[...].astype(F32), acc.shape)
        loads[1].wait()
        loads[2].wait()

        def up(t, carry):
            cols = pl.ds(pl.multiple_of(t * tile, tile), tile)
            hidden = dg(low_ref[...], w_up[:, cols], NN) + b_up_ref[:, cols].astype(F32)
            square = hidden * hidden
            bend = jnp.tanh(0.7978845608028654 * hidden * (1.0 + 0.044715 * square))
            part = 0.5 * (1.0 + bend)
            active[:, cols] = (hidden * part).astype(BF16)
            slope[:, cols] = part + (0.5 * 0.7978845608028654) * hidden * (1.0 - bend * bend) * (
                1.0 + 3.0 * 0.044715 * square
            )
            acc[...] += dg(active[:, cols], w_down[cols, :], NN)
            return carry

        lax.fori_loop(0, FF // tile, up, 0)

        cot = cot_ref[...].astype(F32)
        down = acc[...]
        out_ref[...] = (middle_values() + spread(down, piece(5))).astype(BF16)
        small_ref[:, 3 * D : 4 * D] = sum8(cot * down)
        lhs_t[0] = low_ref[...].T
        gdown = spread(cot, piece(5)).astype(BF16)
        low_ref[...] = gdown
        small_ref[:, 4 * D + FF :] = sum8(gdown.astype(F32))
        lhs_t[1] = gdown.T
        acc[...] = jnp.zeros_like(acc)

        def back(t, carry):
            cols = pl.ds(pl.multiple_of(t * tile, tile), tile)
            ghidden = dg(low_ref[...], w_down[cols, :], NT) * slope[:, cols]
            low = ghidden.astype(BF16)
            small_ref[:, pl.ds(pl.multiple_of(4 * D + t * tile, tile), tile)] = sum8(low.astype(F32))
            acc[...] += dg(low, w_up[:, cols], NT)
            gup = dg(lhs_t[0], low, NN).astype(BF16).reshape(4, 2, 96, tile)
            mine = jnp.where(c == 0, gup[:, 0], gup[:, 1])
            other = jnp.where(c == 0, gup[:, 1], gup[:, 0])
            for hh in range(2):
                rows, lanes_h = slice(hh * 96, (hh + 1) * 96), slice(hh * 384, (hh + 1) * 384)
                g_own[:, t // 2, t % 2, rows, :] = mine[:, :, lanes_h]
                g_give[:, t // 2, t % 2, rows, :] = other[:, :, lanes_h]
            core_up(g_give, t).start()
            gdw = dg(lhs_t[1], active[:, cols], NN).astype(BF16)
            mine = jnp.where(c == 0, gdw[:, :384], gdw[:, 384:])
            other = jnp.where(c == 0, gdw[:, 384:], gdw[:, :384])
            g_own[t, :, :, 192:384, :] = mine.reshape(2, 2, 192, 384)
            g_give[t, :, :, 192:384, :] = other.reshape(2, 2, 192, 384)
            core_down(g_give, t).start()
            return carry

        lax.fori_loop(0, FF // tile, back, 0)

        normed, inv = norm_stats(middle_values())
        gsecond = acc[...]
        small_ref[:, D : 2 * D] = sum8(gsecond)
        small_ref[:, 2 * D : 3 * D] = sum8(gsecond * normed)
        grad = spread(gsecond, gain_ref[...].astype(F32) * (1.0 + piece(4)))
        mean = jnp.mean(grad, axis=-1, keepdims=True)
        along = jnp.mean(grad * normed, axis=-1, keepdims=True)
        gmid = cot_ref[...].astype(F32) + (grad - mean - normed * along) * inv
        gtok_ref[...] = gmid
        small_ref[:, 0:D] = sum8(gmid * branch_ref[...])
        gbranch = spread(gmid, piece(2)).astype(BF16)
        gatt = dg(gbranch, w_out[...], NT)
        for pair in range(HEADS // 2):
            top = gatt[0:half, pair * 128 : (pair + 1) * 128]
            bottom = gatt[half:local, pair * 128 : (pair + 1) * 128]
            lower = lane(top.shape) < 64
            dsend[2 * pair] = jnp.where(lower, top, pltpu.roll(bottom, 64, 1)).astype(BF16)
            dsend[2 * pair + 1] = jnp.where(lower, pltpu.roll(top, 64, 1), bottom).astype(BF16)
        for j in range(OWN):
            for g in range(4):
                send_or_keep(*d_copy(g * OWN + j))

        for hh in range(2):
            gout = dg(att_ref[...], gbranch[:, hh * 384 : (hh + 1) * 384], TN).astype(BF16)
            shaped = gout.reshape(4, 2, 2, 48, 384)
            g_own[:, :, hh, 384:432, :] = jnp.where(c == 0, shaped[:, 0], shaped[:, 1])
            g_give[:, :, hh, 384:432, :] = jnp.where(c == 0, shaped[:, 1], shaped[:, 0])
        core_out(g_give).start()
        for t in range(4):
            core_up(g_give, t).wait_send()
            core_down(g_give, t).wait_send()
        core_out(g_give).wait_send()

    pl.semaphore_wait(barrier, jnp.where(z == n, 17, 18))
    pl.run_scoped(
        middle,
        VMEM((D, D), BF16),
        VMEM((D, FF), BF16),
        VMEM((FF, D), BF16),
        VMEM((local, FF), BF16),
        VMEM((local, FF), F32),
        VMEM((local, D), F32),
        VMEM((local, D), F32),
        VMEM((2, D, local), BF16),
        VMEM((local, D), BF16),
        VMEM((4, 2, 2, ROWS_G, COLS_G), BF16),
    )


    top = pl.ds(0, CUT)
    rest = pl.ds(CUT, ROWS_G - CUT)

    def one_x():
        return remote(g_own.at[pl.ds(0, 2), :, 1 - nx, top], land_x1, one_sem.at[0], one_sem.at[1], (across, w))

    def one_y():
        return remote(
            g_own.at[pl.ds(2, 2), 1 - ny, :, top], land_y1, one_sem.at[2], one_sem.at[3], (along_y, w)
        )

    def two_y():
        return remote(
            g_own.at[pl.ds(0, 2), 1 - ny, nx, top], land_y2, two_sem.at[0], two_sem.at[1], (along_y, w)
        )

    def two_x():
        return remote(
            g_own.at[pl.ds(2, 2), ny, 1 - nx, top], land_x2, two_sem.at[2], two_sem.at[3], (across, w)
        )

    def b1_copy(chip):
        slot = slot_of(chip, z)
        return remote(
            g_own.at[chip, :, :, rest], land_b1.at[slot], b1_send.at[slot], b1_recv.at[slot],
            (n, 2 * chip + c),
        )

    def a2_copy(chip):
        slot = slot_of(chip, z)
        return remote(
            g_own.at[chip, ny, nx, top], land_a2.at[slot], a2_send.at[slot], a2_recv.at[slot],
            (n, 2 * chip + c),
        )

    def b2_copy(other):
        slot = slot_of(other, n)
        return remote(
            g_own.at[z, other // 2, lax.rem(other, 2), rest], land_b2.at[slot], b2_send.at[slot],
            b2_recv.at[slot], (other, w),
        )

    def ag_copy(other):
        return remote(block, land_block.at[n], ag_send.at[slot_of(other, n)], ag_recv.at[n], (other, w))

    def core_finish():
        for t in range(4):
            wait_bytes(g_land.at[:, t // 2, t % 2, pl.ds(0, 192)], g_recv.at[t])
            wait_bytes(g_land.at[t, :, :, pl.ds(192, 192)], g_recv.at[4 + t])
        wait_bytes(g_land.at[:, :, :, pl.ds(384, 48)], g_recv.at[8])

        def add(i, carry):
            chip, y, x = i // 4, lax.rem(i // 2, 2), lax.rem(i, 2)
            g_own[chip, y, x] = (
                g_own[chip, y, x].astype(F32) + g_land[chip, y, x].astype(F32)
            ).astype(BF16)
            return carry

        lax.fori_loop(0, 16, add, 0)
        one_x().start()
        one_y().start()
        for chip in others(z):
            b1_copy(chip).start()

    def stage_two():
        one_x().wait_recv()
        one_y().wait_recv()
        for i in range(2):
            for k in range(2):
                g_own[i, k, nx, 0:CUT] = (
                    g_own[i, k, nx, 0:CUT].astype(F32) + land_x1[i, k].astype(F32)
                ).astype(BF16)
                g_own[2 + i, ny, k, 0:CUT] = (
                    g_own[2 + i, ny, k, 0:CUT].astype(F32) + land_y1[i, k].astype(F32)
                ).astype(BF16)
        two_y().start()
        two_x().start()

    def stage_a2():
        two_y().wait_recv()
        two_x().wait_recv()
        for i in range(2):
            g_own[i, ny, nx, 0:CUT] = (
                g_own[i, ny, nx, 0:CUT].astype(F32) + land_y2[i].astype(F32)
            ).astype(BF16)
            g_own[2 + i, ny, nx, 0:CUT] = (
                g_own[2 + i, ny, nx, 0:CUT].astype(F32) + land_x2[i].astype(F32)
            ).astype(BF16)
        for chip in others(z):
            a2_copy(chip).start()

    def stage_b2():
        for slot in range(3):
            wait_bytes(land_b1.at[slot], b1_recv.at[slot])
        for part in range(4):
            total = g_own[z, part // 2, part % 2, CUT:ROWS_G].astype(F32)
            for slot in range(3):
                total = total + land_b1[slot, part // 2, part % 2].astype(F32)
            g_own[z, part // 2, part % 2, CUT:ROWS_G] = total.astype(BF16)
        for other in others(n):
            b2_copy(other).start()

    def last():
        for slot in range(3):
            wait_bytes(land_a2.at[slot], a2_recv.at[slot])
            wait_bytes(land_b2.at[slot], b2_recv.at[slot])
        upper = g_own[z, ny, nx, 0:CUT].astype(F32)
        lower = g_own[z, ny, nx, CUT:ROWS_G].astype(F32)
        for slot in range(3):
            upper = upper + land_a2[slot].astype(F32)
            lower = lower + land_b2[slot].astype(F32)
        block[0:CUT] = upper.astype(BF16)
        block[CUT:ROWS_G] = lower.astype(BF16)
        for other in others(n):
            ag_copy(other).start()


    bufs_q = ((gq_a, land_qx_a, land_qz_a, land_q_a), (gq_b, land_qx_b, land_qz_b, land_q_b))

    def qx_copy(p):
        gq, land_x, _, _ = bufs_q[p]
        return remote(gq.at[:, 1 - nx], land_x, qx_sem.at[p, 0], qx_sem.at[p, 1], (across, w))

    def qz_copy(p, chip):
        gq, _, land_z, _ = bufs_q[p]
        slot = slot_of(chip, z)
        return remote(
            gq.at[chip, nx], land_z.at[slot], qz_send.at[p, slot], qz_recv.at[p, slot],
            (n, 2 * chip + c),
        )

    def qp_copy(p, other):
        gq, _, _, land = bufs_q[p]
        is_self = jnp.logical_and(other == n, nx == c)
        return (
            is_self, gq.at[z, nx], land.at[group], qp_send.at[p, other], qp_recv.at[p, group],
            (other, 2 * z + nx),
        )

    def q_z(p):
        gq, land_x, _, _ = bufs_q[p]
        qx_copy(p).wait_recv()
        for chip in range(4):
            gq[chip, nx] = (gq[chip, nx].astype(F32) + land_x[chip].astype(F32)).astype(BF16)
        for chip in others(z):
            qz_copy(p, chip).start()

    def q_plane(p):
        gq, _, land_z, _ = bufs_q[p]
        for slot in range(3):
            wait_bytes(land_z.at[slot], qz_recv.at[p, slot])
        total = gq[z, nx].astype(F32)
        for slot in range(3):
            total = total + land_z[slot].astype(F32)
        gq[z, nx] = total.astype(BF16)
        for other in range(4):
            send_or_keep(*qp_copy(p, other))


    def s1_copy(other):
        return remote(
            pack.at[pl.ds(2 * other, 2)], land_s1.at[n], s1_send.at[slot_of(other, n)],
            s1_recv.at[n], (other, w),
        )

    def gc_copy(other):
        return remote(
            gc_mine, land_gc.at[n], gc_send.at[slot_of(other, n)], gc_recv.at[n], (other, w)
        )

    def s2_copy(index):
        i, other = index // 4, lax.rem(index, 4)
        is_self = jnp.logical_and(other == n, w == 2 * n + i)
        return (
            is_self, pack_sum.at[i], land_s2.at[w], s2_send.at[index], s2_recv.at[w],
            (other, 2 * n + i),
        )

    def small_sums(w_ada_ref):

        two = docs_ref[0] == DOCS
        even_rows = lax.rem(lax.broadcasted_iota(jnp.int32, (8, D), 0), 2) == 0

        def even_odd(values):
            even = jnp.sum(jnp.where(even_rows, values, 0.0), axis=0, keepdims=True)
            return even, jnp.sum(jnp.where(even_rows, 0.0, values), axis=0, keepdims=True)

        pack[...] = jnp.zeros_like(pack)
        gc_mine[...] = jnp.zeros_like(gc_mine)

        def put(chunk, row, values, s):
            pack[chunk, row : row + 1, 0:96] = values[:, 96 * s : 96 * s + 96]

        raws = [
            small_one[:, 0:D],
            small_one[:, D : 2 * D],
            small_ref[:, 0:D],
            small_ref[:, D : 2 * D],
            small_ref[:, 2 * D : 3 * D],
            small_ref[:, 3 * D : 4 * D],
        ]
        gains = {1: gain_one_ref, 4: gain_ref}
        for piece in range(6):
            even, odd = even_odd(raws[piece])
            if piece in gains:
                scale = pat_ref[:, piece * D : (piece + 1) * D]
                gain_sum = even * (1.0 + scale[0:1]) + odd * (1.0 + scale[1:2])
                for s in range(8):
                    put(s, 12 if piece == 1 else 13, gain_sum, s)
                gain = gains[piece][...].astype(F32)
                even, odd = even * gain, odd * gain
            first_doc = jnp.where(two, even, even + odd)
            second_doc = jnp.where(two, odd, 0.0)
            for s in range(8):
                at = 8 * piece + s
                put(at // 6, at % 6, first_doc, s)
                put(at // 6, 6 + at % 6, second_doc, s)
            pieces = [*split3(first_doc), *split3(second_doc)]
            stacked = jnp.concatenate([*pieces, jnp.zeros((10, D), F32)], axis=0).astype(BF16)
            part = dg(stacked, w_ada_ref[:, piece * D : (piece + 1) * D], NT)
            gc_mine[0:1] += part[0:1] + part[1:2] + part[2:3]
            gc_mine[1:2] += part[3:4] + part[4:5] + part[5:6]
        for s in range(32):
            col = 4 * D + 96 * s
            row = jnp.sum(small_ref[:, col : col + 96], axis=0, keepdims=True)
            pack[s // 4, 14 + s % 4 : 15 + s % 4, 0:96] = row
        for s in range(8):
            col = 4 * D + FF + 96 * s
            pack[s, 18:19, 0:96] = jnp.sum(small_ref[:, col : col + 96], axis=0, keepdims=True)

        for other in others(n):
            s1_copy(other).start()
            gc_copy(other).start()
        land_gc[n] = gc_mine[...]
        land_s1[n] = pack[pl.ds(2 * n, 2)]
        for other in others(n):
            wait_bytes(land_s1.at[other], s1_recv.at[other])
        total = land_s1[0] + land_s1[1] + land_s1[2] + land_s1[3]
        pack_sum[...] = total
        cond = cond_ref[...].astype(F32)
        for i in range(2):
            pack_sum[i, 19:21, :] = cond

        for index in range(8):
            send_or_keep(*s2_copy(index))


    def heads(
        q_ref, k_ref, v_ref, all_ref, own_ref, tab_ref, w_ada_ref, packed, acc_k, acc_v, acc_w, kept, csend
    ):
        def c_copy(quarter):
            return remote(
                csend.at[quarter], cland.at[quarter], c_send.at[quarter], c_recv.at[quarter],
                sibling(n, z, c),
            )

        def r_copy(quarter):
            is_self = jnp.logical_and(quarter == n, nx == c)
            return (
                is_self,
                csend.at[quarter],
                rland.at[ny, pl.ds(pl.multiple_of(c * half, half), half)],
                r_send.at[quarter],
                r_recv.at[ny, c],
                (quarter, 2 * z + nx),
            )

        loads = [
            pltpu.make_async_copy(src, dst, load_sem.at[i])
            for i, (src, dst) in enumerate(
                (
                    (q_hbm, q_ref),
                    (k_hbm, k_ref),
                    (v_hbm, v_ref),
                    (tab_hbm, tab_ref),
                    (all_hbm, all_ref),
                    (own_hbm, own_ref),
                    (w_ada_hbm, w_ada_ref),
                )
            )
        ]
        for load in loads:
            load.start()
        core_finish()
        for load in loads[:4]:
            load.wait()
        lanes_h = lane((half, 128))
        lanes = lane((local, 128))

        def turned(values, rows):
            cosine, sine = cos_sin(tab_ref[rows, :])
            return values * cosine - halves_turn(values) * sine

        def rounded(values):
            return values.astype(BF16).astype(F32)

        def weights(p):
            gq = bufs_q[p][0]
            at, width = PARTS_Q[p]
            if p == 0:
                loads[4].wait()
            acc_w[:, 0:width] = dg(all_ref[0:local, :], packed[0:local, at : at + width], TN)

            def step(i, carry):
                rows = pl.ds(pl.multiple_of(i * local, local), local)
                acc_w[:, 0:width] += dg(all_ref[rows, :], packed[rows, at : at + width], TN)
                return carry

            lax.fori_loop(1, 4, step, 0)
            gq[...] = acc_w[:, 0:width].astype(BF16).reshape(gq.shape)
            qx_copy(p).start()

        hooks = {(1, 4): stage_two, (2, 2): stage_a2, (2, 4): stage_b2, (2, 6): lambda: q_z(0)}
        for j in range(OWN):
            for quarter in range(4):
                wait_bytes(dland.at[j, quarter], d_recv.at[j, quarter])
            acc_k[...] = jnp.zeros_like(acc_k)
            acc_v[...] = jnp.zeros_like(acc_v)

            def step(i, carry):
                for (at_j, at_i), hook in hooks.items():
                    if at_j == j:
                        pl.when(i == at_i)(hook)
                rows = pl.ds(pl.multiple_of(i * half, half), half)
                grad = pltpu.roll(dland[j, i // 2].astype(F32), lax.rem(i, 2) * 64, 1)
                grad = jnp.where(lanes_h < 64, grad, 0.0).astype(BF16)
                query = q_ref[j, rows, :]
                probs = jnp.exp2(dg(query, k_ref[j], NT) * LOG2E)
                gprobs = probs * dg(grad, v_ref[j], NT)
                scores = (gprobs - probs * jnp.sum(gprobs, axis=1, keepdims=True)).astype(BF16)
                probs = probs.astype(BF16)
                gquery = rounded(dg(scores, k_ref[j], NN) * HEAD_DIM**-0.5)
                packed[rows, Q_AT[j] : Q_AT[j] + 64] = turned(gquery, rows)[:, :64].astype(BF16)
                acc_v[...] += dg(grad.T[:64], probs, NN)
                acc_k[...] += dg(query.T[:64], scores, NN)
                return carry

            lax.fori_loop(0, 8, step, 0)

            def finish(i, carry):
                rows = pl.ds(pl.multiple_of(i * local, local), local)
                both = rounded(jnp.concatenate([acc_k[:, rows], acc_v[:, rows]], axis=0).T)
                packed[rows, KV_AT[j] : KV_AT[j] + 128] = jnp.where(
                    lanes < 64, turned(both, rows), both
                ).astype(BF16)
                return carry

            lax.fori_loop(0, 4, finish, 0)
            if j == 1:
                weights(0)
        packed[:, 576:640] = jnp.zeros((length, 64), BF16)

        def rows_of(quarter, hh):
            return pl.ds(pl.multiple_of(quarter * local + hh * half, half), half)

        def order(i):
            return lax.rem(n + 3 - i, 4)

        loads[5].wait()

        def give(i, carry):
            quarter = order(i)
            csend[quarter] = dg(packed[rows_of(quarter, 1 - c), :], own_ref[...], NT).astype(BF16)
            c_copy(quarter).start()
            return carry

        lax.fori_loop(0, 4, give, 0)

        def keep(i, carry):
            quarter = order(i)
            kept[quarter] = dg(packed[rows_of(quarter, c), :], own_ref[...], NT)
            return carry

        lax.fori_loop(0, 4, keep, 0)

        def add(i, carry):
            quarter = order(i)
            c_copy(quarter).wait()
            csend[quarter] = (kept[quarter] + cland[quarter].astype(F32)).astype(BF16)
            send_or_keep(*r_copy(quarter))
            return carry

        lax.fori_loop(0, 4, add, 0)
        weights(1)
        last()
        q_z(1)
        normed, inv = norm_stats(tokens_ref[...].astype(F32))
        q_plane(0)

        for y in range(2):
            for hh in range(2):
                wait_bytes(rland.at[y, pl.ds(hh * half, half)], r_recv.at[y, hh])
        gfirst = rland[0].astype(F32) + rland[1].astype(F32)
        small_one[:, 0:D] = sum8(gfirst)
        small_one[:, D : 2 * D] = sum8(gfirst * normed)
        grad = spread(gfirst, gain_one_ref[...].astype(F32) * (1.0 + piece(1)))
        mean = jnp.mean(grad, axis=-1, keepdims=True)
        along = jnp.mean(grad * normed, axis=-1, keepdims=True)
        gtok_ref[...] += (grad - mean - normed * along) * inv
        loads[6].wait()
        small_sums(w_ada_ref)

        q_plane(1)
        for quarter in range(4):
            wait_send_unless(*r_copy(quarter))

    pl.run_scoped(
        heads,
        VMEM((OWN, length, 128), BF16),
        VMEM((OWN, length, 128), BF16),
        VMEM((OWN, length, 128), BF16),
        VMEM((length, D), BF16),
        VMEM((D, WCOLS), BF16),
        VMEM((length, 128), F32),
        VMEM(w_ada_hbm.shape, BF16),
        VMEM((length, WCOLS), BF16),
        VMEM((64, length), F32),
        VMEM((64, length), F32),
        VMEM((D, 384), F32),
        VMEM((4, half, D), F32),
        VMEM((4, half, D), BF16),
    )

    for other in others(n):
        wait_bytes(land_gc.at[other], gc_recv.at[other])
    gcond_ref[...] = land_gc[0] + land_gc[1] + land_gc[2] + land_gc[3]
    for row in range(8):
        wait_bytes(land_s2.at[row], s2_recv.at[row])
    packet_ref[...] = land_s2[...]
    land_block[n] = block[...]
    for other in others(n):
        wait_bytes(land_block.at[other], ag_recv.at[other])
    move = pltpu.make_async_copy(land_block, blocks_ref, load_sem.at[0])
    move.start()
    for p in range(2):
        for g in range(4):
            wait_bytes(bufs_q[p][3].at[g], qp_recv.at[p, g])
    moves = [
        move,
        pltpu.make_async_copy(land_q_a, qkv_a_ref, load_sem.at[1]),
        pltpu.make_async_copy(land_q_b, qkv_b_ref, load_sem.at[2]),
    ]
    for later in moves[1:]:
        later.start()


    for later in moves:
        later.wait()
    for head in range(HEADS):
        wait_send_unless(*d_copy(head))
    for copy in (one_x(), one_y(), two_x(), two_y(), qx_copy(0), qx_copy(1)):
        copy.wait_send()

    def drain(quarter, carry):
        for p in range(2):
            wait_send_unless(*qp_copy(p, quarter))
        return carry

    lax.fori_loop(0, 4, drain, 0)
    for i in range(3):
        other, chip = others(n)[i], others(z)[i]
        b1_copy(chip).wait_send()
        a2_copy(chip).wait_send()
        b2_copy(other).wait_send()
        ag_copy(other).wait_send()
        qz_copy(0, chip).wait_send()
        qz_copy(1, chip).wait_send()
        s1_copy(other).wait_send()
        gc_copy(other).wait_send()
    for index in range(8):
        wait_send_unless(*s2_copy(index))


def call_fused(
    docs, tokens, cot, att, cond, pat, gain_one, gain_two, b_up, b_down, w_ada, w_out, w_up, w_down,
    q, k, v, everything, own, tab,
):
    local = tokens.shape[0]
    half = local // 2
    sds = jax.ShapeDtypeStruct
    rest = ROWS_G - CUT
    wide_a, wide_b = PARTS_Q[0][1], PARTS_Q[1][1]

    def low(*shape):
        return VMEM(shape, BF16)

    return pl.pallas_call(
        fused_kernel,
        out_shape=(
            sds((local, D), BF16),
            sds((local, D), F32),
            sds((4, ROWS_G, COLS_G), BF16),
            sds((4, 96, wide_a), BF16),
            sds((4, 96, wide_b), BF16),
            sds((8, CHUNK, 128), F32),
            sds((8, 128), F32),
        ),
        in_specs=[smem()] + [vm()] * 9 + [hbm()] * 10,
        out_specs=(vm(), vm(), hbm(), hbm(), hbm(), vm(), vm()),
        scratch_shapes=[
            VMEM((8, SMALL), F32),
            VMEM((8, 2 * D), F32),
            low(HEADS, half, 128),
            low(OWN, 4, half, 128),
            low(4, 2, 2, ROWS_G, COLS_G),
            low(4, 2, 2, ROWS_G, COLS_G),
            low(2, 2, CUT, COLS_G),
            low(2, 2, CUT, COLS_G),
            low(2, CUT, COLS_G),
            low(2, CUT, COLS_G),
            low(3, 2, 2, rest, COLS_G),
            low(3, CUT, COLS_G),
            low(3, rest, COLS_G),
            low(ROWS_G, COLS_G),
            low(4, ROWS_G, COLS_G),
            low(4, half, D),
            low(2, local, D),
            low(4, 2, 96, wide_a),
            low(4, 2, 96, wide_b),
            low(4, 96, wide_a),
            low(4, 96, wide_b),
            low(3, 96, wide_a),
            low(3, 96, wide_b),
            low(4, 96, wide_a),
            low(4, 96, wide_b),
            VMEM((8, CHUNK, 128), F32),
            VMEM((4, 2, CHUNK, 128), F32),
            VMEM((2, CHUNK, 128), F32),
            VMEM((8, CHUNK, 128), F32),
            VMEM((8, 128), F32),
            VMEM((4, 8, 128), F32),
            dma(7),
            dma(HEADS),
            dma(OWN, 4),
            dma(9),
            dma(9),
            dma(4),
            dma(4),
            dma(3),
            dma(3),
            dma(3),
            dma(3),
            dma(3),
            dma(3),
            dma(3),
            dma(4),
            dma(4),
            dma(4),
            dma(4),
            dma(2, 2),
            dma(2, 2),
            dma(2, 3),
            dma(2, 3),
            dma(2, 4),
            dma(2, 4),
            dma(3),
            dma(4),
            dma(8),
            dma(8),
            dma(3),
            dma(4),
        ],
        compiler_params=params(3, 63),
        cost_estimate=pl.CostEstimate(flops=4 * 10**10, bytes_accessed=5 * 10**7, transcendentals=10**7),
    )(
        docs, tokens, cot, att, cond, pat, gain_one, gain_two, b_up, b_down, w_ada, w_out, w_up, w_down,
        q, k, v, everything, own, tab,
    )


def finish_kernel(
    output_in, gtok_in, blocks, qkv_a, qkv_b, packet, output_out, gtok_out, gqkv, gout, gup, gdown, gada, gvec
):
    output_out[...] = output_in[...]
    gtok_out[...] = gtok_in[...]
    for part in range(4):
        for hh in range(2):
            at = part * 768 + hh * 384
            gup[:, at : at + 384] = blocks[part, hh * 96 : (hh + 1) * 96, :].astype(F32)
        rh, ch = part // 2, part % 2
        gout[rh * 48 : (rh + 1) * 48, ch * 384 : (ch + 1) * 384] = blocks[part, 384:432, :].astype(F32)
    for pair in range(2):
        both = jnp.concatenate(
            [blocks[2 * pair, 192:384, :], blocks[2 * pair + 1, 192:384, :]], axis=0
        ).astype(F32)
        gdown[:, pair * 384 : (pair + 1) * 384] = both.T

    def head_block(part, head):
        g, j = head // OWN, head % OWN
        if part == 0:
            at, upper = Q_AT[j] // 128 * 128, j % 2
        else:
            at, upper = KV_AT[j], part - 1
        qkv, start = (qkv_a, 0) if at < PARTS_Q[1][0] else (qkv_b, PARTS_Q[1][0])
        return qkv[g, :, at - start : at - start + 128].astype(F32), upper

    for part in range(3):
        for pair in range(HEADS // 2):
            even, up = head_block(part, 2 * pair)
            even = pltpu.roll(even, 64, 1) if up else even
            odd, up = head_block(part, 2 * pair + 1)
            odd = odd if up else pltpu.roll(odd, 64, 1)
            at = part * D + pair * 128
            gqkv[:, at : at + 128] = jnp.where(lane(even.shape) < 64, even, odd)

    conds = [packet[:, 19, :], packet[:, 20, :]]
    lhs = jnp.concatenate([conds[0]] * 3 + [conds[1]] * 3, axis=0).astype(BF16)
    for k in range(6):
        first, second = packet[:, k, :], packet[:, 6 + k, :]
        rhs = jnp.concatenate([*split3(first), *split3(second)], axis=0).astype(BF16)
        gada[:, 96 * k : 96 * k + 96] = dg(lhs, rhs, TN)[:, :96]
        gvec[0:1, 96 * k : 96 * k + 96] = jnp.sum(first + second, axis=0, keepdims=True)[:, :96]
    for row, at, k in ((1, 0, 12), (2, 0, 13), (3, 0, 14), (3, 1, 15), (3, 2, 16), (3, 3, 17), (4, 0, 18)):
        gvec[row : row + 1, 96 * at : 96 * at + 96] = jnp.sum(packet[:, k, :], axis=0, keepdims=True)[
            :, :96
        ]


def call_finish(output, gtok, blocks, qkv_a, qkv_b, packet):
    local = output.shape[0]
    sds = jax.ShapeDtypeStruct
    return pl.pallas_call(
        finish_kernel,
        out_shape=(
            sds((local, D), BF16),
            sds((local, D), F32),
            sds((96, 3 * D), F32),
            sds((96, D), F32),
            sds((96, FF), F32),
            sds((384, D), F32),
            sds((128, 576), F32),
            sds((8, 576), F32),
        ),
        in_specs=[vm()] * 6,
        out_specs=(vm(),) * 8,
        compiler_params=pltpu.CompilerParams(vmem_limit_bytes=40 * 2**20),
        cost_estimate=pl.CostEstimate(flops=10**7, bytes_accessed=10**7, transcendentals=0),
    )(output, gtok, blocks, qkv_a, qkv_b, packet)


def plain_backward_kernel(
    tokens_ref,
    pat_ref,
    gain_ref,
    gmid_ref,
    do_ref,
    q_ref,
    k_ref,
    v_ref,
    all_ref,
    own_ref,
    tab_ref,
    gtok_ref,
    gq_ref,
    small_ref,
    packed,
    acc_k,
    acc_v,
    acc_w,
    kept,
    csend,
    cland,
    rsend,
    rland,
    c_send,
    c_recv,
    r_send,
    r_recv,
):
    n, ny, nx, z, c = place()
    local = tokens_ref.shape[0]
    half = local // 2
    length = 4 * local
    plane_barrier(n, z, c)
    lanes = lane((local, 128))

    def turned(values, rows):
        cosine, sine = cos_sin(tab_ref[rows, :])
        return values * cosine - halves_turn(values) * sine

    def rounded(values):
        return values.astype(BF16).astype(F32)

    for j in range(OWN):
        acc_k[...] = jnp.zeros_like(acc_k)
        acc_v[...] = jnp.zeros_like(acc_v)

        def quarter_step(i, carry):
            rows = pl.ds(pl.multiple_of(i * local, local), local)
            block = do_ref[j, i].astype(F32)
            grad = jnp.concatenate([block, pltpu.roll(block, 64, 1)], axis=0)
            grad = jnp.where(lanes < 64, grad, 0.0).astype(BF16)
            query = q_ref[j, rows, :]
            probs = jnp.exp2(dg(query, k_ref[j], NT) * LOG2E)
            gprobs = probs * dg(grad, v_ref[j], NT)
            scores = (gprobs - probs * jnp.sum(gprobs, axis=1, keepdims=True)).astype(BF16)
            probs = probs.astype(BF16)
            gquery = rounded(dg(scores, k_ref[j], NN) * HEAD_DIM**-0.5)
            at = Q_AT[j]
            packed[rows, at : at + 64] = turned(gquery, rows)[:, :64].astype(BF16)
            acc_v[...] += dg(grad.T[:64], probs, NN)
            acc_k[...] += dg(query.T[:64], scores, NN)
            return carry

        lax.fori_loop(0, 4, quarter_step, 0)

        def finish(i, carry):
            rows = pl.ds(pl.multiple_of(i * local, local), local)
            both = jnp.concatenate([acc_k[:, rows], acc_v[:, rows]], axis=0).T
            both = rounded(both)
            packed[rows, KV_AT[j] : KV_AT[j] + 128] = jnp.where(
                lanes < 64, turned(both, rows), both
            ).astype(BF16)
            return carry

        lax.fori_loop(0, 4, finish, 0)
    packed[:, 576:640] = jnp.zeros((length, 64), BF16)

    def rows_of(quarter, hh):
        return pl.ds(pl.multiple_of(quarter * local + hh * half, half), half)

    def c_copy(quarter):
        return remote(
            csend.at[quarter], cland.at[quarter], c_send.at[quarter], c_recv.at[quarter],
            sibling(n, z, c),
        )

    def r_copy(quarter):
        is_self = jnp.logical_and(quarter == n, nx == c)
        return (
            is_self,
            rsend.at[quarter],
            rland.at[ny, pl.ds(pl.multiple_of(c * half, half), half)],
            r_send.at[quarter],
            r_recv.at[ny, c],
            (quarter, 2 * z + nx),
        )

    def order(i):
        return lax.rem(n + 3 - i, 4)

    def give(i, carry):
        quarter = order(i)
        csend[quarter] = dg(packed[rows_of(quarter, 1 - c), :], own_ref[...], NT).astype(BF16)
        c_copy(quarter).start()
        return carry

    lax.fori_loop(0, 4, give, 0)

    def keep(i, carry):
        quarter = order(i)
        kept[quarter] = dg(packed[rows_of(quarter, c), :], own_ref[...], NT)
        return carry

    lax.fori_loop(0, 4, keep, 0)

    def add(i, carry):
        quarter = order(i)
        wait_bytes(cland.at[quarter], c_recv.at[quarter])
        rsend[quarter] = (kept[quarter] + cland[quarter].astype(F32)).astype(BF16)
        send_or_keep(*r_copy(quarter))
        return carry

    lax.fori_loop(0, 4, add, 0)

    acc_w[...] = jnp.zeros_like(acc_w)

    def weights(i, carry):
        rows = pl.ds(pl.multiple_of(i * local, local), local)
        acc_w[...] += dg(all_ref[rows, :], packed[rows, :], TN)
        return carry

    lax.fori_loop(0, 4, weights, 0)
    gq_ref[...] = acc_w[...].astype(BF16).reshape(gq_ref.shape)

    normed, inv = norm_stats(tokens_ref[...].astype(F32))
    for y in range(2):
        for hh in range(2):
            wait_bytes(rland.at[y, pl.ds(hh * half, half)], r_recv.at[y, hh])
    gfirst = rland[0].astype(F32) + rland[1].astype(F32)
    small_ref[:, 0:D] = sum8(gfirst)
    small_ref[:, D : 2 * D] = sum8(gfirst * normed)
    amp = gain_ref[...].astype(F32) * (1.0 + pat_ref[:, D : 2 * D])
    grad = flat8(by8(gfirst) * amp[None])
    mean = jnp.mean(grad, axis=-1, keepdims=True)
    along = jnp.mean(grad * normed, axis=-1, keepdims=True)
    gtok_ref[...] = gmid_ref[...] + (grad - mean - normed * along) * inv

    def drain(quarter, carry):
        c_copy(quarter).wait_send()
        wait_send_unless(*r_copy(quarter))
        return carry

    lax.fori_loop(0, 4, drain, 0)


def call_plain_backward(tokens, pat, gain, gmid, do, q, k, v, everything, own, tab):
    local = tokens.shape[0]
    half = local // 2
    length = 4 * local
    sds = jax.ShapeDtypeStruct
    return pl.pallas_call(
        plain_backward_kernel,
        out_shape=(
            sds((local, D), F32),
            sds((8, 96, WCOLS), BF16),
            sds((8, 2 * D), F32),
        ),
        in_specs=[vm()] * 11,
        out_specs=(vm(),) * 3,
        scratch_shapes=[
            VMEM((length, WCOLS), BF16),
            VMEM((64, length), F32),
            VMEM((64, length), F32),
            VMEM((D, WCOLS), F32),
            VMEM((4, half, D), F32),
            VMEM((4, half, D), BF16),
            VMEM((4, half, D), BF16),
            VMEM((4, half, D), BF16),
            VMEM((2, local, D), BF16),
            dma(4),
            dma(4),
            dma(4),
            dma(2, 2),
        ],
        compiler_params=params(2, 60),
        cost_estimate=pl.CostEstimate(flops=2 * 10**10, bytes_accessed=3 * 10**7, transcendentals=10**7),
    )(tokens, pat, gain, gmid, do, q, k, v, everything, own, tab)


def plain_sums(g, gq, own_ids):
    n, z, c = own_ids
    up = g[:, :, :192].reshape(8, 4, 2, 96, 384).transpose(0, 3, 1, 2, 4).reshape(D, FF)
    down = g[:, :, 192:384].reshape(8, D, 384).transpose(0, 2, 1).reshape(FF, D)
    out = g[:, :, 384:].reshape(8, 2, 2, 48, 384).transpose(0, 1, 3, 2, 4).reshape(D, D)
    flat = gq.reshape(D, WCOLS)
    pieces = []
    for starts in (Q_AT, KV_AT, [at + HEAD_DIM for at in KV_AT]):
        pieces.append(jnp.concatenate([flat[:, at : at + HEAD_DIM] for at in starts], axis=1))
    group = 2 * (n // 2) + c
    whole = jnp.zeros((D, 3, 4, OWN * HEAD_DIM), F32)
    for part in range(3):
        whole = lax.dynamic_update_slice(
            whole, pieces[part].astype(F32)[:, None, None, :], (0, part, group, 0)
        )
    whole = whole.reshape(D, 3 * D)

    def total(values):
        share = lax.psum_scatter(values.astype(F32), "wide", scatter_dimension=0, tiled=True)
        return lax.psum(share, "narrow")

    return total(whole), total(out), total(up), total(down)


def body(
    tokens,
    condition,
    docs_per_row,
    w_ada,
    b_ada,
    gain_one,
    w_qkv,
    w_out,
    gain_two,
    w_up,
    b_up,
    w_down,
    b_down,
    cotangent,
):
    local = tokens.shape[1]
    x = tokens.reshape(local, D)
    cot = cotangent.reshape(local, D)
    cond = condition.reshape(DOCS, -1)
    table = jnp.asarray(rotary_table(4 * local))

    def line(vector):
        return vector.reshape(1, -1)

    att, everything, q, k, v, pat, own, tab = call_forward(
        docs_per_row, x, cond, w_ada, line(b_ada), line(gain_one), w_qkv, table
    )
    if (lax.axis_size("narrow"), lax.axis_size("wide")) == (4, 8):
        output, gtok, blocks, qkv_a, qkv_b, packet, gcond = call_fused(
            docs_per_row, x, cot, att, cond, pat, line(gain_one), line(gain_two), line(b_up),
            line(b_down), w_ada, w_out, w_up, w_down, q, k, v, everything, own, tab,
        )
        output, gtok, gqkv, gout, gup, gdown, gada, gvec = call_finish(
            output, gtok, blocks, qkv_a, qkv_b, packet
        )
        return (
            output[None],
            gtok[None],
            gcond[None, :DOCS],
            gada,
            gvec[0],
            gvec[1, :96],
            gqkv,
            gout,
            gvec[2, :96],
            gup,
            gvec[3, :384],
            gdown,
            gvec[4, :96],
        )

    output, gmid, g, small_two, do = call_middle(
        x, cot, att, pat, line(gain_two), w_out, w_up, line(b_up), w_down, line(b_down)
    )
    gtok, gq, small_one = call_plain_backward(
        x, pat, line(gain_one), gmid, do, q, k, v, everything, own, tab
    )
    n, w = lax.axis_index("narrow"), lax.axis_index("wide")
    sum_qkv, sum_out, sum_up, sum_down = plain_sums(g, gq, (n, w // 2, w % 2))

    small = jnp.concatenate([small_one, small_two], axis=1).reshape(4, 2, -1).sum(0)
    small = lax.psum(small, "narrow")
    shift_one, raw_one, gate_one, shift_two, raw_two, gate_two = jnp.split(small[:, : 6 * D], 6, axis=1)
    scales = pat[:2].reshape(2, 6, D)
    sum_gain_one = jnp.sum(raw_one * (1.0 + scales[:, 1]), axis=0)
    sum_gain_two = jnp.sum(raw_two * (1.0 + scales[:, 4]), axis=0)
    grads = jnp.concatenate(
        [
            shift_one,
            raw_one * gain_one.astype(F32),
            gate_one,
            shift_two,
            raw_two * gain_two.astype(F32),
            gate_two,
        ],
        axis=1,
    )
    two = docs_per_row[0] == DOCS
    grad_mods = jnp.stack(
        [jnp.where(two, grads[0], grads[0] + grads[1]), jnp.where(two, grads[1], 0.0)]
    )
    high = lax.Precision.HIGHEST
    grad_condition = jnp.einsum("sm,cm->sc", grad_mods, w_ada.astype(F32), precision=high)[None]
    part_ada = jnp.einsum("sm,sc->mc", grad_mods, cond.astype(F32), precision=high)

    def share(values):
        return lax.psum_scatter(values, "wide", scatter_dimension=0, tiled=True)

    sum_b_up = jnp.sum(small[:, 6 * D : 6 * D + FF], axis=0)
    sum_b_down = jnp.sum(small[:, 6 * D + FF :], axis=0)
    return (
        output[None],
        gtok[None],
        grad_condition,
        share(part_ada).T,
        share(jnp.sum(grad_mods, axis=0)),
        share(sum_gain_one),
        sum_qkv,
        sum_out,
        share(sum_gain_two),
        sum_up,
        share(sum_b_up),
        sum_down,
        share(sum_b_down),
    )


def solution(mesh):
    in_specs = (
        P("wide", "narrow", None),
        P("wide", None, None),
        P("wide"),
        P(),
        P(),
        P(),
        P(),
        P(),
        P(),
        P(),
        P(),
        P(),
        P(),
        P("wide", "narrow", None),
    )
    out_specs = (
        P("wide", "narrow", None),
        P("wide", "narrow", None),
        P("wide", None, None),
        P(None, "wide"),
        P("wide"),
        P("wide"),
        P("wide", None),
        P("wide", None),
        P("wide"),
        P("wide", None),
        P("wide"),
        P("wide", None),
        P("wide"),
    )
    return jax.shard_map(body, mesh=mesh, in_specs=in_specs, out_specs=out_specs, check_vma=False)
```

```python
import functools

import jax
import jax.numpy as jnp
import numpy as np
from jax import lax
from jax.experimental import pallas as pl
from jax.experimental.pallas import tpu as pltpu
from jax.sharding import PartitionSpec as P

D = 768
HEADS = 12
HEAD_DIM = 64
FF = 3072
DOCS = 2
EPS = 1e-05
LOG2E = 1.4426950408889634
BIG = 1e30
OWN = 3
WCOLS = 640
KV_AT = (0, 128, 384)
Q_AT = (256, 320, 512)
ROWS_G = 432
COLS_G = 384
MESH = pl.DeviceIdType.MESH
F32 = jnp.float32
BF16 = jnp.bfloat16
NN = (((1,), (0,)), ((), ()))
NT = (((1,), (1,)), ((), ()))
TN = (((0,), (0,)), ((), ()))
VMEM = pltpu.VMEM
ANY = pl.ANY


def dg(a, b, dims):
    return lax.dot_general(a, b, dims, preferred_element_type=F32)


def place():
    n = lax.axis_index("narrow")
    w = lax.axis_index("wide")
    return n, n // 2, lax.rem(n, 2), w // 2, lax.rem(w, 2)


def sibling(n, z, c):
    return (n, 2 * z + 1 - c)


def plane_barrier(n, z, c):
    barrier = pltpu.get_barrier_semaphore()
    me = n * 2 + c
    for step in range(1, 8):
        other = lax.rem(me + step, 8)
        pl.semaphore_signal(
            barrier, inc=1, device_id=(other // 2, 2 * z + lax.rem(other, 2)), device_id_type=MESH
        )
    pl.semaphore_wait(barrier, 7)


def remote(src, dst, send, recv, device):
    return pltpu.make_async_remote_copy(
        src_ref=src, dst_ref=dst, send_sem=send, recv_sem=recv, device_id=device, device_id_type=MESH
    )


def send_or_keep(is_self, src, dst, send, recv, device):
    @pl.when(is_self)
    def _():
        pltpu.make_async_copy(src, dst, recv).start()

    @pl.when(jnp.logical_not(is_self))
    def _():
        remote(src, dst, send, recv, device).start()


def wait_send_unless(is_self, src, dst, send, recv, device):
    @pl.when(jnp.logical_not(is_self))
    def _():
        remote(src, dst, send, recv, device).wait_send()


def wait_bytes(ref, sem):
    pltpu.make_async_copy(ref, ref, sem).wait()


def row_of(ref):
    return ref[...].astype(F32).reshape(1, ref.shape[0])


def lane(shape):
    return lax.broadcasted_iota(jnp.int32, shape, len(shape) - 1)


def by8(values):
    return values.reshape(values.shape[0] // 8, 8, values.shape[1])


def flat8(values):
    return values.reshape(values.shape[0] * 8, values.shape[2])


def sum8(values):
    return jnp.sum(by8(values), axis=0)


def norm_stats(values):
    mean = jnp.mean(values, axis=-1, keepdims=True)
    centred = values - mean
    spread = jnp.mean(centred * centred, axis=-1, keepdims=True)
    inv = lax.rsqrt(spread + EPS)
    return centred * inv, inv


def halves_turn(values):
    where = lax.rem(lane(values.shape), 64) < 32
    return jnp.where(where, pltpu.roll(values, 96, 1), pltpu.roll(values, 32, 1))


def cos_sin(table):
    lanes = lane(table.shape)
    other = pltpu.roll(table, 64, 1)
    cosine = jnp.where(lanes < 64, table, other)
    sine = jnp.where(lanes < 64, other, table)
    return cosine, jnp.where(lax.rem(lanes, 64) < 32, -sine, sine)


def split3(column):
    high = column.astype(BF16).astype(F32)
    rest = column - high
    middle = rest.astype(BF16).astype(F32)
    low = (rest - middle).astype(BF16).astype(F32)
    return high, middle, low


def forward_kernel(
    docs_ref,
    tokens_ref,
    cond_ref,
    w_ada_ref,
    b_ada_ref,
    gain_ref,
    w_qkv_hbm,
    table_hbm,
    att_ref,
    all_ref,
    q_ref,
    k_ref,
    v_ref,
    pat_ref,
    own_ref,
    tab_ref,
    mine,
    gathered,
    w_qkv,
    tables,
    osend,
    oland,
    docs_mine,
    docs_other,
    load_sem,
    docs_sem,
    a_send,
    a_recv,
    f_send,
    f_recv,
    o_send,
    o_recv,
    all_sem,
):
    n, ny, nx, z, c = place()
    local = tokens_ref.shape[0]
    half = local // 2
    length = local * 4
    loads = [
        pltpu.make_async_copy(w_qkv_hbm, w_qkv, load_sem.at[0]),
        pltpu.make_async_copy(table_hbm, tables, load_sem.at[1]),
    ]
    for load in loads:
        load.start()
    docs_mine[...] = jnp.full(docs_mine.shape, docs_ref[0], jnp.int32).astype(F32)
    plane_barrier(n, z, c)
    docs_copy = remote(docs_mine, docs_other, docs_sem.at[0], docs_sem.at[1], sibling(n, z, c))
    docs_copy.start()

    two = docs_ref[0] == DOCS
    parity = lax.rem(lax.broadcasted_iota(jnp.int32, (16, 128), 0), 2)
    odd = jnp.logical_and(parity == 1, two)
    cond = cond_ref[...].astype(F32)
    cond16 = jnp.where(odd, cond[1:2, :], cond[0:1, :]).astype(BF16)
    pat_ref[...] = dg(cond16, w_ada_ref[...], NN)[:8] + row_of(b_ada_ref)

    shift = pat_ref[:, 0:D]
    amp = row_of(gain_ref) * (1.0 + pat_ref[:, D : 2 * D])

    def a_copy(my, hh):
        target = 2 * my + c
        is_self = jnp.logical_and(target == n, c == hh)
        return (
            is_self,
            mine.at[pl.ds(hh * half, half)],
            gathered.at[pl.ds(pl.multiple_of(n * local + hh * half, half), half)],
            a_send.at[my * 2 + hh],
            a_recv.at[n],
            (target, 2 * z + hh),
        )

    for hh in range(2):
        normed, _ = norm_stats(tokens_ref[hh * half : (hh + 1) * half, :].astype(F32))
        mine[hh * half : (hh + 1) * half, :] = flat8(by8(normed) * amp[None] + shift[None]).astype(
            BF16
        )
        for my in range(2):
            send_or_keep(*a_copy(my, hh))

    for load in loads:
        load.wait()
    group = 2 * ny + c
    lanes_w = lane((D, 128))

    def columns(part, j, at):
        col = part * HEADS + group * OWN + j
        block = w_qkv[:, pl.ds(pl.multiple_of((col // 2) * 128, 128), 128)].astype(F32)
        return pltpu.roll(block, lax.rem(col + at, 2) * 64, 1)

    for j in range(OWN):
        own_ref[:, KV_AT[j] : KV_AT[j] + 128] = jnp.where(
            lanes_w < 64, columns(1, j, 0), columns(2, j, 1)
        ).astype(BF16)
    own_ref[:, 256:384] = jnp.where(lanes_w < 64, columns(0, 0, 0), columns(0, 1, 1)).astype(BF16)
    own_ref[:, 512:640] = jnp.where(lanes_w < 64, columns(0, 2, 0), 0.0).astype(BF16)

    docs_copy.wait()
    docs_heads = jnp.where(nx == c, docs_mine[...], docs_other[...])
    tab_ref[...] = jnp.where(docs_heads[0:1] == DOCS, tables[1], tables[0])

    lanes = lane((8, 128))
    odd8 = jnp.logical_and(parity[:8] == 1, docs_heads == DOCS)
    tail_q = jnp.where(lanes == 64, jnp.where(odd8, 0.0, 1.0), 0.0)
    tail_q = jnp.where(lanes == 65, jnp.where(odd8, 1.0, 0.0), tail_q)
    tail_k = jnp.where(lanes == 64, jnp.where(odd8, -BIG, 0.0), 0.0)
    tail_k = jnp.where(lanes == 65, jnp.where(odd8, 0.0, -BIG), tail_k)
    tail_k = jnp.where(jnp.logical_and(lanes >= 66, lanes < 69), 1.0, tail_k)

    def with_tail(values, tail):
        shaped = by8(values)
        return flat8(jnp.where(lane(shaped.shape) < 64, shaped, tail[None])).astype(BF16)

    def project(source):
        def step(i, carry):
            rows = pl.ds(pl.multiple_of(source * local + i * half, half), half)
            wide = dg(gathered[rows, :], own_ref[...], NN)
            cosine, sine = cos_sin(tab_ref[rows, :])

            def rot(values):
                return values * cosine + halves_turn(values) * sine

            for j in range(OWN):
                block = wide[:, KV_AT[j] : KV_AT[j] + 128]
                k_ref[j, rows, :] = with_tail(rot(block), tail_k)
                v_ref[j, rows, :] = jnp.where(
                    lane(block.shape) < 64, pltpu.roll(block, 64, 1), 1.0
                ).astype(BF16)
            first = rot(wide[:, 256:384]) * HEAD_DIM**-0.5
            q_ref[0, rows, :] = with_tail(first, tail_q)
            q_ref[1, rows, :] = with_tail(pltpu.roll(first, 64, 1), tail_q)
            q_ref[2, rows, :] = with_tail(rot(wide[:, 512:640]) * HEAD_DIM**-0.5, tail_q)
            return carry

        lax.fori_loop(0, 2, step, 0)

    def part(source, hh):
        return gathered.at[pl.ds(pl.multiple_of(source * local + hh * half, half), half)]

    def forward(source):
        wait_bytes(part(source, c), a_recv.at[source])
        remote(
            part(source, c), part(source, c), f_send.at[source], f_recv.at[source], sibling(n, z, c)
        ).start()

    sources = [n, lax.rem(n + 2, 4), n + 1 - 2 * nx, lax.rem(n + 3 - 2 * nx, 4)]

    def arrive(source):
        wait_bytes(part(source, 1 - c), f_recv.at[source])
        project(source)

    forward(sources[0])
    forward(sources[1])
    arrive(sources[0])
    forward(sources[2])
    arrive(sources[1])
    forward(sources[3])
    arrive(sources[2])
    arrive(sources[3])
    keep = pltpu.make_async_copy(gathered, all_ref, all_sem)
    keep.start()

    def o_copy(j, quarter):
        is_self = jnp.logical_and(quarter == n, nx == c)
        return (
            is_self,
            osend.at[j, quarter],
            oland.at[group * OWN + j],
            o_send.at[j, quarter],
            o_recv.at[group * OWN + j],
            (quarter, 2 * z + nx),
        )

    def attend(index, carry):
        j = index // 4
        quarter = lax.rem(n + 3 - lax.rem(index, 4), 4)
        start = quarter * local
        scores = []
        for u in range(2):
            rows = pl.ds(pl.multiple_of(start + u * half, half), half)
            scores.append(dg(q_ref[j, rows, :], k_ref[j], NT))
        outs = []
        for u in range(2):
            rows = pl.ds(pl.multiple_of(start + u * half, half), half)
            top = jnp.max(scores[u], axis=1, keepdims=True)
            weights = jnp.exp2((scores[u] - top) * LOG2E)
            total = jnp.sum(weights, axis=1, keepdims=True)
            mixed = dg((weights * (1.0 / total)).astype(BF16), v_ref[j], NN)
            high, middle, low = split3(top + jnp.log(total))
            query = q_ref[j, rows, :].astype(F32)
            lanes_q = lane(query.shape)
            query = jnp.where(lanes_q == 66, -high, query)
            query = jnp.where(lanes_q == 67, -middle, query)
            q_ref[j, rows, :] = jnp.where(lanes_q == 68, -low, query).astype(BF16)
            outs.append(mixed)
        osend[j, quarter] = jnp.where(
            lane(outs[0].shape) < 64, outs[0], pltpu.roll(outs[1], 64, 1)
        ).astype(BF16)
        send_or_keep(*o_copy(j, quarter))
        return carry

    lax.fori_loop(0, OWN * 4, attend, 0)

    for head in range(HEADS):
        wait_bytes(oland.at[head], o_recv.at[head])
    for pair in range(HEADS // 2):
        even = oland[2 * pair].astype(F32)
        odd_head = oland[2 * pair + 1].astype(F32)
        low = lane(even.shape) < 64
        cols = slice(pair * 128, (pair + 1) * 128)
        att_ref[0:half, cols] = jnp.where(low, even, pltpu.roll(odd_head, 64, 1)).astype(BF16)
        att_ref[half:local, cols] = jnp.where(low, pltpu.roll(even, 64, 1), odd_head).astype(BF16)

    for hh in range(2):
        for my in range(2):
            wait_send_unless(*a_copy(my, hh))
    for source in range(4):
        remote(
            part(source, c), part(source, c), f_send.at[source], f_recv.at[source], sibling(n, z, c)
        ).wait_send()

    def drain(index, carry):
        wait_send_unless(*o_copy(index // 4, lax.rem(index, 4)))
        return carry

    lax.fori_loop(0, OWN * 4, drain, 0)
    keep.wait()


def vm():
    return pl.BlockSpec(memory_space=VMEM)


def hbm():
    return pl.BlockSpec(memory_space=ANY)


def smem():
    return pl.BlockSpec(memory_space=pltpu.SMEM)


def params(collective_id, limit=56):
    return pltpu.CompilerParams(
        collective_id=collective_id, has_side_effects=True, vmem_limit_bytes=limit * 2**20
    )


def dma(*shape):
    return pltpu.SemaphoreType.DMA(shape)


def call_forward(docs, tokens, cond, w_ada, b_ada, gain, w_qkv, table):
    local = tokens.shape[0]
    length = 4 * local
    half = local // 2
    sds = jax.ShapeDtypeStruct
    return pl.pallas_call(
        forward_kernel,
        out_shape=(
            sds((local, D), BF16),
            sds((length, D), BF16),
            sds((OWN, length, 128), BF16),
            sds((OWN, length, 128), BF16),
            sds((OWN, length, 128), BF16),
            sds((8, 6 * D), F32),
            sds((D, WCOLS), BF16),
            sds((length, 128), F32),
        ),
        in_specs=[smem(), vm(), vm(), vm(), vm(), vm(), hbm(), hbm()],
        out_specs=(vm(), hbm(), vm(), vm(), vm(), vm(), vm(), vm()),
        scratch_shapes=[
            VMEM((local, D), BF16),
            VMEM((length, D), BF16),
            VMEM((D, 3 * D), BF16),
            VMEM((2, length, 128), F32),
            VMEM((OWN, 4, half, 128), BF16),
            VMEM((HEADS, half, 128), BF16),
            VMEM((8, 128), F32),
            VMEM((8, 128), F32),
            dma(2),
            dma(2),
            dma(4),
            dma(4),
            dma(4),
            dma(4),
            dma(OWN, 4),
            dma(HEADS),
            pltpu.SemaphoreType.DMA,
        ],
        compiler_params=params(0),
        cost_estimate=pl.CostEstimate(flops=10**10, bytes_accessed=2 * 10**7, transcendentals=10**7),
    )(docs, tokens, cond, w_ada, b_ada, gain, w_qkv, table)


def rotary_table(length):
    freq = 10000.0 ** (-np.arange(HEAD_DIM // 2, dtype=np.float64) * 2.0 / HEAD_DIM)
    tables = []
    for docs in (1, DOCS):
        angle = (np.arange(length) // docs)[:, None] * freq[None, :]
        cosine, sine = np.cos(angle), np.sin(angle)
        tables.append(np.concatenate([cosine, cosine, sine, sine], axis=1))
    return np.stack(tables).astype(np.float32)


SMALL = 4 * D + FF + D


def middle_kernel(
    tokens_ref,
    cot_ref,
    att_ref,
    pat_ref,
    gain_ref,
    w_out_ref,
    w_up_ref,
    b_up_ref,
    w_down_ref,
    b_down_ref,
    out_ref,
    gmid_ref,
    g_ref,
    small_ref,
    do_ref,
    second_ref,
    active_ref,
    slope_ref,
    down_ref,
    gsecond_ref,
    middle_ref,
    branch_ref,
    lhs_t,
    gdown_ref,
    dsend,
    dland,
    d_send,
    d_recv,
):
    n, ny, nx, z, c = place()
    group = 2 * ny + c
    local = tokens_ref.shape[0]
    half = local // 2
    tile = 768
    plane_barrier(n, z, c)

    def piece(index):
        return pat_ref[:, index * D : (index + 1) * D]

    def spread(values, pattern):
        return flat8(by8(values) * pattern[None])

    branch_ref[...] = dg(att_ref[...], w_out_ref[...], NN)
    middle = tokens_ref[...].astype(F32) + spread(branch_ref[...], piece(2))
    middle_ref[...] = middle
    amp = row_of(gain_ref) * (1.0 + piece(4))
    normed, _ = norm_stats(middle)
    second = flat8(by8(normed) * amp[None] + piece(3)[None]).astype(BF16)
    second_ref[...] = second
    down_ref[...] = jnp.broadcast_to(row_of(b_down_ref), down_ref.shape)

    def up(t, carry):
        cols = pl.ds(pl.multiple_of(t * tile, tile), tile)
        hidden = dg(second_ref[...], w_up_ref[:, cols], NN) + b_up_ref[cols].astype(F32).reshape(1, tile)
        square = hidden * hidden
        bend = jnp.tanh(0.7978845608028654 * hidden * (1.0 + 0.044715 * square))
        part = 0.5 * (1.0 + bend)
        active_ref[:, cols] = (hidden * part).astype(BF16)
        slope_ref[:, cols] = part + (0.5 * 0.7978845608028654) * hidden * (1.0 - bend * bend) * (
            1.0 + 3.0 * 0.044715 * square
        )
        down_ref[...] += dg(active_ref[:, cols], w_down_ref[cols, :], NN)
        return carry

    lax.fori_loop(0, FF // tile, up, 0)

    cot = cot_ref[...].astype(F32)
    down = down_ref[...]
    out_ref[...] = (middle_ref[...] + spread(down, piece(5))).astype(BF16)
    small_ref[:, 3 * D : 4 * D] = sum8(cot * down)
    gdown = spread(cot, piece(5)).astype(BF16)
    gdown_ref[...] = gdown
    small_ref[:, 4 * D + FF :] = sum8(gdown.astype(F32))
    lhs_t[0] = second_ref[...].T
    lhs_t[1] = gdown.T
    gsecond_ref[...] = jnp.zeros_like(gsecond_ref)

    def back(t, carry):
        cols = pl.ds(pl.multiple_of(t * tile, tile), tile)
        ghidden = dg(gdown_ref[...], w_down_ref[cols, :], NT) * slope_ref[:, cols]
        low = ghidden.astype(BF16)
        small_ref[:, pl.ds(pl.multiple_of(4 * D + t * tile, tile), tile)] = sum8(low.astype(F32))
        gsecond_ref[...] += dg(low, w_up_ref[:, cols], NT)
        gup = dg(lhs_t[0], low, NN).astype(BF16)
        for hh in range(2):
            g_ref[:, t, hh * 96 : (hh + 1) * 96, :] = gup[:, hh * 384 : (hh + 1) * 384].reshape(
                8, 96, 384
            )
        gdw = dg(lhs_t[1], active_ref[:, cols], NN).astype(BF16)
        for hh in range(2):
            g_ref[2 * t + hh, :, 192:384, :] = gdw[:, hh * 384 : (hh + 1) * 384].reshape(4, 192, 384)
        return carry

    lax.fori_loop(0, FF // tile, back, 0)

    normed, inv = norm_stats(middle_ref[...])
    gsecond = gsecond_ref[...]
    small_ref[:, D : 2 * D] = sum8(gsecond)
    small_ref[:, 2 * D : 3 * D] = sum8(gsecond * normed)
    amp = row_of(gain_ref) * (1.0 + piece(4))
    grad = spread(gsecond, amp)
    mean = jnp.mean(grad, axis=-1, keepdims=True)
    along = jnp.mean(grad * normed, axis=-1, keepdims=True)
    gmid = cot_ref[...].astype(F32) + (grad - mean - normed * along) * inv
    gmid_ref[...] = gmid
    small_ref[:, 0:D] = sum8(gmid * branch_ref[...])
    gbranch = spread(gmid, piece(2)).astype(BF16)
    gatt = dg(gbranch, w_out_ref[...], NT)

    def d_copy(quarter_x, pick_y, cc, j):
        target = 2 * pick_y + c
        head = (2 * pick_y + cc) * OWN + j
        is_self = jnp.logical_and(target == n, c == cc)
        return (
            is_self,
            dsend.at[head],
            dland.at[j, n],
            d_send.at[head],
            d_recv.at[j, n],
            (target, 2 * z + cc),
        )

    copies = []
    for pair in range(HEADS // 2):
        top = gatt[0:half, pair * 128 : (pair + 1) * 128]
        bottom = gatt[half:local, pair * 128 : (pair + 1) * 128]
        low = lane(top.shape) < 64
        dsend[2 * pair] = jnp.where(low, top, pltpu.roll(bottom, 64, 1)).astype(BF16)
        dsend[2 * pair + 1] = jnp.where(low, pltpu.roll(top, 64, 1), bottom).astype(BF16)
    for head in range(HEADS):
        copies.append(d_copy(None, head // OWN // 2, (head // OWN) % 2, head % OWN))
        send_or_keep(*copies[-1])

    for hh in range(2):
        gout = dg(att_ref[...], gbranch[:, hh * 384 : (hh + 1) * 384], TN).astype(BF16)
        shaped = gout.reshape(8, 2, 48, 384)
        for rh in range(2):
            g_ref[:, rh * 2 + hh, 384:432, :] = shaped[:, rh]

    for j in range(OWN):
        for quarter in range(4):
            wait_bytes(dland.at[j, quarter], d_recv.at[j, quarter])
    do_ref[...] = dland[...]
    for copy in copies:
        wait_send_unless(*copy)


def call_middle(tokens, cot, att, pat, gain, w_out, w_up, b_up, w_down, b_down):
    local = tokens.shape[0]
    half = local // 2
    sds = jax.ShapeDtypeStruct
    return pl.pallas_call(
        middle_kernel,
        out_shape=(
            sds((local, D), BF16),
            sds((local, D), F32),
            sds((8, 4, ROWS_G, COLS_G), BF16),
            sds((8, SMALL), F32),
            sds((OWN, 4, half, 128), BF16),
        ),
        in_specs=[vm()] * 10,
        out_specs=(vm(),) * 5,
        scratch_shapes=[
            VMEM((local, D), BF16),
            VMEM((local, FF), BF16),
            VMEM((local, FF), F32),
            VMEM((local, D), F32),
            VMEM((local, D), F32),
            VMEM((local, D), F32),
            VMEM((local, D), F32),
            VMEM((2, D, local), BF16),
            VMEM((local, D), BF16),
            VMEM((HEADS, half, 128), BF16),
            VMEM((OWN, 4, half, 128), BF16),
            dma(HEADS),
            dma(OWN, 4),
        ],
        compiler_params=params(1, 60),
        cost_estimate=pl.CostEstimate(flops=2 * 10**10, bytes_accessed=3 * 10**7, transcendentals=10**7),
    )(tokens, cot, att, pat, gain, w_out, w_up, b_up, w_down, b_down)


CUT = 320
CHUNK = 24
PARTS_Q = ((0, 384), (384, 256))


def slot_of(other, me):
    return lax.rem(other - me + 3, 4)


def fused_kernel(
    docs_ref,
    tokens_ref,
    cot_ref,
    att_ref,
    cond_ref,
    pat_ref,
    gain_one_ref,
    gain_ref,
    b_up_ref,
    b_down_ref,
    w_ada_hbm,
    w_out_hbm,
    w_up_hbm,
    w_down_hbm,
    q_hbm,
    k_hbm,
    v_hbm,
    all_hbm,
    own_hbm,
    tab_hbm,
    out_ref,
    gtok_ref,
    blocks_ref,
    qkv_a_ref,
    qkv_b_ref,
    packet_ref,
    gcond_ref,
    small_ref,
    small_one,
    dsend,
    dland,
    g_own,
    g_land,
    land_x1,
    land_y1,
    land_x2,
    land_y2,
    land_b1,
    land_a2,
    land_b2,
    block,
    land_block,
    cland,
    rland,
    gq_a,
    gq_b,
    land_qx_a,
    land_qx_b,
    land_qz_a,
    land_qz_b,
    land_q_a,
    land_q_b,
    pack,
    land_s1,
    pack_sum,
    land_s2,
    gc_mine,
    land_gc,
    load_sem,
    d_send,
    d_recv,
    g_send,
    g_recv,
    one_sem,
    two_sem,
    b1_send,
    b1_recv,
    a2_send,
    a2_recv,
    b2_send,
    b2_recv,
    ag_send,
    ag_recv,
    c_send,
    c_recv,
    r_send,
    r_recv,
    qx_sem,
    qz_send,
    qz_recv,
    qp_send,
    qp_recv,
    s1_send,
    s1_recv,
    s2_send,
    s2_recv,
    gc_send,
    gc_recv,
):
    n, ny, nx, z, c = place()
    w = 2 * z + c
    local = tokens_ref.shape[0]
    half = local // 2
    length = local * 4
    group = 2 * ny + c
    tile = 768
    across = n + 1 - 2 * nx
    along_y = lax.rem(n + 2, 4)

    barrier = pltpu.get_barrier_semaphore()

    def greet(device):
        pl.semaphore_signal(barrier, inc=1, device_id=device, device_id_type=MESH)

    me = n * 2 + c
    for step in range(1, 8):
        other = lax.rem(me + step, 8)
        greet((other // 2, 2 * z + lax.rem(other, 2)))
    for step in range(1, 4):
        greet((n, 2 * lax.rem(z + step, 4) + c))
    for row in range(8):

        @pl.when(jnp.logical_not(jnp.logical_and(z == n, row == w)))
        def _():
            greet((z, row))

    def others(base):
        return [lax.rem(base + step, 4) for step in (1, 2, 3)]

    def piece(index):
        return pat_ref[:, index * D : (index + 1) * D]

    def spread(values, pattern):
        return flat8(by8(values) * pattern[None])


    def core_up(g_give, t):
        return remote(
            g_give.at[:, t // 2, t % 2, pl.ds(0, 192)],
            g_land.at[:, t // 2, t % 2, pl.ds(0, 192)],
            g_send.at[t],
            g_recv.at[t],
            sibling(n, z, c),
        )

    def core_down(g_give, t):
        return remote(
            g_give.at[t, :, :, pl.ds(192, 192)],
            g_land.at[t, :, :, pl.ds(192, 192)],
            g_send.at[4 + t],
            g_recv.at[4 + t],
            sibling(n, z, c),
        )

    def core_out(g_give):
        return remote(
            g_give.at[:, :, :, pl.ds(384, 48)],
            g_land.at[:, :, :, pl.ds(384, 48)],
            g_send.at[8],
            g_recv.at[8],
            sibling(n, z, c),
        )

    def d_copy(head):
        pick_y, cc, j = head // OWN // 2, head // OWN % 2, head % OWN
        target = 2 * pick_y + c
        is_self = jnp.logical_and(target == n, c == cc)
        return (
            is_self,
            dsend.at[head],
            dland.at[j, n],
            d_send.at[head],
            d_recv.at[j, n],
            (target, 2 * z + cc),
        )


    def middle(
        w_out, w_up, w_down, active, slope, acc, branch_ref, lhs_t, low_ref, g_give
    ):
        loads = [
            pltpu.make_async_copy(src, dst, load_sem.at[i])
            for i, (src, dst) in enumerate(((w_out_hbm, w_out), (w_up_hbm, w_up), (w_down_hbm, w_down)))
        ]
        for load in loads:
            load.start()
        loads[0].wait()
        branch_ref[...] = dg(att_ref[...], w_out[...], NN)

        def middle_values():
            return tokens_ref[...].astype(F32) + spread(branch_ref[...], piece(2))

        normed, _ = norm_stats(middle_values())
        amp = row_of(gain_ref) * (1.0 + piece(4))
        low_ref[...] = flat8(by8(normed) * amp[None] + piece(3)[None]).astype(BF16)
        acc[...] = jnp.broadcast_to(row_of(b_down_ref), acc.shape)
        loads[1].wait()
        loads[2].wait()

        def up(t, carry):
            cols = pl.ds(pl.multiple_of(t * tile, tile), tile)
            hidden = dg(low_ref[...], w_up[:, cols], NN) + b_up_ref[cols].astype(F32).reshape(1, tile)
            square = hidden * hidden
            bend = jnp.tanh(0.7978845608028654 * hidden * (1.0 + 0.044715 * square))
            part = 0.5 * (1.0 + bend)
            active[:, cols] = (hidden * part).astype(BF16)
            slope[:, cols] = part + (0.5 * 0.7978845608028654) * hidden * (1.0 - bend * bend) * (
                1.0 + 3.0 * 0.044715 * square
            )
            acc[...] += dg(active[:, cols], w_down[cols, :], NN)
            return carry

        lax.fori_loop(0, FF // tile, up, 0)

        cot = cot_ref[...].astype(F32)
        down = acc[...]
        out_ref[...] = (middle_values() + spread(down, piece(5))).astype(BF16)
        small_ref[:, 3 * D : 4 * D] = sum8(cot * down)
        lhs_t[0] = low_ref[...].T
        gdown = spread(cot, piece(5)).astype(BF16)
        low_ref[...] = gdown
        small_ref[:, 4 * D + FF :] = sum8(gdown.astype(F32))
        lhs_t[1] = gdown.T
        acc[...] = jnp.zeros_like(acc)
        pl.semaphore_wait(barrier, jnp.where(z == n, 17, 18))

        def back(t, carry):
            cols = pl.ds(pl.multiple_of(t * tile, tile), tile)
            ghidden = dg(low_ref[...], w_down[cols, :], NT) * slope[:, cols]
            low = ghidden.astype(BF16)
            small_ref[:, pl.ds(pl.multiple_of(4 * D + t * tile, tile), tile)] = sum8(low.astype(F32))
            acc[...] += dg(low, w_up[:, cols], NT)
            gup = dg(lhs_t[0], low, NN).astype(BF16).reshape(4, 2, 96, tile)
            mine = jnp.where(c == 0, gup[:, 0], gup[:, 1])
            other = jnp.where(c == 0, gup[:, 1], gup[:, 0])
            for hh in range(2):
                rows, lanes_h = slice(hh * 96, (hh + 1) * 96), slice(hh * 384, (hh + 1) * 384)
                g_own[:, t // 2, t % 2, rows, :] = mine[:, :, lanes_h]
                g_give[:, t // 2, t % 2, rows, :] = other[:, :, lanes_h]
            core_up(g_give, t).start()
            gdw = dg(lhs_t[1], active[:, cols], NN).astype(BF16)
            mine = jnp.where(c == 0, gdw[:, :384], gdw[:, 384:])
            other = jnp.where(c == 0, gdw[:, 384:], gdw[:, :384])
            g_own[t, :, :, 192:384, :] = mine.reshape(2, 2, 192, 384)
            g_give[t, :, :, 192:384, :] = other.reshape(2, 2, 192, 384)
            core_down(g_give, t).start()
            return carry

        lax.fori_loop(0, FF // tile, back, 0)

        normed, inv = norm_stats(middle_values())
        gsecond = acc[...]
        small_ref[:, D : 2 * D] = sum8(gsecond)
        small_ref[:, 2 * D : 3 * D] = sum8(gsecond * normed)
        grad = spread(gsecond, row_of(gain_ref) * (1.0 + piece(4)))
        mean = jnp.mean(grad, axis=-1, keepdims=True)
        along = jnp.mean(grad * normed, axis=-1, keepdims=True)
        gmid = cot_ref[...].astype(F32) + (grad - mean - normed * along) * inv
        gtok_ref[...] = gmid
        small_ref[:, 0:D] = sum8(gmid * branch_ref[...])
        gbranch = spread(gmid, piece(2)).astype(BF16)
        gatt = dg(gbranch, w_out[...], NT)
        for pair in range(HEADS // 2):
            top = gatt[0:half, pair * 128 : (pair + 1) * 128]
            bottom = gatt[half:local, pair * 128 : (pair + 1) * 128]
            lower = lane(top.shape) < 64
            dsend[2 * pair] = jnp.where(lower, top, pltpu.roll(bottom, 64, 1)).astype(BF16)
            dsend[2 * pair + 1] = jnp.where(lower, pltpu.roll(top, 64, 1), bottom).astype(BF16)
        for j in range(OWN):
            for g in range(4):
                send_or_keep(*d_copy(g * OWN + j))

        for hh in range(2):
            gout = dg(att_ref[...], gbranch[:, hh * 384 : (hh + 1) * 384], TN).astype(BF16)
            shaped = gout.reshape(4, 2, 2, 48, 384)
            g_own[:, :, hh, 384:432, :] = jnp.where(c == 0, shaped[:, 0], shaped[:, 1])
            g_give[:, :, hh, 384:432, :] = jnp.where(c == 0, shaped[:, 1], shaped[:, 0])
        core_out(g_give).start()
        for t in range(4):
            core_up(g_give, t).wait_send()
            core_down(g_give, t).wait_send()
        core_out(g_give).wait_send()

    pl.run_scoped(
        middle,
        VMEM((D, D), BF16),
        VMEM((D, FF), BF16),
        VMEM((FF, D), BF16),
        VMEM((local, FF), BF16),
        VMEM((local, FF), F32),
        VMEM((local, D), F32),
        VMEM((local, D), F32),
        VMEM((2, D, local), BF16),
        VMEM((local, D), BF16),
        VMEM((4, 2, 2, ROWS_G, COLS_G), BF16),
    )


    top = pl.ds(0, CUT)
    rest = pl.ds(CUT, ROWS_G - CUT)

    def one_x():
        return remote(g_own.at[pl.ds(0, 2), :, 1 - nx, top], land_x1, one_sem.at[0], one_sem.at[1], (across, w))

    def one_y():
        return remote(
            g_own.at[pl.ds(2, 2), 1 - ny, :, top], land_y1, one_sem.at[2], one_sem.at[3], (along_y, w)
        )

    def two_y():
        return remote(
            g_own.at[pl.ds(0, 2), 1 - ny, nx, top], land_y2, two_sem.at[0], two_sem.at[1], (along_y, w)
        )

    def two_x():
        return remote(
            g_own.at[pl.ds(2, 2), ny, 1 - nx, top], land_x2, two_sem.at[2], two_sem.at[3], (across, w)
        )

    def b1_copy(chip):
        slot = slot_of(chip, z)
        return remote(
            g_own.at[chip, :, :, rest], land_b1.at[slot], b1_send.at[slot], b1_recv.at[slot],
            (n, 2 * chip + c),
        )

    def a2_copy(chip):
        slot = slot_of(chip, z)
        return remote(
            g_own.at[chip, ny, nx, top], land_a2.at[slot], a2_send.at[slot], a2_recv.at[slot],
            (n, 2 * chip + c),
        )

    def b2_copy(other):
        slot = slot_of(other, n)
        return remote(
            g_own.at[z, other // 2, lax.rem(other, 2), rest], land_b2.at[slot], b2_send.at[slot],
            b2_recv.at[slot], (other, w),
        )

    def ag_copy(other):
        return remote(block, land_block.at[n], ag_send.at[slot_of(other, n)], ag_recv.at[n], (other, w))

    def core_finish():
        for t in range(4):
            wait_bytes(g_land.at[:, t // 2, t % 2, pl.ds(0, 192)], g_recv.at[t])
            wait_bytes(g_land.at[t, :, :, pl.ds(192, 192)], g_recv.at[4 + t])
        wait_bytes(g_land.at[:, :, :, pl.ds(384, 48)], g_recv.at[8])

        def add(i, carry):
            chip, y, x = i // 4, lax.rem(i // 2, 2), lax.rem(i, 2)
            g_own[chip, y, x] = (
                g_own[chip, y, x].astype(F32) + g_land[chip, y, x].astype(F32)
            ).astype(BF16)
            return carry

        lax.fori_loop(0, 16, add, 0)
        one_x().start()
        one_y().start()
        for chip in others(z):
            b1_copy(chip).start()

    def stage_two():
        one_x().wait_recv()
        one_y().wait_recv()
        for i in range(2):
            for k in range(2):
                g_own[i, k, nx, 0:CUT] = (
                    g_own[i, k, nx, 0:CUT].astype(F32) + land_x1[i, k].astype(F32)
                ).astype(BF16)
                g_own[2 + i, ny, k, 0:CUT] = (
                    g_own[2 + i, ny, k, 0:CUT].astype(F32) + land_y1[i, k].astype(F32)
                ).astype(BF16)
        two_y().start()
        two_x().start()

    def stage_a2():
        two_y().wait_recv()
        two_x().wait_recv()
        for i in range(2):
            g_own[i, ny, nx, 0:CUT] = (
                g_own[i, ny, nx, 0:CUT].astype(F32) + land_y2[i].astype(F32)
            ).astype(BF16)
            g_own[2 + i, ny, nx, 0:CUT] = (
                g_own[2 + i, ny, nx, 0:CUT].astype(F32) + land_x2[i].astype(F32)
            ).astype(BF16)
        for chip in others(z):
            a2_copy(chip).start()

    def stage_b2():
        for slot in range(3):
            wait_bytes(land_b1.at[slot], b1_recv.at[slot])
        for part in range(4):
            total = g_own[z, part // 2, part % 2, CUT:ROWS_G].astype(F32)
            for slot in range(3):
                total = total + land_b1[slot, part // 2, part % 2].astype(F32)
            g_own[z, part // 2, part % 2, CUT:ROWS_G] = total.astype(BF16)
        for other in others(n):
            b2_copy(other).start()

    def last():
        for slot in range(3):
            wait_bytes(land_a2.at[slot], a2_recv.at[slot])
            wait_bytes(land_b2.at[slot], b2_recv.at[slot])
        upper = g_own[z, ny, nx, 0:CUT].astype(F32)
        lower = g_own[z, ny, nx, CUT:ROWS_G].astype(F32)
        for slot in range(3):
            upper = upper + land_a2[slot].astype(F32)
            lower = lower + land_b2[slot].astype(F32)
        block[0:CUT] = upper.astype(BF16)
        block[CUT:ROWS_G] = lower.astype(BF16)
        for other in others(n):
            ag_copy(other).start()


    bufs_q = ((gq_a, land_qx_a, land_qz_a, land_q_a), (gq_b, land_qx_b, land_qz_b, land_q_b))

    def qx_copy(p):
        gq, land_x, _, _ = bufs_q[p]
        return remote(gq.at[:, 1 - nx], land_x, qx_sem.at[p, 0], qx_sem.at[p, 1], (across, w))

    def qz_copy(p, chip):
        gq, _, land_z, _ = bufs_q[p]
        slot = slot_of(chip, z)
        return remote(
            gq.at[chip, nx], land_z.at[slot], qz_send.at[p, slot], qz_recv.at[p, slot],
            (n, 2 * chip + c),
        )

    def qp_copy(p, other):
        gq, _, _, land = bufs_q[p]
        is_self = jnp.logical_and(other == n, nx == c)
        return (
            is_self, gq.at[z, nx], land.at[group], qp_send.at[p, other], qp_recv.at[p, group],
            (other, 2 * z + nx),
        )

    def q_z(p):
        gq, land_x, _, _ = bufs_q[p]
        qx_copy(p).wait_recv()
        for chip in range(4):
            gq[chip, nx] = (gq[chip, nx].astype(F32) + land_x[chip].astype(F32)).astype(BF16)
        for chip in others(z):
            qz_copy(p, chip).start()

    def q_plane(p):
        gq, _, land_z, _ = bufs_q[p]
        for slot in range(3):
            wait_bytes(land_z.at[slot], qz_recv.at[p, slot])
        total = gq[z, nx].astype(F32)
        for slot in range(3):
            total = total + land_z[slot].astype(F32)
        gq[z, nx] = total.astype(BF16)
        for other in range(4):
            send_or_keep(*qp_copy(p, other))


    def s1_copy(other):
        return remote(
            pack.at[pl.ds(2 * other, 2)], land_s1.at[n], s1_send.at[slot_of(other, n)],
            s1_recv.at[n], (other, w),
        )

    def gc_copy(other):
        return remote(
            gc_mine, land_gc.at[n], gc_send.at[slot_of(other, n)], gc_recv.at[n], (other, w)
        )

    def s2_copy(index):
        i, other = index // 4, lax.rem(index, 4)
        is_self = jnp.logical_and(other == n, w == 2 * n + i)
        return (
            is_self, pack_sum.at[i], land_s2.at[w], s2_send.at[index], s2_recv.at[w],
            (other, 2 * n + i),
        )

    def small_sums(w_ada_ref):

        two = docs_ref[0] == DOCS
        even_rows = lax.rem(lax.broadcasted_iota(jnp.int32, (8, D), 0), 2) == 0

        def even_odd(values):
            even = jnp.sum(jnp.where(even_rows, values, 0.0), axis=0, keepdims=True)
            return even, jnp.sum(jnp.where(even_rows, 0.0, values), axis=0, keepdims=True)

        pack[...] = jnp.zeros_like(pack)
        gc_mine[...] = jnp.zeros_like(gc_mine)

        def put(chunk, row, values, s):
            pack[chunk, row : row + 1, 0:96] = values[:, 96 * s : 96 * s + 96]

        raws = [
            small_one[:, 0:D],
            small_one[:, D : 2 * D],
            small_ref[:, 0:D],
            small_ref[:, D : 2 * D],
            small_ref[:, 2 * D : 3 * D],
            small_ref[:, 3 * D : 4 * D],
        ]
        gains = {1: gain_one_ref, 4: gain_ref}
        for piece in range(6):
            even, odd = even_odd(raws[piece])
            if piece in gains:
                scale = pat_ref[:, piece * D : (piece + 1) * D]
                gain_sum = even * (1.0 + scale[0:1]) + odd * (1.0 + scale[1:2])
                for s in range(8):
                    put(s, 12 if piece == 1 else 13, gain_sum, s)
                gain = row_of(gains[piece])
                even, odd = even * gain, odd * gain
            first_doc = jnp.where(two, even, even + odd)
            second_doc = jnp.where(two, odd, 0.0)
            for s in range(8):
                at = 8 * piece + s
                put(at // 6, at % 6, first_doc, s)
                put(at // 6, 6 + at % 6, second_doc, s)
            pieces = [*split3(first_doc), *split3(second_doc)]
            stacked = jnp.concatenate([*pieces, jnp.zeros((10, D), F32)], axis=0).astype(BF16)
            part = dg(stacked, w_ada_ref[:, piece * D : (piece + 1) * D], NT)
            gc_mine[0:1] += part[0:1] + part[1:2] + part[2:3]
            gc_mine[1:2] += part[3:4] + part[4:5] + part[5:6]
        for s in range(32):
            col = 4 * D + 96 * s
            row = jnp.sum(small_ref[:, col : col + 96], axis=0, keepdims=True)
            pack[s // 4, 14 + s % 4 : 15 + s % 4, 0:96] = row
        for s in range(8):
            col = 4 * D + FF + 96 * s
            pack[s, 18:19, 0:96] = jnp.sum(small_ref[:, col : col + 96], axis=0, keepdims=True)

        for other in others(n):
            s1_copy(other).start()
            gc_copy(other).start()
        last()
        land_gc[n] = gc_mine[...]
        land_s1[n] = pack[pl.ds(2 * n, 2)]
        for other in others(n):
            wait_bytes(land_s1.at[other], s1_recv.at[other])
        total = land_s1[0] + land_s1[1] + land_s1[2] + land_s1[3]
        pack_sum[...] = total
        cond = cond_ref[...].astype(F32)
        for i in range(2):
            pack_sum[i, 19:21, :] = cond

        for index in range(8):
            send_or_keep(*s2_copy(index))


    def heads(
        q_ref, k_ref, v_ref, all_ref, own_ref, tab_ref, w_ada_ref, packed, acc_k, acc_v, acc_w, kept, csend
    ):
        def c_copy(quarter):
            return remote(
                csend.at[quarter], cland.at[quarter], c_send.at[quarter], c_recv.at[quarter],
                sibling(n, z, c),
            )

        def r_copy(quarter):
            is_self = jnp.logical_and(quarter == n, nx == c)
            return (
                is_self,
                csend.at[quarter],
                rland.at[ny, pl.ds(pl.multiple_of(c * half, half), half)],
                r_send.at[quarter],
                r_recv.at[ny, c],
                (quarter, 2 * z + nx),
            )

        loads = [
            pltpu.make_async_copy(src, dst, load_sem.at[i])
            for i, (src, dst) in enumerate(
                (
                    (q_hbm, q_ref),
                    (k_hbm, k_ref),
                    (v_hbm, v_ref),
                    (tab_hbm, tab_ref),
                    (all_hbm, all_ref),
                    (own_hbm, own_ref),
                    (w_ada_hbm, w_ada_ref),
                )
            )
        ]
        for load in loads:
            load.start()
        core_finish()
        for load in loads[:4]:
            load.wait()
        lanes_h = lane((half, 128))
        lanes = lane((local, 128))

        def turned(values, rows):
            cosine, sine = cos_sin(tab_ref[rows, :])
            return values * cosine - halves_turn(values) * sine

        def rounded(values):
            return values.astype(BF16).astype(F32)

        def weights(p):
            gq = bufs_q[p][0]
            at, width = PARTS_Q[p]
            if p == 0:
                loads[4].wait()
            acc_w[:, 0:width] = dg(all_ref[0:local, :], packed[0:local, at : at + width], TN)

            def step(i, carry):
                rows = pl.ds(pl.multiple_of(i * local, local), local)
                acc_w[:, 0:width] += dg(all_ref[rows, :], packed[rows, at : at + width], TN)
                return carry

            lax.fori_loop(1, 4, step, 0)
            gq[...] = acc_w[:, 0:width].astype(BF16).reshape(gq.shape)
            qx_copy(p).start()

        hooks = {(1, 6): stage_two, (2, 4): stage_a2, (2, 5): stage_b2, (2, 7): lambda: q_z(0)}
        for j in range(OWN):
            for quarter in range(4):
                wait_bytes(dland.at[j, quarter], d_recv.at[j, quarter])
            acc_k[...] = jnp.zeros_like(acc_k)
            acc_v[...] = jnp.zeros_like(acc_v)

            def step(i, carry):
                for (at_j, at_i), hook in hooks.items():
                    if at_j == j:
                        pl.when(i == at_i)(hook)
                rows = pl.ds(pl.multiple_of(i * half, half), half)
                grad = pltpu.roll(dland[j, i // 2].astype(F32), lax.rem(i, 2) * 64, 1)
                grad = jnp.where(lanes_h < 64, grad, 0.0).astype(BF16)
                query = q_ref[j, rows, :]
                probs = jnp.exp2(dg(query, k_ref[j], NT) * LOG2E)
                gprobs = probs * dg(grad, v_ref[j], NT)
                scores = (gprobs - probs * jnp.sum(gprobs, axis=1, keepdims=True)).astype(BF16)
                probs = probs.astype(BF16)
                gquery = rounded(dg(scores, k_ref[j], NN) * HEAD_DIM**-0.5)
                packed[rows, Q_AT[j] : Q_AT[j] + 64] = turned(gquery, rows)[:, :64].astype(BF16)
                acc_v[...] += dg(grad.T[:64], probs, NN)
                acc_k[...] += dg(query.T[:64], scores, NN)
                return carry

            lax.fori_loop(0, 8, step, 0)

            def finish(i, carry):
                rows = pl.ds(pl.multiple_of(i * local, local), local)
                both = rounded(jnp.concatenate([acc_k[:, rows], acc_v[:, rows]], axis=0).T)
                packed[rows, KV_AT[j] : KV_AT[j] + 128] = jnp.where(
                    lanes < 64, turned(both, rows), both
                ).astype(BF16)
                return carry

            lax.fori_loop(0, 4, finish, 0)
            if j == 1:
                weights(0)
        packed[:, 576:640] = jnp.zeros((length, 64), BF16)

        def rows_of(quarter, hh):
            return pl.ds(pl.multiple_of(quarter * local + hh * half, half), half)

        def order(i):
            return lax.rem(n + 3 - i, 4)

        loads[5].wait()

        def give(i, carry):
            quarter = order(i)
            csend[quarter] = dg(packed[rows_of(quarter, 1 - c), :], own_ref[...], NT).astype(BF16)
            c_copy(quarter).start()
            return carry

        lax.fori_loop(0, 4, give, 0)

        def keep(i, carry):
            quarter = order(i)
            kept[quarter] = dg(packed[rows_of(quarter, c), :], own_ref[...], NT)
            return carry

        lax.fori_loop(0, 4, keep, 0)

        def add(i, carry):
            quarter = order(i)
            c_copy(quarter).wait()
            csend[quarter] = (kept[quarter] + cland[quarter].astype(F32)).astype(BF16)
            send_or_keep(*r_copy(quarter))
            return carry

        lax.fori_loop(0, 4, add, 0)
        weights(1)
        normed, inv = norm_stats(tokens_ref[...].astype(F32))
        q_plane(0)
        q_z(1)

        for y in range(2):
            for hh in range(2):
                wait_bytes(rland.at[y, pl.ds(hh * half, half)], r_recv.at[y, hh])
        gfirst = rland[0].astype(F32) + rland[1].astype(F32)
        small_one[:, 0:D] = sum8(gfirst)
        small_one[:, D : 2 * D] = sum8(gfirst * normed)
        grad = spread(gfirst, row_of(gain_one_ref) * (1.0 + piece(1)))
        mean = jnp.mean(grad, axis=-1, keepdims=True)
        along = jnp.mean(grad * normed, axis=-1, keepdims=True)
        gtok_ref[...] += (grad - mean - normed * along) * inv
        loads[6].wait()
        small_sums(w_ada_ref)

        q_plane(1)
        for quarter in range(4):
            wait_send_unless(*r_copy(quarter))

    pl.run_scoped(
        heads,
        VMEM((OWN, length, 128), BF16),
        VMEM((OWN, length, 128), BF16),
        VMEM((OWN, length, 128), BF16),
        VMEM((length, D), BF16),
        VMEM((D, WCOLS), BF16),
        VMEM((length, 128), F32),
        VMEM(w_ada_hbm.shape, BF16),
        VMEM((length, WCOLS), BF16),
        VMEM((64, length), F32),
        VMEM((64, length), F32),
        VMEM((D, 384), F32),
        VMEM((4, half, D), F32),
        VMEM((4, half, D), BF16),
    )

    for other in others(n):
        wait_bytes(land_gc.at[other], gc_recv.at[other])
    gcond_ref[...] = land_gc[0] + land_gc[1] + land_gc[2] + land_gc[3]
    for row in range(8):
        wait_bytes(land_s2.at[row], s2_recv.at[row])
    packet_ref[...] = land_s2[...]
    land_block[n] = block[...]
    for other in others(n):
        wait_bytes(land_block.at[other], ag_recv.at[other])
    move = pltpu.make_async_copy(land_block, blocks_ref, load_sem.at[0])
    move.start()
    for p in range(2):
        for g in range(4):
            wait_bytes(bufs_q[p][3].at[g], qp_recv.at[p, g])
    moves = [
        move,
        pltpu.make_async_copy(land_q_a, qkv_a_ref, load_sem.at[1]),
        pltpu.make_async_copy(land_q_b, qkv_b_ref, load_sem.at[2]),
    ]
    for later in moves[1:]:
        later.start()


    for later in moves:
        later.wait()
    for head in range(HEADS):
        wait_send_unless(*d_copy(head))
    for copy in (one_x(), one_y(), two_x(), two_y(), qx_copy(0), qx_copy(1)):
        copy.wait_send()

    def drain(quarter, carry):
        for p in range(2):
            wait_send_unless(*qp_copy(p, quarter))
        return carry

    lax.fori_loop(0, 4, drain, 0)
    for i in range(3):
        other, chip = others(n)[i], others(z)[i]
        b1_copy(chip).wait_send()
        a2_copy(chip).wait_send()
        b2_copy(other).wait_send()
        ag_copy(other).wait_send()
        qz_copy(0, chip).wait_send()
        qz_copy(1, chip).wait_send()
        s1_copy(other).wait_send()
        gc_copy(other).wait_send()
    for index in range(8):
        wait_send_unless(*s2_copy(index))


def call_fused(
    docs, tokens, cot, att, cond, pat, gain_one, gain_two, b_up, b_down, w_ada, w_out, w_up, w_down,
    q, k, v, everything, own, tab,
):
    local = tokens.shape[0]
    half = local // 2
    sds = jax.ShapeDtypeStruct
    rest = ROWS_G - CUT
    wide_a, wide_b = PARTS_Q[0][1], PARTS_Q[1][1]

    def low(*shape):
        return VMEM(shape, BF16)

    return pl.pallas_call(
        fused_kernel,
        out_shape=(
            sds((local, D), BF16),
            sds((local, D), F32),
            sds((4, ROWS_G, COLS_G), BF16),
            sds((4, 96, wide_a), BF16),
            sds((4, 96, wide_b), BF16),
            sds((8, CHUNK, 128), F32),
            sds((8, 128), F32),
        ),
        in_specs=[smem()] + [vm()] * 9 + [hbm()] * 10,
        out_specs=(vm(), vm(), hbm(), hbm(), hbm(), vm(), vm()),
        scratch_shapes=[
            VMEM((8, SMALL), F32),
            VMEM((8, 2 * D), F32),
            low(HEADS, half, 128),
            low(OWN, 4, half, 128),
            low(4, 2, 2, ROWS_G, COLS_G),
            low(4, 2, 2, ROWS_G, COLS_G),
            low(2, 2, CUT, COLS_G),
            low(2, 2, CUT, COLS_G),
            low(2, CUT, COLS_G),
            low(2, CUT, COLS_G),
            low(3, 2, 2, rest, COLS_G),
            low(3, CUT, COLS_G),
            low(3, rest, COLS_G),
            low(ROWS_G, COLS_G),
            low(4, ROWS_G, COLS_G),
            low(4, half, D),
            low(2, local, D),
            low(4, 2, 96, wide_a),
            low(4, 2, 96, wide_b),
            low(4, 96, wide_a),
            low(4, 96, wide_b),
            low(3, 96, wide_a),
            low(3, 96, wide_b),
            low(4, 96, wide_a),
            low(4, 96, wide_b),
            VMEM((8, CHUNK, 128), F32),
            VMEM((4, 2, CHUNK, 128), F32),
            VMEM((2, CHUNK, 128), F32),
            VMEM((8, CHUNK, 128), F32),
            VMEM((8, 128), F32),
            VMEM((4, 8, 128), F32),
            dma(7),
            dma(HEADS),
            dma(OWN, 4),
            dma(9),
            dma(9),
            dma(4),
            dma(4),
            dma(3),
            dma(3),
            dma(3),
            dma(3),
            dma(3),
            dma(3),
            dma(3),
            dma(4),
            dma(4),
            dma(4),
            dma(4),
            dma(2, 2),
            dma(2, 2),
            dma(2, 3),
            dma(2, 3),
            dma(2, 4),
            dma(2, 4),
            dma(3),
            dma(4),
            dma(8),
            dma(8),
            dma(3),
            dma(4),
        ],
        compiler_params=params(3, 63),
        cost_estimate=pl.CostEstimate(flops=4 * 10**10, bytes_accessed=5 * 10**7, transcendentals=10**7),
    )(
        docs, tokens, cot, att, cond, pat, gain_one, gain_two, b_up, b_down, w_ada, w_out, w_up, w_down,
        q, k, v, everything, own, tab,
    )


def finish_kernel(
    output_in, gtok_in, blocks, qkv_a, qkv_b, packet, gcond_in, output_out, gtok_out, gcond_out, gqkv, gout, gup, gdown, gada, gvec_ada,
    gvec_one, gvec_two, gvec_up, gvec_down, wide, pass_sem
):
    passed = [
        pltpu.make_async_copy(output_in, output_out, pass_sem.at[0]),
        pltpu.make_async_copy(gtok_in, gtok_out, pass_sem.at[1]),
    ]
    for copy in passed:
        copy.start()
    gcond_out[0] = gcond_in[0:DOCS]
    for part in range(4):
        for hh in range(2):
            at = part * 768 + hh * 384
            gup[:, at : at + 384] = blocks[part, hh * 96 : (hh + 1) * 96, :].astype(F32)
        rh, ch = part // 2, part % 2
        gout[rh * 48 : (rh + 1) * 48, ch * 384 : (ch + 1) * 384] = blocks[part, 384:432, :].astype(F32)
    for pair in range(2):
        both = jnp.concatenate(
            [blocks[2 * pair, 192:384, :], blocks[2 * pair + 1, 192:384, :]], axis=0
        ).astype(F32)
        gdown[:, pair * 384 : (pair + 1) * 384] = both.T

    def head_block(part, head):
        g, j = head // OWN, head % OWN
        if part == 0:
            at, upper = Q_AT[j] // 128 * 128, j % 2
        else:
            at, upper = KV_AT[j], part - 1
        qkv, start = (qkv_a, 0) if at < PARTS_Q[1][0] else (qkv_b, PARTS_Q[1][0])
        return qkv[g, :, at - start : at - start + 128].astype(F32), upper

    for part in range(3):
        for pair in range(HEADS // 2):
            even, up = head_block(part, 2 * pair)
            even = pltpu.roll(even, 64, 1) if up else even
            odd, up = head_block(part, 2 * pair + 1)
            odd = odd if up else pltpu.roll(odd, 64, 1)
            at = part * D + pair * 128
            gqkv[:, at : at + 128] = jnp.where(lane(even.shape) < 64, even, odd)

    conds = [packet[:, 19, :], packet[:, 20, :]]
    lhs = jnp.concatenate([conds[0]] * 3 + [conds[1]] * 3, axis=0).astype(BF16)
    for k in range(6):
        first, second = packet[:, k, :], packet[:, 6 + k, :]
        rhs = jnp.concatenate([*split3(first), *split3(second)], axis=0).astype(BF16)
        gada[96 * k : 96 * k + 96, :] = dg(rhs, lhs, TN)[:96]
        wide[0:1, 96 * k : 96 * k + 96] = jnp.sum(first + second, axis=0, keepdims=True)[:, :96]
    for row, at, k in ((1, 0, 12), (2, 0, 13), (3, 0, 14), (3, 1, 15), (3, 2, 16), (3, 3, 17), (4, 0, 18)):
        wide[row : row + 1, 96 * at : 96 * at + 96] = jnp.sum(packet[:, k, :], axis=0, keepdims=True)[
            :, :96
        ]
    for ref, row in ((gvec_ada, 0), (gvec_one, 1), (gvec_two, 2), (gvec_up, 3), (gvec_down, 4)):
        ref[...] = wide[row : row + 1, 0 : ref.shape[0]].reshape(ref.shape)
    for copy in passed:
        copy.wait()


def call_finish(output, gtok, blocks, qkv_a, qkv_b, packet, gcond):
    local = output.shape[0]
    sds = jax.ShapeDtypeStruct
    return pl.pallas_call(
        finish_kernel,
        out_shape=(
            sds((local, D), BF16),
            sds((local, D), F32),
            sds((1, DOCS, 128), F32),
            sds((96, 3 * D), F32),
            sds((96, D), F32),
            sds((96, FF), F32),
            sds((384, D), F32),
            sds((576, 128), F32),
            sds((576,), F32),
            sds((96,), F32),
            sds((96,), F32),
            sds((384,), F32),
            sds((96,), F32),
        ),
        in_specs=[vm()] * 7,
        out_specs=(hbm(), hbm()) + (vm(),) * 11,
        scratch_shapes=[VMEM((8, 576), F32), dma(2)],
        compiler_params=pltpu.CompilerParams(vmem_limit_bytes=62 * 2**20),
        cost_estimate=pl.CostEstimate(flops=10**7, bytes_accessed=10**7, transcendentals=0),
    )(output, gtok, blocks, qkv_a, qkv_b, packet, gcond)


def plain_backward_kernel(
    tokens_ref,
    pat_ref,
    gain_ref,
    gmid_ref,
    do_ref,
    q_ref,
    k_ref,
    v_ref,
    all_ref,
    own_ref,
    tab_ref,
    gtok_ref,
    gq_ref,
    small_ref,
    packed,
    acc_k,
    acc_v,
    acc_w,
    kept,
    csend,
    cland,
    rsend,
    rland,
    c_send,
    c_recv,
    r_send,
    r_recv,
):
    n, ny, nx, z, c = place()
    local = tokens_ref.shape[0]
    half = local // 2
    length = 4 * local
    plane_barrier(n, z, c)
    lanes = lane((local, 128))

    def turned(values, rows):
        cosine, sine = cos_sin(tab_ref[rows, :])
        return values * cosine - halves_turn(values) * sine

    def rounded(values):
        return values.astype(BF16).astype(F32)

    for j in range(OWN):
        acc_k[...] = jnp.zeros_like(acc_k)
        acc_v[...] = jnp.zeros_like(acc_v)

        def quarter_step(i, carry):
            rows = pl.ds(pl.multiple_of(i * local, local), local)
            block = do_ref[j, i].astype(F32)
            grad = jnp.concatenate([block, pltpu.roll(block, 64, 1)], axis=0)
            grad = jnp.where(lanes < 64, grad, 0.0).astype(BF16)
            query = q_ref[j, rows, :]
            probs = jnp.exp2(dg(query, k_ref[j], NT) * LOG2E)
            gprobs = probs * dg(grad, v_ref[j], NT)
            scores = (gprobs - probs * jnp.sum(gprobs, axis=1, keepdims=True)).astype(BF16)
            probs = probs.astype(BF16)
            gquery = rounded(dg(scores, k_ref[j], NN) * HEAD_DIM**-0.5)
            at = Q_AT[j]
            packed[rows, at : at + 64] = turned(gquery, rows)[:, :64].astype(BF16)
            acc_v[...] += dg(grad.T[:64], probs, NN)
            acc_k[...] += dg(query.T[:64], scores, NN)
            return carry

        lax.fori_loop(0, 4, quarter_step, 0)

        def finish(i, carry):
            rows = pl.ds(pl.multiple_of(i * local, local), local)
            both = jnp.concatenate([acc_k[:, rows], acc_v[:, rows]], axis=0).T
            both = rounded(both)
            packed[rows, KV_AT[j] : KV_AT[j] + 128] = jnp.where(
                lanes < 64, turned(both, rows), both
            ).astype(BF16)
            return carry

        lax.fori_loop(0, 4, finish, 0)
    packed[:, 576:640] = jnp.zeros((length, 64), BF16)

    def rows_of(quarter, hh):
        return pl.ds(pl.multiple_of(quarter * local + hh * half, half), half)

    def c_copy(quarter):
        return remote(
            csend.at[quarter], cland.at[quarter], c_send.at[quarter], c_recv.at[quarter],
            sibling(n, z, c),
        )

    def r_copy(quarter):
        is_self = jnp.logical_and(quarter == n, nx == c)
        return (
            is_self,
            rsend.at[quarter],
            rland.at[ny, pl.ds(pl.multiple_of(c * half, half), half)],
            r_send.at[quarter],
            r_recv.at[ny, c],
            (quarter, 2 * z + nx),
        )

    def order(i):
        return lax.rem(n + 3 - i, 4)

    def give(i, carry):
        quarter = order(i)
        csend[quarter] = dg(packed[rows_of(quarter, 1 - c), :], own_ref[...], NT).astype(BF16)
        c_copy(quarter).start()
        return carry

    lax.fori_loop(0, 4, give, 0)

    def keep(i, carry):
        quarter = order(i)
        kept[quarter] = dg(packed[rows_of(quarter, c), :], own_ref[...], NT)
        return carry

    lax.fori_loop(0, 4, keep, 0)

    def add(i, carry):
        quarter = order(i)
        wait_bytes(cland.at[quarter], c_recv.at[quarter])
        rsend[quarter] = (kept[quarter] + cland[quarter].astype(F32)).astype(BF16)
        send_or_keep(*r_copy(quarter))
        return carry

    lax.fori_loop(0, 4, add, 0)

    acc_w[...] = jnp.zeros_like(acc_w)

    def weights(i, carry):
        rows = pl.ds(pl.multiple_of(i * local, local), local)
        acc_w[...] += dg(all_ref[rows, :], packed[rows, :], TN)
        return carry

    lax.fori_loop(0, 4, weights, 0)
    gq_ref[...] = acc_w[...].astype(BF16).reshape(gq_ref.shape)

    normed, inv = norm_stats(tokens_ref[...].astype(F32))
    for y in range(2):
        for hh in range(2):
            wait_bytes(rland.at[y, pl.ds(hh * half, half)], r_recv.at[y, hh])
    gfirst = rland[0].astype(F32) + rland[1].astype(F32)
    small_ref[:, 0:D] = sum8(gfirst)
    small_ref[:, D : 2 * D] = sum8(gfirst * normed)
    amp = row_of(gain_ref) * (1.0 + pat_ref[:, D : 2 * D])
    grad = flat8(by8(gfirst) * amp[None])
    mean = jnp.mean(grad, axis=-1, keepdims=True)
    along = jnp.mean(grad * normed, axis=-1, keepdims=True)
    gtok_ref[...] = gmid_ref[...] + (grad - mean - normed * along) * inv

    def drain(quarter, carry):
        c_copy(quarter).wait_send()
        wait_send_unless(*r_copy(quarter))
        return carry

    lax.fori_loop(0, 4, drain, 0)


def call_plain_backward(tokens, pat, gain, gmid, do, q, k, v, everything, own, tab):
    local = tokens.shape[0]
    half = local // 2
    length = 4 * local
    sds = jax.ShapeDtypeStruct
    return pl.pallas_call(
        plain_backward_kernel,
        out_shape=(
            sds((local, D), F32),
            sds((8, 96, WCOLS), BF16),
            sds((8, 2 * D), F32),
        ),
        in_specs=[vm()] * 11,
        out_specs=(vm(),) * 3,
        scratch_shapes=[
            VMEM((length, WCOLS), BF16),
            VMEM((64, length), F32),
            VMEM((64, length), F32),
            VMEM((D, WCOLS), F32),
            VMEM((4, half, D), F32),
            VMEM((4, half, D), BF16),
            VMEM((4, half, D), BF16),
            VMEM((4, half, D), BF16),
            VMEM((2, local, D), BF16),
            dma(4),
            dma(4),
            dma(4),
            dma(2, 2),
        ],
        compiler_params=params(2, 60),
        cost_estimate=pl.CostEstimate(flops=2 * 10**10, bytes_accessed=3 * 10**7, transcendentals=10**7),
    )(tokens, pat, gain, gmid, do, q, k, v, everything, own, tab)


def plain_sums(g, gq, own_ids):
    n, z, c = own_ids
    up = g[:, :, :192].reshape(8, 4, 2, 96, 384).transpose(0, 3, 1, 2, 4).reshape(D, FF)
    down = g[:, :, 192:384].reshape(8, D, 384).transpose(0, 2, 1).reshape(FF, D)
    out = g[:, :, 384:].reshape(8, 2, 2, 48, 384).transpose(0, 1, 3, 2, 4).reshape(D, D)
    flat = gq.reshape(D, WCOLS)
    pieces = []
    for starts in (Q_AT, KV_AT, [at + HEAD_DIM for at in KV_AT]):
        pieces.append(jnp.concatenate([flat[:, at : at + HEAD_DIM] for at in starts], axis=1))
    group = 2 * (n // 2) + c
    whole = jnp.zeros((D, 3, 4, OWN * HEAD_DIM), F32)
    for part in range(3):
        whole = lax.dynamic_update_slice(
            whole, pieces[part].astype(F32)[:, None, None, :], (0, part, group, 0)
        )
    whole = whole.reshape(D, 3 * D)

    def total(values):
        share = lax.psum_scatter(values.astype(F32), "wide", scatter_dimension=0, tiled=True)
        return lax.psum(share, "narrow")

    return total(whole), total(out), total(up), total(down)


def body(
    tokens,
    condition,
    docs_per_row,
    w_ada,
    b_ada,
    gain_one,
    w_qkv,
    w_out,
    gain_two,
    w_up,
    b_up,
    w_down,
    b_down,
    cotangent,
):
    local = tokens.shape[1]
    x = tokens.reshape(local, D)
    cot = cotangent.reshape(local, D)
    cond = condition.reshape(DOCS, -1)
    table = jnp.asarray(rotary_table(4 * local))

    att, everything, q, k, v, pat, own, tab = call_forward(
        docs_per_row, x, cond, w_ada, b_ada, gain_one, w_qkv, table
    )
    if (lax.axis_size("narrow"), lax.axis_size("wide")) == (4, 8):
        output, gtok, blocks, qkv_a, qkv_b, packet, gcond = call_fused(
            docs_per_row, x, cot, att, cond, pat, gain_one, gain_two, b_up,
            b_down, w_ada, w_out, w_up, w_down, q, k, v, everything, own, tab,
        )
        output, gtok, gcond, gqkv, gout, gup, gdown, gada, *vectors = call_finish(
            output, gtok, blocks, qkv_a, qkv_b, packet, gcond
        )
        gvec_ada, gvec_one, gvec_two, gvec_up, gvec_down = vectors
        return (
            output[None],
            gtok[None],
            gcond,
            gada.T,
            gvec_ada,
            gvec_one,
            gqkv,
            gout,
            gvec_two,
            gup,
            gvec_up,
            gdown,
            gvec_down,
        )

    output, gmid, g, small_two, do = call_middle(
        x, cot, att, pat, gain_two, w_out, w_up, b_up, w_down, b_down
    )
    gtok, gq, small_one = call_plain_backward(
        x, pat, gain_one, gmid, do, q, k, v, everything, own, tab
    )
    n, w = lax.axis_index("narrow"), lax.axis_index("wide")
    sum_qkv, sum_out, sum_up, sum_down = plain_sums(g, gq, (n, w // 2, w % 2))

    small = jnp.concatenate([small_one, small_two], axis=1).reshape(4, 2, -1).sum(0)
    small = lax.psum(small, "narrow")
    shift_one, raw_one, gate_one, shift_two, raw_two, gate_two = jnp.split(small[:, : 6 * D], 6, axis=1)
    scales = pat[:2].reshape(2, 6, D)
    sum_gain_one = jnp.sum(raw_one * (1.0 + scales[:, 1]), axis=0)
    sum_gain_two = jnp.sum(raw_two * (1.0 + scales[:, 4]), axis=0)
    grads = jnp.concatenate(
        [
            shift_one,
            raw_one * gain_one.astype(F32),
            gate_one,
            shift_two,
            raw_two * gain_two.astype(F32),
            gate_two,
        ],
        axis=1,
    )
    two = docs_per_row[0] == DOCS
    grad_mods = jnp.stack(
        [jnp.where(two, grads[0], grads[0] + grads[1]), jnp.where(two, grads[1], 0.0)]
    )
    high = lax.Precision.HIGHEST
    grad_condition = jnp.einsum("sm,cm->sc", grad_mods, w_ada.astype(F32), precision=high)[None]
    part_ada = jnp.einsum("sm,sc->mc", grad_mods, cond.astype(F32), precision=high)

    def share(values):
        return lax.psum_scatter(values, "wide", scatter_dimension=0, tiled=True)

    sum_b_up = jnp.sum(small[:, 6 * D : 6 * D + FF], axis=0)
    sum_b_down = jnp.sum(small[:, 6 * D + FF :], axis=0)
    return (
        output[None],
        gtok[None],
        grad_condition,
        share(part_ada).T,
        share(jnp.sum(grad_mods, axis=0)),
        share(sum_gain_one),
        sum_qkv,
        sum_out,
        share(sum_gain_two),
        sum_up,
        share(sum_b_up),
        sum_down,
        share(sum_b_down),
    )


def solution(mesh):
    in_specs = (
        P("wide", "narrow", None),
        P("wide", None, None),
        P("wide"),
        P(),
        P(),
        P(),
        P(),
        P(),
        P(),
        P(),
        P(),
        P(),
        P(),
        P("wide", "narrow", None),
    )
    out_specs = (
        P("wide", "narrow", None),
        P("wide", "narrow", None),
        P("wide", None, None),
        P(None, "wide"),
        P("wide"),
        P("wide"),
        P("wide", None),
        P("wide", None),
        P("wide"),
        P("wide", None),
        P("wide"),
        P("wide", None),
        P("wide"),
    )
    return jax.shard_map(body, mesh=mesh, in_specs=in_specs, out_specs=out_specs, check_vma=False)
```

```python
import functools

import jax
import jax.numpy as jnp
import numpy as np
from jax import lax
from jax.experimental import pallas as pl
from jax.experimental.pallas import tpu as pltpu
from jax.sharding import PartitionSpec as P

D = 768
HEADS = 12
HEAD_DIM = 64
FF = 3072
DOCS = 2
EPS = 1e-05
LOG2E = 1.4426950408889634
BIG = 1e30
OWN = 3
WCOLS = 640
KV_AT = (0, 128, 384)
Q_AT = (256, 320, 512)
ROWS_G = 432
COLS_G = 384
MESH = pl.DeviceIdType.MESH
F32 = jnp.float32
BF16 = jnp.bfloat16
NN = (((1,), (0,)), ((), ()))
NT = (((1,), (1,)), ((), ()))
TN = (((0,), (0,)), ((), ()))
VMEM = pltpu.VMEM
ANY = pl.ANY


def dg(a, b, dims):
    return lax.dot_general(a, b, dims, preferred_element_type=F32)


def place():
    n = lax.axis_index("narrow")
    w = lax.axis_index("wide")
    return n, n // 2, lax.rem(n, 2), w // 2, lax.rem(w, 2)


def sibling(n, z, c):
    return (n, 2 * z + 1 - c)


def plane_barrier(n, z, c, wait=True):
    barrier = pltpu.get_barrier_semaphore()
    me = n * 2 + c
    for step in range(1, 8):
        other = lax.rem(me + step, 8)
        pl.semaphore_signal(
            barrier, inc=1, device_id=(other // 2, 2 * z + lax.rem(other, 2)), device_id_type=MESH
        )
    if wait:
        pl.semaphore_wait(barrier, 7)


def remote(src, dst, send, recv, device):
    return pltpu.make_async_remote_copy(
        src_ref=src, dst_ref=dst, send_sem=send, recv_sem=recv, device_id=device, device_id_type=MESH
    )


def send_or_keep(is_self, src, dst, send, recv, device):
    @pl.when(is_self)
    def _():
        pltpu.make_async_copy(src, dst, recv).start()

    @pl.when(jnp.logical_not(is_self))
    def _():
        remote(src, dst, send, recv, device).start()


def wait_send_unless(is_self, src, dst, send, recv, device):
    @pl.when(jnp.logical_not(is_self))
    def _():
        remote(src, dst, send, recv, device).wait_send()


def wait_bytes(ref, sem):
    pltpu.make_async_copy(ref, ref, sem).wait()


def row_of(ref):
    return ref[...].astype(F32).reshape(1, ref.shape[0])


def lane(shape):
    return lax.broadcasted_iota(jnp.int32, shape, len(shape) - 1)


def by8(values):
    return values.reshape(values.shape[0] // 8, 8, values.shape[1])


def flat8(values):
    return values.reshape(values.shape[0] * 8, values.shape[2])


def sum8(values):
    return jnp.sum(by8(values), axis=0)


def norm_stats(values):
    mean = jnp.mean(values, axis=-1, keepdims=True)
    centred = values - mean
    spread = jnp.mean(centred * centred, axis=-1, keepdims=True)
    inv = lax.rsqrt(spread + EPS)
    return centred * inv, inv


def halves_turn(values):
    where = lax.rem(lane(values.shape), 64) < 32
    return jnp.where(where, pltpu.roll(values, 96, 1), pltpu.roll(values, 32, 1))


def cos_sin(table):
    lanes = lane(table.shape)
    other = pltpu.roll(table, 64, 1)
    cosine = jnp.where(lanes < 64, table, other)
    sine = jnp.where(lanes < 64, other, table)
    return cosine, jnp.where(lax.rem(lanes, 64) < 32, -sine, sine)


def split3(column):
    high = column.astype(BF16).astype(F32)
    rest = column - high
    middle = rest.astype(BF16).astype(F32)
    low = (rest - middle).astype(BF16).astype(F32)
    return high, middle, low


def forward_kernel(
    docs_ref,
    tokens_ref,
    cond_ref,
    w_ada_ref,
    b_ada_ref,
    gain_ref,
    w_qkv_hbm,
    table_hbm,
    att_ref,
    all_hbm,
    q_hbm,
    k_hbm,
    v_hbm,
    pat_ref,
    own_hbm,
    tab_hbm,
    q_ref,
    k_ref,
    v_ref,
    own_ref,
    tab_ref,
    mine,
    gathered,
    w_qkv,
    tables,
    osend,
    oland,
    docs_mine,
    docs_other,
    load_sem,
    docs_sem,
    a_send,
    a_recv,
    f_send,
    f_recv,
    o_send,
    o_recv,
    keep_sem,
):
    n, ny, nx, z, c = place()
    local = tokens_ref.shape[0]
    half = local // 2
    length = local * 4
    loads = [
        pltpu.make_async_copy(w_qkv_hbm, w_qkv, load_sem.at[0]),
        pltpu.make_async_copy(table_hbm, tables, load_sem.at[1]),
    ]
    for load in loads:
        load.start()
    docs_mine[...] = jnp.full(docs_mine.shape, docs_ref[0], jnp.int32).astype(F32)
    plane_barrier(n, z, c, wait=False)
    docs_copy = remote(docs_mine, docs_other, docs_sem.at[0], docs_sem.at[1], sibling(n, z, c))

    two = docs_ref[0] == DOCS
    parity = lax.rem(lax.broadcasted_iota(jnp.int32, (16, 128), 0), 2)
    odd = jnp.logical_and(parity == 1, two)
    cond = cond_ref[...].astype(F32)
    cond16 = jnp.where(odd, cond[1:2, :], cond[0:1, :]).astype(BF16)
    pat_ref[...] = dg(cond16, w_ada_ref[...], NN)[:8] + row_of(b_ada_ref)

    shift = pat_ref[:, 0:D]
    amp = row_of(gain_ref) * (1.0 + pat_ref[:, D : 2 * D])

    def a_copy(my, hh):
        target = 2 * my + c
        is_self = jnp.logical_and(target == n, c == hh)
        return (
            is_self,
            mine.at[pl.ds(hh * half, half)],
            gathered.at[pl.ds(pl.multiple_of(n * local + hh * half, half), half)],
            a_send.at[my * 2 + hh],
            a_recv.at[n],
            (target, 2 * z + hh),
        )

    for hh in range(2):
        normed, _ = norm_stats(tokens_ref[hh * half : (hh + 1) * half, :].astype(F32))
        mine[hh * half : (hh + 1) * half, :] = flat8(by8(normed) * amp[None] + shift[None]).astype(
            BF16
        )
        if hh == 0:
            pl.semaphore_wait(pltpu.get_barrier_semaphore(), 7)
            docs_copy.start()
        for my in range(2):
            send_or_keep(*a_copy(my, hh))

    for load in loads:
        load.wait()
    group = 2 * ny + c
    lanes_w = lane((D, 128))

    def columns(part, j, at):
        col = part * HEADS + group * OWN + j
        block = w_qkv[:, pl.ds(pl.multiple_of((col // 2) * 128, 128), 128)].astype(F32)
        return pltpu.roll(block, lax.rem(col + at, 2) * 64, 1)

    for j in range(OWN):
        own_ref[:, KV_AT[j] : KV_AT[j] + 128] = jnp.where(
            lanes_w < 64, columns(1, j, 0), columns(2, j, 1)
        ).astype(BF16)
    own_ref[:, 256:384] = jnp.where(lanes_w < 64, columns(0, 0, 0), columns(0, 1, 1)).astype(BF16)
    own_ref[:, 512:640] = jnp.where(lanes_w < 64, columns(0, 2, 0), 0.0).astype(BF16)

    docs_copy.wait()
    docs_heads = jnp.where(nx == c, docs_mine[...], docs_other[...])
    tab_ref[...] = jnp.where(docs_heads[0:1] == DOCS, tables[1], tables[0])

    lanes = lane((8, 128))
    odd8 = jnp.logical_and(parity[:8] == 1, docs_heads == DOCS)
    tail_q = jnp.where(lanes == 64, jnp.where(odd8, 0.0, 1.0), 0.0)
    tail_q = jnp.where(lanes == 65, jnp.where(odd8, 1.0, 0.0), tail_q)
    tail_k = jnp.where(lanes == 64, jnp.where(odd8, -BIG, 0.0), 0.0)
    tail_k = jnp.where(lanes == 65, jnp.where(odd8, 0.0, -BIG), tail_k)
    tail_k = jnp.where(jnp.logical_and(lanes >= 66, lanes < 69), 1.0, tail_k)

    def with_tail(values, tail):
        shaped = by8(values)
        return flat8(jnp.where(lane(shaped.shape) < 64, shaped, tail[None])).astype(BF16)

    def project(source):
        def step(i, carry):
            rows = pl.ds(pl.multiple_of(source * local + i * half, half), half)
            wide = dg(gathered[rows, :], own_ref[...], NN)
            cosine, sine = cos_sin(tab_ref[rows, :])

            def rot(values):
                return values * cosine + halves_turn(values) * sine

            for j in range(OWN):
                block = wide[:, KV_AT[j] : KV_AT[j] + 128]
                k_ref[j, rows, :] = with_tail(rot(block), tail_k)
                v_ref[j, rows, :] = jnp.where(
                    lane(block.shape) < 64, pltpu.roll(block, 64, 1), 1.0
                ).astype(BF16)
            first = rot(wide[:, 256:384]) * HEAD_DIM**-0.5
            q_ref[0, rows, :] = with_tail(first, tail_q)
            q_ref[1, rows, :] = with_tail(pltpu.roll(first, 64, 1), tail_q)
            q_ref[2, rows, :] = with_tail(rot(wide[:, 512:640]) * HEAD_DIM**-0.5, tail_q)
            return carry

        lax.fori_loop(0, 2, step, 0)

    def part(source, hh):
        return gathered.at[pl.ds(pl.multiple_of(source * local + hh * half, half), half)]

    def forward(source):
        wait_bytes(part(source, c), a_recv.at[source])
        remote(
            part(source, c), part(source, c), f_send.at[source], f_recv.at[source], sibling(n, z, c)
        ).start()

    sources = [n, lax.rem(n + 2, 4), n + 1 - 2 * nx, lax.rem(n + 3 - 2 * nx, 4)]

    def arrive(source):
        wait_bytes(part(source, 1 - c), f_recv.at[source])
        project(source)

    forward(sources[0])
    forward(sources[1])
    arrive(sources[0])
    forward(sources[2])
    arrive(sources[1])
    forward(sources[3])
    arrive(sources[2])
    arrive(sources[3])
    keeps = [
        pltpu.make_async_copy(src, dst, keep_sem.at[i])
        for i, (src, dst) in enumerate(
            (
                (gathered, all_hbm),
                (k_ref, k_hbm),
                (v_ref, v_hbm),
                (own_ref, own_hbm),
                (tab_ref, tab_hbm),
                (q_ref, q_hbm),
            )
        )
    ]
    for keep in keeps[:5]:
        keep.start()

    def o_copy(j, quarter):
        is_self = jnp.logical_and(quarter == n, nx == c)
        return (
            is_self,
            osend.at[j, quarter],
            oland.at[group * OWN + j],
            o_send.at[j, quarter],
            o_recv.at[group * OWN + j],
            (quarter, 2 * z + nx),
        )

    def attend(index, carry):
        j = index // 4
        quarter = lax.rem(n + 3 - lax.rem(index, 4), 4)
        start = quarter * local
        scores = []
        for u in range(2):
            rows = pl.ds(pl.multiple_of(start + u * half, half), half)
            scores.append(dg(q_ref[j, rows, :], k_ref[j], NT))
        outs = []
        for u in range(2):
            rows = pl.ds(pl.multiple_of(start + u * half, half), half)
            top = jnp.max(scores[u], axis=1, keepdims=True)
            weights = jnp.exp2((scores[u] - top) * LOG2E)
            total = jnp.sum(weights, axis=1, keepdims=True)
            mixed = dg((weights * (1.0 / total)).astype(BF16), v_ref[j], NN)
            high, middle, low = split3(top + jnp.log(total))
            query = q_ref[j, rows, :].astype(F32)
            lanes_q = lane(query.shape)
            query = jnp.where(lanes_q == 66, -high, query)
            query = jnp.where(lanes_q == 67, -middle, query)
            q_ref[j, rows, :] = jnp.where(lanes_q == 68, -low, query).astype(BF16)
            outs.append(mixed)
        osend[j, quarter] = jnp.where(
            lane(outs[0].shape) < 64, outs[0], pltpu.roll(outs[1], 64, 1)
        ).astype(BF16)
        send_or_keep(*o_copy(j, quarter))
        return carry

    lax.fori_loop(0, OWN * 4, attend, 0)
    keeps[5].start()

    for head in range(HEADS):
        wait_bytes(oland.at[head], o_recv.at[head])
    for pair in range(HEADS // 2):
        even = oland[2 * pair].astype(F32)
        odd_head = oland[2 * pair + 1].astype(F32)
        low = lane(even.shape) < 64
        cols = slice(pair * 128, (pair + 1) * 128)
        att_ref[0:half, cols] = jnp.where(low, even, pltpu.roll(odd_head, 64, 1)).astype(BF16)
        att_ref[half:local, cols] = jnp.where(low, pltpu.roll(even, 64, 1), odd_head).astype(BF16)

    for hh in range(2):
        for my in range(2):
            wait_send_unless(*a_copy(my, hh))
    for source in range(4):
        remote(
            part(source, c), part(source, c), f_send.at[source], f_recv.at[source], sibling(n, z, c)
        ).wait_send()

    def drain(index, carry):
        wait_send_unless(*o_copy(index // 4, lax.rem(index, 4)))
        return carry

    lax.fori_loop(0, OWN * 4, drain, 0)
    for keep in keeps:
        keep.wait()


def vm():
    return pl.BlockSpec(memory_space=VMEM)


def hbm():
    return pl.BlockSpec(memory_space=ANY)


def smem():
    return pl.BlockSpec(memory_space=pltpu.SMEM)


def params(collective_id, limit=56):
    return pltpu.CompilerParams(
        collective_id=collective_id, has_side_effects=True, vmem_limit_bytes=limit * 2**20
    )


def dma(*shape):
    return pltpu.SemaphoreType.DMA(shape)


def call_forward(docs, tokens, cond, w_ada, b_ada, gain, w_qkv, table):
    local = tokens.shape[0]
    length = 4 * local
    half = local // 2
    sds = jax.ShapeDtypeStruct
    return pl.pallas_call(
        forward_kernel,
        out_shape=(
            sds((local, D), BF16),
            sds((length, D), BF16),
            sds((OWN, length, 128), BF16),
            sds((OWN, length, 128), BF16),
            sds((OWN, length, 128), BF16),
            sds((8, 6 * D), F32),
            sds((D, WCOLS), BF16),
            sds((length, 128), F32),
        ),
        in_specs=[smem(), vm(), vm(), vm(), vm(), vm(), hbm(), hbm()],
        out_specs=(vm(), hbm(), hbm(), hbm(), hbm(), vm(), hbm(), hbm()),
        scratch_shapes=[
            VMEM((OWN, length, 128), BF16),
            VMEM((OWN, length, 128), BF16),
            VMEM((OWN, length, 128), BF16),
            VMEM((D, WCOLS), BF16),
            VMEM((length, 128), F32),
            VMEM((local, D), BF16),
            VMEM((length, D), BF16),
            VMEM((D, 3 * D), BF16),
            VMEM((2, length, 128), F32),
            VMEM((OWN, 4, half, 128), BF16),
            VMEM((HEADS, half, 128), BF16),
            VMEM((8, 128), F32),
            VMEM((8, 128), F32),
            dma(2),
            dma(2),
            dma(4),
            dma(4),
            dma(4),
            dma(4),
            dma(OWN, 4),
            dma(HEADS),
            dma(6),
        ],
        compiler_params=params(0),
        cost_estimate=pl.CostEstimate(flops=10**10, bytes_accessed=2 * 10**7, transcendentals=10**7),
    )(docs, tokens, cond, w_ada, b_ada, gain, w_qkv, table)


def rotary_table(length):
    freq = 10000.0 ** (-np.arange(HEAD_DIM // 2, dtype=np.float64) * 2.0 / HEAD_DIM)
    tables = []
    for docs in (1, DOCS):
        angle = (np.arange(length) // docs)[:, None] * freq[None, :]
        cosine, sine = np.cos(angle), np.sin(angle)
        tables.append(np.concatenate([cosine, cosine, sine, sine], axis=1))
    return np.stack(tables).astype(np.float32)


SMALL = 4 * D + FF + D


def middle_kernel(
    tokens_ref,
    cot_ref,
    att_ref,
    pat_ref,
    gain_ref,
    w_out_ref,
    w_up_ref,
    b_up_ref,
    w_down_ref,
    b_down_ref,
    out_ref,
    gmid_ref,
    g_ref,
    small_ref,
    do_ref,
    second_ref,
    active_ref,
    slope_ref,
    down_ref,
    gsecond_ref,
    middle_ref,
    branch_ref,
    lhs_t,
    gdown_ref,
    dsend,
    dland,
    d_send,
    d_recv,
):
    n, ny, nx, z, c = place()
    group = 2 * ny + c
    local = tokens_ref.shape[0]
    half = local // 2
    tile = 768
    plane_barrier(n, z, c)

    def piece(index):
        return pat_ref[:, index * D : (index + 1) * D]

    def spread(values, pattern):
        return flat8(by8(values) * pattern[None])

    branch_ref[...] = dg(att_ref[...], w_out_ref[...], NN)
    middle = tokens_ref[...].astype(F32) + spread(branch_ref[...], piece(2))
    middle_ref[...] = middle
    amp = row_of(gain_ref) * (1.0 + piece(4))
    normed, _ = norm_stats(middle)
    second = flat8(by8(normed) * amp[None] + piece(3)[None]).astype(BF16)
    second_ref[...] = second
    down_ref[...] = jnp.broadcast_to(row_of(b_down_ref), down_ref.shape)

    def up(t, carry):
        cols = pl.ds(pl.multiple_of(t * tile, tile), tile)
        hidden = dg(second_ref[...], w_up_ref[:, cols], NN) + b_up_ref[cols].astype(F32).reshape(1, tile)
        square = hidden * hidden
        bend = jnp.tanh(0.7978845608028654 * hidden * (1.0 + 0.044715 * square))
        part = 0.5 * (1.0 + bend)
        active_ref[:, cols] = (hidden * part).astype(BF16)
        slope_ref[:, cols] = part + (0.5 * 0.7978845608028654) * hidden * (1.0 - bend * bend) * (
            1.0 + 3.0 * 0.044715 * square
        )
        down_ref[...] += dg(active_ref[:, cols], w_down_ref[cols, :], NN)
        return carry

    lax.fori_loop(0, FF // tile, up, 0)

    cot = cot_ref[...].astype(F32)
    down = down_ref[...]
    out_ref[...] = (middle_ref[...] + spread(down, piece(5))).astype(BF16)
    small_ref[:, 3 * D : 4 * D] = sum8(cot * down)
    gdown = spread(cot, piece(5)).astype(BF16)
    gdown_ref[...] = gdown
    small_ref[:, 4 * D + FF :] = sum8(gdown.astype(F32))
    lhs_t[0] = second_ref[...].T
    lhs_t[1] = gdown.T
    gsecond_ref[...] = jnp.zeros_like(gsecond_ref)

    def back(t, carry):
        cols = pl.ds(pl.multiple_of(t * tile, tile), tile)
        ghidden = dg(gdown_ref[...], w_down_ref[cols, :], NT) * slope_ref[:, cols]
        low = ghidden.astype(BF16)
        small_ref[:, pl.ds(pl.multiple_of(4 * D + t * tile, tile), tile)] = sum8(low.astype(F32))
        gsecond_ref[...] += dg(low, w_up_ref[:, cols], NT)
        gup = dg(lhs_t[0], low, NN).astype(BF16)
        for hh in range(2):
            g_ref[:, t, hh * 96 : (hh + 1) * 96, :] = gup[:, hh * 384 : (hh + 1) * 384].reshape(
                8, 96, 384
            )
        gdw = dg(lhs_t[1], active_ref[:, cols], NN).astype(BF16)
        for hh in range(2):
            g_ref[2 * t + hh, :, 192:384, :] = gdw[:, hh * 384 : (hh + 1) * 384].reshape(4, 192, 384)
        return carry

    lax.fori_loop(0, FF // tile, back, 0)

    normed, inv = norm_stats(middle_ref[...])
    gsecond = gsecond_ref[...]
    small_ref[:, D : 2 * D] = sum8(gsecond)
    small_ref[:, 2 * D : 3 * D] = sum8(gsecond * normed)
    amp = row_of(gain_ref) * (1.0 + piece(4))
    grad = spread(gsecond, amp)
    mean = jnp.mean(grad, axis=-1, keepdims=True)
    along = jnp.mean(grad * normed, axis=-1, keepdims=True)
    gmid = cot_ref[...].astype(F32) + (grad - mean - normed * along) * inv
    gmid_ref[...] = gmid
    small_ref[:, 0:D] = sum8(gmid * branch_ref[...])
    gbranch = spread(gmid, piece(2)).astype(BF16)
    gatt = dg(gbranch, w_out_ref[...], NT)

    def d_copy(quarter_x, pick_y, cc, j):
        target = 2 * pick_y + c
        head = (2 * pick_y + cc) * OWN + j
        is_self = jnp.logical_and(target == n, c == cc)
        return (
            is_self,
            dsend.at[head],
            dland.at[j, n],
            d_send.at[head],
            d_recv.at[j, n],
            (target, 2 * z + cc),
        )

    copies = []
    for pair in range(HEADS // 2):
        top = gatt[0:half, pair * 128 : (pair + 1) * 128]
        bottom = gatt[half:local, pair * 128 : (pair + 1) * 128]
        low = lane(top.shape) < 64
        dsend[2 * pair] = jnp.where(low, top, pltpu.roll(bottom, 64, 1)).astype(BF16)
        dsend[2 * pair + 1] = jnp.where(low, pltpu.roll(top, 64, 1), bottom).astype(BF16)
    for head in range(HEADS):
        copies.append(d_copy(None, head // OWN // 2, (head // OWN) % 2, head % OWN))
        send_or_keep(*copies[-1])

    for hh in range(2):
        gout = dg(att_ref[...], gbranch[:, hh * 384 : (hh + 1) * 384], TN).astype(BF16)
        shaped = gout.reshape(8, 2, 48, 384)
        for rh in range(2):
            g_ref[:, rh * 2 + hh, 384:432, :] = shaped[:, rh]

    for j in range(OWN):
        for quarter in range(4):
            wait_bytes(dland.at[j, quarter], d_recv.at[j, quarter])
    do_ref[...] = dland[...]
    for copy in copies:
        wait_send_unless(*copy)


def call_middle(tokens, cot, att, pat, gain, w_out, w_up, b_up, w_down, b_down):
    local = tokens.shape[0]
    half = local // 2
    sds = jax.ShapeDtypeStruct
    return pl.pallas_call(
        middle_kernel,
        out_shape=(
            sds((local, D), BF16),
            sds((local, D), F32),
            sds((8, 4, ROWS_G, COLS_G), BF16),
            sds((8, SMALL), F32),
            sds((OWN, 4, half, 128), BF16),
        ),
        in_specs=[vm()] * 10,
        out_specs=(vm(),) * 5,
        scratch_shapes=[
            VMEM((local, D), BF16),
            VMEM((local, FF), BF16),
            VMEM((local, FF), F32),
            VMEM((local, D), F32),
            VMEM((local, D), F32),
            VMEM((local, D), F32),
            VMEM((local, D), F32),
            VMEM((2, D, local), BF16),
            VMEM((local, D), BF16),
            VMEM((HEADS, half, 128), BF16),
            VMEM((OWN, 4, half, 128), BF16),
            dma(HEADS),
            dma(OWN, 4),
        ],
        compiler_params=params(1, 60),
        cost_estimate=pl.CostEstimate(flops=2 * 10**10, bytes_accessed=3 * 10**7, transcendentals=10**7),
    )(tokens, cot, att, pat, gain, w_out, w_up, b_up, w_down, b_down)


CUT = 320
CHUNK = 24
PARTS_Q = ((0, 384), (384, 256))


def slot_of(other, me):
    return lax.rem(other - me + 3, 4)


def fused_kernel(
    docs_ref,
    tokens_ref,
    cot_ref,
    att_ref,
    cond_ref,
    pat_ref,
    gain_one_ref,
    gain_ref,
    b_up_ref,
    b_down_ref,
    w_ada_hbm,
    w_out_hbm,
    w_up_hbm,
    w_down_hbm,
    q_hbm,
    k_hbm,
    v_hbm,
    all_hbm,
    own_hbm,
    tab_hbm,
    out_ref,
    gtok_ref,
    blocks_ref,
    qkv_a_ref,
    qkv_b_ref,
    packet_ref,
    gcond_ref,
    small_ref,
    small_one,
    dsend,
    dland,
    g_own,
    g_land,
    land_x1,
    land_y1,
    land_x2,
    land_y2,
    land_b1,
    land_a2,
    land_b2,
    block,
    land_block,
    cland,
    rland,
    gq_a,
    gq_b,
    land_qx_a,
    land_qx_b,
    land_qz_a,
    land_qz_b,
    land_q_a,
    land_q_b,
    pack,
    land_s1,
    pack_sum,
    land_s2,
    gc_mine,
    land_gc,
    load_sem,
    d_send,
    d_recv,
    g_send,
    g_recv,
    one_sem,
    two_sem,
    b1_send,
    b1_recv,
    a2_send,
    a2_recv,
    b2_send,
    b2_recv,
    ag_send,
    ag_recv,
    c_send,
    c_recv,
    r_send,
    r_recv,
    qx_sem,
    qz_send,
    qz_recv,
    qp_send,
    qp_recv,
    s1_send,
    s1_recv,
    s2_send,
    s2_recv,
    gc_send,
    gc_recv,
):
    n, ny, nx, z, c = place()
    w = 2 * z + c
    local = tokens_ref.shape[0]
    half = local // 2
    length = local * 4
    group = 2 * ny + c
    tile = 768
    across = n + 1 - 2 * nx
    along_y = lax.rem(n + 2, 4)

    barrier = pltpu.get_barrier_semaphore()

    def greet(device):
        pl.semaphore_signal(barrier, inc=1, device_id=device, device_id_type=MESH)

    me = n * 2 + c
    for step in range(1, 8):
        other = lax.rem(me + step, 8)
        greet((other // 2, 2 * z + lax.rem(other, 2)))
    for step in range(1, 4):
        greet((n, 2 * lax.rem(z + step, 4) + c))
    for row in range(8):

        @pl.when(jnp.logical_not(jnp.logical_and(z == n, row == w)))
        def _():
            greet((z, row))

    def others(base):
        return [lax.rem(base + step, 4) for step in (1, 2, 3)]

    def piece(index):
        return pat_ref[:, index * D : (index + 1) * D]

    def spread(values, pattern):
        return flat8(by8(values) * pattern[None])


    def core_up(g_give, t):
        return remote(
            g_give.at[:, t // 2, t % 2, pl.ds(0, 192)],
            g_land.at[:, t // 2, t % 2, pl.ds(0, 192)],
            g_send.at[t],
            g_recv.at[t],
            sibling(n, z, c),
        )

    def core_down(g_give, t):
        return remote(
            g_give.at[t, :, :, pl.ds(192, 192)],
            g_land.at[t, :, :, pl.ds(192, 192)],
            g_send.at[4 + t],
            g_recv.at[4 + t],
            sibling(n, z, c),
        )

    def core_out(g_give):
        return remote(
            g_give.at[:, :, :, pl.ds(384, 48)],
            g_land.at[:, :, :, pl.ds(384, 48)],
            g_send.at[8],
            g_recv.at[8],
            sibling(n, z, c),
        )

    def d_copy(head):
        pick_y, cc, j = head // OWN // 2, head // OWN % 2, head % OWN
        target = 2 * pick_y + c
        is_self = jnp.logical_and(target == n, c == cc)
        return (
            is_self,
            dsend.at[head],
            dland.at[j, n],
            d_send.at[head],
            d_recv.at[j, n],
            (target, 2 * z + cc),
        )


    def middle(
        w_out, w_up, w_down, active, slope, acc, branch_ref, lhs_t, low_ref, g_give
    ):
        loads = [
            pltpu.make_async_copy(src, dst, load_sem.at[i])
            for i, (src, dst) in enumerate(((w_out_hbm, w_out), (w_up_hbm, w_up), (w_down_hbm, w_down)))
        ]
        for load in loads:
            load.start()
        loads[0].wait()
        branch_ref[...] = dg(att_ref[...], w_out[...], NN)

        def middle_values():
            return tokens_ref[...].astype(F32) + spread(branch_ref[...], piece(2))

        normed, _ = norm_stats(middle_values())
        amp = row_of(gain_ref) * (1.0 + piece(4))
        low_ref[...] = flat8(by8(normed) * amp[None] + piece(3)[None]).astype(BF16)
        acc[...] = jnp.broadcast_to(row_of(b_down_ref), acc.shape)
        loads[1].wait()
        loads[2].wait()

        def up(t, carry):
            cols = pl.ds(pl.multiple_of(t * tile, tile), tile)
            hidden = dg(low_ref[...], w_up[:, cols], NN) + b_up_ref[cols].astype(F32).reshape(1, tile)
            square = hidden * hidden
            bend = jnp.tanh(0.7978845608028654 * hidden * (1.0 + 0.044715 * square))
            part = 0.5 * (1.0 + bend)
            active[:, cols] = (hidden * part).astype(BF16)
            slope[:, cols] = part + (0.5 * 0.7978845608028654) * hidden * (1.0 - bend * bend) * (
                1.0 + 3.0 * 0.044715 * square
            )
            acc[...] += dg(active[:, cols], w_down[cols, :], NN)
            return carry

        lax.fori_loop(0, FF // tile, up, 0)

        cot = cot_ref[...].astype(F32)
        down = acc[...]
        out_ref[...] = (middle_values() + spread(down, piece(5))).astype(BF16)
        small_ref[:, 3 * D : 4 * D] = sum8(cot * down)
        lhs_t[0] = low_ref[...].T
        gdown = spread(cot, piece(5)).astype(BF16)
        low_ref[...] = gdown
        small_ref[:, 4 * D + FF :] = sum8(gdown.astype(F32))
        lhs_t[1] = gdown.T
        acc[...] = jnp.zeros_like(acc)
        pl.semaphore_wait(barrier, jnp.where(z == n, 17, 18))

        def back(t, carry):
            cols = pl.ds(pl.multiple_of(t * tile, tile), tile)
            ghidden = dg(low_ref[...], w_down[cols, :], NT) * slope[:, cols]
            low = ghidden.astype(BF16)
            small_ref[:, pl.ds(pl.multiple_of(4 * D + t * tile, tile), tile)] = sum8(low.astype(F32))
            acc[...] += dg(low, w_up[:, cols], NT)
            gup = dg(lhs_t[0], low, NN).astype(BF16).reshape(4, 2, 96, tile)
            mine = jnp.where(c == 0, gup[:, 0], gup[:, 1])
            other = jnp.where(c == 0, gup[:, 1], gup[:, 0])
            for hh in range(2):
                rows, lanes_h = slice(hh * 96, (hh + 1) * 96), slice(hh * 384, (hh + 1) * 384)
                g_own[:, t // 2, t % 2, rows, :] = mine[:, :, lanes_h]
                g_give[:, t // 2, t % 2, rows, :] = other[:, :, lanes_h]
            core_up(g_give, t).start()
            gdw = dg(lhs_t[1], active[:, cols], NN).astype(BF16)
            mine = jnp.where(c == 0, gdw[:, :384], gdw[:, 384:])
            other = jnp.where(c == 0, gdw[:, 384:], gdw[:, :384])
            g_own[t, :, :, 192:384, :] = mine.reshape(2, 2, 192, 384)
            g_give[t, :, :, 192:384, :] = other.reshape(2, 2, 192, 384)
            core_down(g_give, t).start()
            return carry

        lax.fori_loop(0, FF // tile, back, 0)

        normed, inv = norm_stats(middle_values())
        gsecond = acc[...]
        small_ref[:, D : 2 * D] = sum8(gsecond)
        small_ref[:, 2 * D : 3 * D] = sum8(gsecond * normed)
        grad = spread(gsecond, row_of(gain_ref) * (1.0 + piece(4)))
        mean = jnp.mean(grad, axis=-1, keepdims=True)
        along = jnp.mean(grad * normed, axis=-1, keepdims=True)
        gmid = cot_ref[...].astype(F32) + (grad - mean - normed * along) * inv
        gtok_ref[...] = gmid
        small_ref[:, 0:D] = sum8(gmid * branch_ref[...])
        gbranch = spread(gmid, piece(2)).astype(BF16)
        gatt = dg(gbranch, w_out[...], NT)
        for pair in range(HEADS // 2):
            top = gatt[0:half, pair * 128 : (pair + 1) * 128]
            bottom = gatt[half:local, pair * 128 : (pair + 1) * 128]
            lower = lane(top.shape) < 64
            dsend[2 * pair] = jnp.where(lower, top, pltpu.roll(bottom, 64, 1)).astype(BF16)
            dsend[2 * pair + 1] = jnp.where(lower, pltpu.roll(top, 64, 1), bottom).astype(BF16)
        for j in range(OWN):
            for g in range(4):
                send_or_keep(*d_copy(g * OWN + j))

        both = dg(att_ref[...], gbranch, TN).astype(BF16)
        for hh in range(2):
            shaped = both[:, hh * 384 : (hh + 1) * 384].reshape(4, 2, 2, 48, 384)
            g_own[:, :, hh, 384:432, :] = jnp.where(c == 0, shaped[:, 0], shaped[:, 1])
            g_give[:, :, hh, 384:432, :] = jnp.where(c == 0, shaped[:, 1], shaped[:, 0])
        core_out(g_give).start()
        for t in range(4):
            core_up(g_give, t).wait_send()
            core_down(g_give, t).wait_send()
        core_out(g_give).wait_send()

    pl.run_scoped(
        middle,
        VMEM((D, D), BF16),
        VMEM((D, FF), BF16),
        VMEM((FF, D), BF16),
        VMEM((local, FF), BF16),
        VMEM((local, FF), F32),
        VMEM((local, D), F32),
        VMEM((local, D), F32),
        VMEM((2, D, local), BF16),
        VMEM((local, D), BF16),
        VMEM((4, 2, 2, ROWS_G, COLS_G), BF16),
    )


    top = pl.ds(0, CUT)
    rest = pl.ds(CUT, ROWS_G - CUT)

    def one_x():
        return remote(g_own.at[pl.ds(0, 2), :, 1 - nx, top], land_x1, one_sem.at[0], one_sem.at[1], (across, w))

    def one_y():
        return remote(
            g_own.at[pl.ds(2, 2), 1 - ny, :, top], land_y1, one_sem.at[2], one_sem.at[3], (along_y, w)
        )

    def two_y():
        return remote(
            g_own.at[pl.ds(0, 2), 1 - ny, nx, top], land_y2, two_sem.at[0], two_sem.at[1], (along_y, w)
        )

    def two_x():
        return remote(
            g_own.at[pl.ds(2, 2), ny, 1 - nx, top], land_x2, two_sem.at[2], two_sem.at[3], (across, w)
        )

    def b1_copy(chip):
        slot = slot_of(chip, z)
        return remote(
            g_own.at[chip, :, :, rest], land_b1.at[slot], b1_send.at[slot], b1_recv.at[slot],
            (n, 2 * chip + c),
        )

    def a2_copy(chip):
        slot = slot_of(chip, z)
        return remote(
            g_own.at[chip, ny, nx, top], land_a2.at[slot], a2_send.at[slot], a2_recv.at[slot],
            (n, 2 * chip + c),
        )

    def b2_copy(other):
        slot = slot_of(other, n)
        return remote(
            g_own.at[z, other // 2, lax.rem(other, 2), rest], land_b2.at[slot], b2_send.at[slot],
            b2_recv.at[slot], (other, w),
        )

    def ag_copy(other):
        return remote(block, land_block.at[n], ag_send.at[slot_of(other, n)], ag_recv.at[n], (other, w))

    def core_finish():
        for t in range(4):
            wait_bytes(g_land.at[:, t // 2, t % 2, pl.ds(0, 192)], g_recv.at[t])
            wait_bytes(g_land.at[t, :, :, pl.ds(192, 192)], g_recv.at[4 + t])
        wait_bytes(g_land.at[:, :, :, pl.ds(384, 48)], g_recv.at[8])

        def add(i, carry):
            chip, y, x = i // 4, lax.rem(i // 2, 2), lax.rem(i, 2)
            g_own[chip, y, x] = (
                g_own[chip, y, x].astype(F32) + g_land[chip, y, x].astype(F32)
            ).astype(BF16)
            return carry

        lax.fori_loop(0, 16, add, 0)
        one_x().start()
        one_y().start()
        for chip in others(z):
            b1_copy(chip).start()

    def stage_two():
        one_x().wait_recv()
        one_y().wait_recv()
        for i in range(2):
            for k in range(2):
                g_own[i, k, nx, 0:CUT] = (
                    g_own[i, k, nx, 0:CUT].astype(F32) + land_x1[i, k].astype(F32)
                ).astype(BF16)
                g_own[2 + i, ny, k, 0:CUT] = (
                    g_own[2 + i, ny, k, 0:CUT].astype(F32) + land_y1[i, k].astype(F32)
                ).astype(BF16)
        two_y().start()
        two_x().start()

    def stage_a2():
        two_y().wait_recv()
        two_x().wait_recv()
        for i in range(2):
            g_own[i, ny, nx, 0:CUT] = (
                g_own[i, ny, nx, 0:CUT].astype(F32) + land_y2[i].astype(F32)
            ).astype(BF16)
            g_own[2 + i, ny, nx, 0:CUT] = (
                g_own[2 + i, ny, nx, 0:CUT].astype(F32) + land_x2[i].astype(F32)
            ).astype(BF16)
        for chip in others(z):
            a2_copy(chip).start()

    def stage_b2():
        for slot in range(3):
            wait_bytes(land_b1.at[slot], b1_recv.at[slot])
        for part in range(4):
            total = g_own[z, part // 2, part % 2, CUT:ROWS_G].astype(F32)
            for slot in range(3):
                total = total + land_b1[slot, part // 2, part % 2].astype(F32)
            g_own[z, part // 2, part % 2, CUT:ROWS_G] = total.astype(BF16)
        for other in others(n):
            b2_copy(other).start()

    def last():
        for slot in range(3):
            wait_bytes(land_a2.at[slot], a2_recv.at[slot])
            wait_bytes(land_b2.at[slot], b2_recv.at[slot])
        upper = g_own[z, ny, nx, 0:CUT].astype(F32)
        lower = g_own[z, ny, nx, CUT:ROWS_G].astype(F32)
        for slot in range(3):
            upper = upper + land_a2[slot].astype(F32)
            lower = lower + land_b2[slot].astype(F32)
        block[0:CUT] = upper.astype(BF16)
        block[CUT:ROWS_G] = lower.astype(BF16)
        for other in others(n):
            ag_copy(other).start()


    bufs_q = ((gq_a, land_qx_a, land_qz_a, land_q_a), (gq_b, land_qx_b, land_qz_b, land_q_b))

    def qx_copy(p):
        gq, land_x, _, _ = bufs_q[p]
        return remote(gq.at[:, 1 - nx], land_x, qx_sem.at[p, 0], qx_sem.at[p, 1], (across, w))

    def qz_copy(p, chip):
        gq, _, land_z, _ = bufs_q[p]
        slot = slot_of(chip, z)
        return remote(
            gq.at[chip, nx], land_z.at[slot], qz_send.at[p, slot], qz_recv.at[p, slot],
            (n, 2 * chip + c),
        )

    def qp_copy(p, other):
        gq, _, _, land = bufs_q[p]
        is_self = jnp.logical_and(other == n, nx == c)
        return (
            is_self, gq.at[z, nx], land.at[group], qp_send.at[p, other], qp_recv.at[p, group],
            (other, 2 * z + nx),
        )

    def q_z(p):
        gq, land_x, _, _ = bufs_q[p]
        qx_copy(p).wait_recv()
        for chip in range(4):
            gq[chip, nx] = (gq[chip, nx].astype(F32) + land_x[chip].astype(F32)).astype(BF16)
        for chip in others(z):
            qz_copy(p, chip).start()

    def q_plane(p):
        gq, _, land_z, _ = bufs_q[p]
        for slot in range(3):
            wait_bytes(land_z.at[slot], qz_recv.at[p, slot])
        total = gq[z, nx].astype(F32)
        for slot in range(3):
            total = total + land_z[slot].astype(F32)
        gq[z, nx] = total.astype(BF16)
        for other in range(4):
            send_or_keep(*qp_copy(p, other))


    def s1_copy(other):
        return remote(
            pack.at[pl.ds(2 * other, 2)], land_s1.at[n], s1_send.at[slot_of(other, n)],
            s1_recv.at[n], (other, w),
        )

    def gc_copy(other):
        return remote(
            gc_mine, land_gc.at[n], gc_send.at[slot_of(other, n)], gc_recv.at[n], (other, w)
        )

    def s2_copy(index):
        i, other = index // 4, lax.rem(index, 4)
        is_self = jnp.logical_and(other == n, w == 2 * n + i)
        return (
            is_self, pack_sum.at[i], land_s2.at[w], s2_send.at[index], s2_recv.at[w],
            (other, 2 * n + i),
        )

    def small_part(w_ada_ref, pieces_now):

        two = docs_ref[0] == DOCS
        even_rows = lax.rem(lax.broadcasted_iota(jnp.int32, (8, D), 0), 2) == 0

        def even_odd(values):
            even = jnp.sum(jnp.where(even_rows, values, 0.0), axis=0, keepdims=True)
            return even, jnp.sum(jnp.where(even_rows, 0.0, values), axis=0, keepdims=True)


        def put(chunk, row, values, s):
            pack[chunk, row : row + 1, 0:96] = values[:, 96 * s : 96 * s + 96]

        raws = [
            small_one[:, 0:D],
            small_one[:, D : 2 * D],
            small_ref[:, 0:D],
            small_ref[:, D : 2 * D],
            small_ref[:, 2 * D : 3 * D],
            small_ref[:, 3 * D : 4 * D],
        ]
        gains = {1: gain_one_ref, 4: gain_ref}
        for piece in pieces_now:
            even, odd = even_odd(raws[piece])
            if piece in gains:
                scale = pat_ref[:, piece * D : (piece + 1) * D]
                gain_sum = even * (1.0 + scale[0:1]) + odd * (1.0 + scale[1:2])
                for s in range(8):
                    put(s, 12 if piece == 1 else 13, gain_sum, s)
                gain = row_of(gains[piece])
                even, odd = even * gain, odd * gain
            first_doc = jnp.where(two, even, even + odd)
            second_doc = jnp.where(two, odd, 0.0)
            for s in range(8):
                at = 8 * piece + s
                put(at // 6, at % 6, first_doc, s)
                put(at // 6, 6 + at % 6, second_doc, s)
            terms = [*split3(first_doc), *split3(second_doc)]
            stacked = jnp.concatenate([*terms, jnp.zeros((10, D), F32)], axis=0).astype(BF16)
            part = dg(stacked, w_ada_ref[:, piece * D : (piece + 1) * D], NT)
            gc_mine[0:1] += part[0:1] + part[1:2] + part[2:3]
            gc_mine[1:2] += part[3:4] + part[4:5] + part[5:6]

    def small_early(w_ada_ref):
        pack[...] = jnp.zeros_like(pack)
        gc_mine[...] = jnp.zeros_like(gc_mine)
        small_part(w_ada_ref, (2, 3, 4, 5))
        for s in range(32):
            col = 4 * D + 96 * s
            row = jnp.sum(small_ref[:, col : col + 96], axis=0, keepdims=True)
            pack[s // 4, 14 + s % 4 : 15 + s % 4, 0:96] = row
        for s in range(8):
            col = 4 * D + FF + 96 * s
            pack[s, 18:19, 0:96] = jnp.sum(small_ref[:, col : col + 96], axis=0, keepdims=True)


    def small_sums(w_ada_ref):
        small_part(w_ada_ref, (0, 1))
        for other in others(n):
            s1_copy(other).start()
            gc_copy(other).start()
        last()
        land_gc[n] = gc_mine[...]
        land_s1[n] = pack[pl.ds(2 * n, 2)]
        for other in others(n):
            wait_bytes(land_s1.at[other], s1_recv.at[other])
        total = land_s1[0] + land_s1[1] + land_s1[2] + land_s1[3]
        pack_sum[...] = total
        cond = cond_ref[...].astype(F32)
        for i in range(2):
            pack_sum[i, 19:21, :] = cond

        for index in range(8):
            send_or_keep(*s2_copy(index))


    def heads(
        q_ref, k_ref, v_ref, all_ref, own_ref, tab_ref, w_ada_ref, packed, acc_k, acc_v, acc_w, kept, csend
    ):
        def c_copy(quarter):
            return remote(
                csend.at[quarter], cland.at[quarter], c_send.at[quarter], c_recv.at[quarter],
                sibling(n, z, c),
            )

        def r_copy(quarter):
            is_self = jnp.logical_and(quarter == n, nx == c)
            return (
                is_self,
                csend.at[quarter],
                rland.at[ny, pl.ds(pl.multiple_of(c * half, half), half)],
                r_send.at[quarter],
                r_recv.at[ny, c],
                (quarter, 2 * z + nx),
            )

        loads = [
            pltpu.make_async_copy(src, dst, load_sem.at[i])
            for i, (src, dst) in enumerate(
                (
                    (q_hbm, q_ref),
                    (k_hbm, k_ref),
                    (v_hbm, v_ref),
                    (tab_hbm, tab_ref),
                    (all_hbm, all_ref),
                    (own_hbm, own_ref),
                    (w_ada_hbm, w_ada_ref),
                )
            )
        ]
        for load in loads:
            load.start()
        core_finish()
        for load in loads[:4]:
            load.wait()
        lanes_h = lane((half, 128))
        lanes = lane((local, 128))

        def turned(values, rows):
            cosine, sine = cos_sin(tab_ref[rows, :])
            return values * cosine - halves_turn(values) * sine

        def rounded(values):
            return values.astype(BF16).astype(F32)

        def weights(p):
            gq = bufs_q[p][0]
            at, width = PARTS_Q[p]
            if p == 0:
                loads[4].wait()
            acc_w[:, 0:width] = dg(all_ref[0:local, :], packed[0:local, at : at + width], TN)

            def step(i, carry):
                rows = pl.ds(pl.multiple_of(i * local, local), local)
                acc_w[:, 0:width] += dg(all_ref[rows, :], packed[rows, at : at + width], TN)
                return carry

            lax.fori_loop(1, 4, step, 0)
            gq[...] = acc_w[:, 0:width].astype(BF16).reshape(gq.shape)
            qx_copy(p).start()

        hooks = {(1, 6): stage_two, (2, 4): stage_a2, (2, 5): stage_b2, (2, 7): lambda: q_z(0)}
        for j in range(OWN):
            for quarter in range(4):
                wait_bytes(dland.at[j, quarter], d_recv.at[j, quarter])
            acc_k[...] = jnp.zeros_like(acc_k)
            acc_v[...] = jnp.zeros_like(acc_v)

            def step(i, carry):
                for (at_j, at_i), hook in hooks.items():
                    if at_j == j:
                        pl.when(i == at_i)(hook)
                rows = pl.ds(pl.multiple_of(i * half, half), half)
                grad = pltpu.roll(dland[j, i // 2].astype(F32), lax.rem(i, 2) * 64, 1)
                grad = jnp.where(lanes_h < 64, grad, 0.0).astype(BF16)
                query = q_ref[j, rows, :]
                probs = jnp.exp2(dg(query, k_ref[j], NT) * LOG2E)
                gprobs = probs * dg(grad, v_ref[j], NT)
                scores = (gprobs - probs * jnp.sum(gprobs, axis=1, keepdims=True)).astype(BF16)
                probs = probs.astype(BF16)
                gquery = rounded(dg(scores, k_ref[j], NN) * HEAD_DIM**-0.5)
                packed[rows, Q_AT[j] : Q_AT[j] + 64] = turned(gquery, rows)[:, :64].astype(BF16)
                acc_v[...] += dg(grad.T[:64], probs, NN)
                acc_k[...] += dg(query.T[:64], scores, NN)
                return carry

            lax.fori_loop(0, 8, step, 0)

            def finish(i, carry):
                rows = pl.ds(pl.multiple_of(i * local, local), local)
                both = rounded(jnp.concatenate([acc_k[:, rows], acc_v[:, rows]], axis=0).T)
                packed[rows, KV_AT[j] : KV_AT[j] + 128] = jnp.where(
                    lanes < 64, turned(both, rows), both
                ).astype(BF16)
                return carry

            lax.fori_loop(0, 4, finish, 0)
            if j == 1:
                weights(0)
        packed[:, 576:640] = jnp.zeros((length, 64), BF16)

        def rows_of(quarter, hh):
            return pl.ds(pl.multiple_of(quarter * local + hh * half, half), half)

        def order(i):
            return lax.rem(n + 3 - i, 4)

        loads[5].wait()

        def give(i, carry):
            quarter = order(i)
            csend[quarter] = dg(packed[rows_of(quarter, 1 - c), :], own_ref[...], NT).astype(BF16)
            c_copy(quarter).start()
            return carry

        lax.fori_loop(0, 4, give, 0)

        def keep(i, carry):
            quarter = order(i)
            kept[quarter] = dg(packed[rows_of(quarter, c), :], own_ref[...], NT)
            return carry

        lax.fori_loop(0, 4, keep, 0)

        def add(i, carry):
            quarter = order(i)
            c_copy(quarter).wait()
            csend[quarter] = (kept[quarter] + cland[quarter].astype(F32)).astype(BF16)
            send_or_keep(*r_copy(quarter))
            return carry

        lax.fori_loop(0, 4, add, 0)
        weights(1)
        loads[6].wait()
        small_early(w_ada_ref)
        normed, inv = norm_stats(tokens_ref[...].astype(F32))
        q_plane(0)
        q_z(1)

        for y in range(2):
            for hh in range(2):
                wait_bytes(rland.at[y, pl.ds(hh * half, half)], r_recv.at[y, hh])
        gfirst = rland[0].astype(F32) + rland[1].astype(F32)
        small_one[:, 0:D] = sum8(gfirst)
        small_one[:, D : 2 * D] = sum8(gfirst * normed)
        grad = spread(gfirst, row_of(gain_one_ref) * (1.0 + piece(1)))
        mean = jnp.mean(grad, axis=-1, keepdims=True)
        along = jnp.mean(grad * normed, axis=-1, keepdims=True)
        gtok_ref[...] += (grad - mean - normed * along) * inv
        small_sums(w_ada_ref)

        q_plane(1)
        for quarter in range(4):
            wait_send_unless(*r_copy(quarter))

    pl.run_scoped(
        heads,
        VMEM((OWN, length, 128), BF16),
        VMEM((OWN, length, 128), BF16),
        VMEM((OWN, length, 128), BF16),
        VMEM((length, D), BF16),
        VMEM((D, WCOLS), BF16),
        VMEM((length, 128), F32),
        VMEM(w_ada_hbm.shape, BF16),
        VMEM((length, WCOLS), BF16),
        VMEM((64, length), F32),
        VMEM((64, length), F32),
        VMEM((D, 384), F32),
        VMEM((4, half, D), F32),
        VMEM((4, half, D), BF16),
    )

    for other in others(n):
        wait_bytes(land_gc.at[other], gc_recv.at[other])
    gcond_ref[...] = land_gc[0] + land_gc[1] + land_gc[2] + land_gc[3]
    for row in range(8):
        wait_bytes(land_s2.at[row], s2_recv.at[row])
    packet_ref[...] = land_s2[...]
    land_block[n] = block[...]
    for other in others(n):
        wait_bytes(land_block.at[other], ag_recv.at[other])
    move = pltpu.make_async_copy(land_block, blocks_ref, load_sem.at[0])
    move.start()
    for p in range(2):
        for g in range(4):
            wait_bytes(bufs_q[p][3].at[g], qp_recv.at[p, g])
    moves = [
        move,
        pltpu.make_async_copy(land_q_a, qkv_a_ref, load_sem.at[1]),
        pltpu.make_async_copy(land_q_b, qkv_b_ref, load_sem.at[2]),
    ]
    for later in moves[1:]:
        later.start()


    for later in moves:
        later.wait()
    for head in range(HEADS):
        wait_send_unless(*d_copy(head))
    for copy in (one_x(), one_y(), two_x(), two_y(), qx_copy(0), qx_copy(1)):
        copy.wait_send()

    def drain(quarter, carry):
        for p in range(2):
            wait_send_unless(*qp_copy(p, quarter))
        return carry

    lax.fori_loop(0, 4, drain, 0)
    for i in range(3):
        other, chip = others(n)[i], others(z)[i]
        b1_copy(chip).wait_send()
        a2_copy(chip).wait_send()
        b2_copy(other).wait_send()
        ag_copy(other).wait_send()
        qz_copy(0, chip).wait_send()
        qz_copy(1, chip).wait_send()
        s1_copy(other).wait_send()
        gc_copy(other).wait_send()
    for index in range(8):
        wait_send_unless(*s2_copy(index))


def call_fused(
    docs, tokens, cot, att, cond, pat, gain_one, gain_two, b_up, b_down, w_ada, w_out, w_up, w_down,
    q, k, v, everything, own, tab,
):
    local = tokens.shape[0]
    half = local // 2
    sds = jax.ShapeDtypeStruct
    rest = ROWS_G - CUT
    wide_a, wide_b = PARTS_Q[0][1], PARTS_Q[1][1]

    def low(*shape):
        return VMEM(shape, BF16)

    return pl.pallas_call(
        fused_kernel,
        out_shape=(
            sds((local, D), BF16),
            sds((local, D), F32),
            sds((4, ROWS_G, COLS_G), BF16),
            sds((4, 96, wide_a), BF16),
            sds((4, 96, wide_b), BF16),
            sds((8, CHUNK, 128), F32),
            sds((8, 128), F32),
        ),
        in_specs=[smem()] + [vm()] * 9 + [hbm()] * 10,
        out_specs=(vm(), vm(), hbm(), hbm(), hbm(), vm(), vm()),
        scratch_shapes=[
            VMEM((8, SMALL), F32),
            VMEM((8, 2 * D), F32),
            low(HEADS, half, 128),
            low(OWN, 4, half, 128),
            low(4, 2, 2, ROWS_G, COLS_G),
            low(4, 2, 2, ROWS_G, COLS_G),
            low(2, 2, CUT, COLS_G),
            low(2, 2, CUT, COLS_G),
            low(2, CUT, COLS_G),
            low(2, CUT, COLS_G),
            low(3, 2, 2, rest, COLS_G),
            low(3, CUT, COLS_G),
            low(3, rest, COLS_G),
            low(ROWS_G, COLS_G),
            low(4, ROWS_G, COLS_G),
            low(4, half, D),
            low(2, local, D),
            low(4, 2, 96, wide_a),
            low(4, 2, 96, wide_b),
            low(4, 96, wide_a),
            low(4, 96, wide_b),
            low(3, 96, wide_a),
            low(3, 96, wide_b),
            low(4, 96, wide_a),
            low(4, 96, wide_b),
            VMEM((8, CHUNK, 128), F32),
            VMEM((4, 2, CHUNK, 128), F32),
            VMEM((2, CHUNK, 128), F32),
            VMEM((8, CHUNK, 128), F32),
            VMEM((8, 128), F32),
            VMEM((4, 8, 128), F32),
            dma(7),
            dma(HEADS),
            dma(OWN, 4),
            dma(9),
            dma(9),
            dma(4),
            dma(4),
            dma(3),
            dma(3),
            dma(3),
            dma(3),
            dma(3),
            dma(3),
            dma(3),
            dma(4),
            dma(4),
            dma(4),
            dma(4),
            dma(2, 2),
            dma(2, 2),
            dma(2, 3),
            dma(2, 3),
            dma(2, 4),
            dma(2, 4),
            dma(3),
            dma(4),
            dma(8),
            dma(8),
            dma(3),
            dma(4),
        ],
        compiler_params=params(3, 63),
        cost_estimate=pl.CostEstimate(flops=4 * 10**10, bytes_accessed=5 * 10**7, transcendentals=10**7),
    )(
        docs, tokens, cot, att, cond, pat, gain_one, gain_two, b_up, b_down, w_ada, w_out, w_up, w_down,
        q, k, v, everything, own, tab,
    )


def finish_kernel(
    output_in, gtok_in, blocks, qkv_a, qkv_b, packet, gcond_in, output_out, gtok_out, gcond_out, gqkv_out, gout_out, gup_out, gdown_out, gada_out, gvec_ada,
    gvec_one, gvec_two, gvec_up, gvec_down, wide, pass_sem, gqkv, gout, gup, gdown, gada, send_sem
):
    passed = [
        pltpu.make_async_copy(output_in, output_out, pass_sem.at[0]),
        pltpu.make_async_copy(gtok_in, gtok_out, pass_sem.at[1]),
    ]
    for copy in passed:
        copy.start()
    gcond_out[0] = gcond_in[0:DOCS]
    sends = [
        pltpu.make_async_copy(src, dst, send_sem.at[i])
        for i, (src, dst) in enumerate(
            ((gup, gup_out), (gout, gout_out), (gdown, gdown_out), (gqkv, gqkv_out), (gada, gada_out))
        )
    ]
    for part in range(4):
        for hh in range(2):
            at = part * 768 + hh * 384
            gup[:, at : at + 384] = blocks[part, hh * 96 : (hh + 1) * 96, :].astype(F32)
        rh, ch = part // 2, part % 2
        gout[rh * 48 : (rh + 1) * 48, ch * 384 : (ch + 1) * 384] = blocks[part, 384:432, :].astype(F32)
    sends[0].start()
    sends[1].start()
    for pair in range(2):
        both = jnp.concatenate(
            [blocks[2 * pair, 192:384, :], blocks[2 * pair + 1, 192:384, :]], axis=0
        ).astype(F32)
        gdown[:, pair * 384 : (pair + 1) * 384] = both.T

    sends[2].start()

    def head_block(part, head):
        g, j = head // OWN, head % OWN
        if part == 0:
            at, upper = Q_AT[j] // 128 * 128, j % 2
        else:
            at, upper = KV_AT[j], part - 1
        qkv, start = (qkv_a, 0) if at < PARTS_Q[1][0] else (qkv_b, PARTS_Q[1][0])
        return qkv[g, :, at - start : at - start + 128].astype(F32), upper

    for part in range(3):
        for pair in range(HEADS // 2):
            even, up = head_block(part, 2 * pair)
            even = pltpu.roll(even, 64, 1) if up else even
            odd, up = head_block(part, 2 * pair + 1)
            odd = odd if up else pltpu.roll(odd, 64, 1)
            at = part * D + pair * 128
            gqkv[:, at : at + 128] = jnp.where(lane(even.shape) < 64, even, odd)

    sends[3].start()
    conds = [packet[:, 19, :], packet[:, 20, :]]
    lhs = jnp.concatenate([conds[0]] * 3 + [conds[1]] * 3, axis=0).astype(BF16)
    for k in range(6):
        first, second = packet[:, k, :], packet[:, 6 + k, :]
        rhs = jnp.concatenate([*split3(first), *split3(second)], axis=0).astype(BF16)
        gada[96 * k : 96 * k + 96, :] = dg(rhs, lhs, TN)[:96]
        wide[0:1, 96 * k : 96 * k + 96] = jnp.sum(first + second, axis=0, keepdims=True)[:, :96]
    for row, at, k in ((1, 0, 12), (2, 0, 13), (3, 0, 14), (3, 1, 15), (3, 2, 16), (3, 3, 17), (4, 0, 18)):
        wide[row : row + 1, 96 * at : 96 * at + 96] = jnp.sum(packet[:, k, :], axis=0, keepdims=True)[
            :, :96
        ]
    sends[4].start()
    for ref, row in ((gvec_ada, 0), (gvec_one, 1), (gvec_two, 2), (gvec_up, 3), (gvec_down, 4)):
        ref[...] = wide[row : row + 1, 0 : ref.shape[0]].reshape(ref.shape)
    for copy in passed + sends:
        copy.wait()


def call_finish(output, gtok, blocks, qkv_a, qkv_b, packet, gcond):
    local = output.shape[0]
    sds = jax.ShapeDtypeStruct
    return pl.pallas_call(
        finish_kernel,
        out_shape=(
            sds((local, D), BF16),
            sds((local, D), F32),
            sds((1, DOCS, 128), F32),
            sds((96, 3 * D), F32),
            sds((96, D), F32),
            sds((96, FF), F32),
            sds((384, D), F32),
            sds((576, 128), F32),
            sds((576,), F32),
            sds((96,), F32),
            sds((96,), F32),
            sds((384,), F32),
            sds((96,), F32),
        ),
        in_specs=[vm()] * 7,
        out_specs=(hbm(), hbm(), vm()) + (hbm(),) * 5 + (vm(),) * 5,
        scratch_shapes=[
            VMEM((8, 576), F32),
            dma(2),
            VMEM((96, 3 * D), F32),
            VMEM((96, D), F32),
            VMEM((96, FF), F32),
            VMEM((384, D), F32),
            VMEM((576, 128), F32),
            dma(5),
        ],
        compiler_params=pltpu.CompilerParams(vmem_limit_bytes=62 * 2**20),
        cost_estimate=pl.CostEstimate(flops=10**7, bytes_accessed=10**7, transcendentals=0),
    )(output, gtok, blocks, qkv_a, qkv_b, packet, gcond)


def plain_backward_kernel(
    tokens_ref,
    pat_ref,
    gain_ref,
    gmid_ref,
    do_ref,
    q_ref,
    k_ref,
    v_ref,
    all_ref,
    own_ref,
    tab_ref,
    gtok_ref,
    gq_ref,
    small_ref,
    packed,
    acc_k,
    acc_v,
    acc_w,
    kept,
    csend,
    cland,
    rsend,
    rland,
    c_send,
    c_recv,
    r_send,
    r_recv,
):
    n, ny, nx, z, c = place()
    local = tokens_ref.shape[0]
    half = local // 2
    length = 4 * local
    plane_barrier(n, z, c)
    lanes = lane((local, 128))

    def turned(values, rows):
        cosine, sine = cos_sin(tab_ref[rows, :])
        return values * cosine - halves_turn(values) * sine

    def rounded(values):
        return values.astype(BF16).astype(F32)

    for j in range(OWN):
        acc_k[...] = jnp.zeros_like(acc_k)
        acc_v[...] = jnp.zeros_like(acc_v)

        def quarter_step(i, carry):
            rows = pl.ds(pl.multiple_of(i * local, local), local)
            block = do_ref[j, i].astype(F32)
            grad = jnp.concatenate([block, pltpu.roll(block, 64, 1)], axis=0)
            grad = jnp.where(lanes < 64, grad, 0.0).astype(BF16)
            query = q_ref[j, rows, :]
            probs = jnp.exp2(dg(query, k_ref[j], NT) * LOG2E)
            gprobs = probs * dg(grad, v_ref[j], NT)
            scores = (gprobs - probs * jnp.sum(gprobs, axis=1, keepdims=True)).astype(BF16)
            probs = probs.astype(BF16)
            gquery = rounded(dg(scores, k_ref[j], NN) * HEAD_DIM**-0.5)
            at = Q_AT[j]
            packed[rows, at : at + 64] = turned(gquery, rows)[:, :64].astype(BF16)
            acc_v[...] += dg(grad.T[:64], probs, NN)
            acc_k[...] += dg(query.T[:64], scores, NN)
            return carry

        lax.fori_loop(0, 4, quarter_step, 0)

        def finish(i, carry):
            rows = pl.ds(pl.multiple_of(i * local, local), local)
            both = jnp.concatenate([acc_k[:, rows], acc_v[:, rows]], axis=0).T
            both = rounded(both)
            packed[rows, KV_AT[j] : KV_AT[j] + 128] = jnp.where(
                lanes < 64, turned(both, rows), both
            ).astype(BF16)
            return carry

        lax.fori_loop(0, 4, finish, 0)
    packed[:, 576:640] = jnp.zeros((length, 64), BF16)

    def rows_of(quarter, hh):
        return pl.ds(pl.multiple_of(quarter * local + hh * half, half), half)

    def c_copy(quarter):
        return remote(
            csend.at[quarter], cland.at[quarter], c_send.at[quarter], c_recv.at[quarter],
            sibling(n, z, c),
        )

    def r_copy(quarter):
        is_self = jnp.logical_and(quarter == n, nx == c)
        return (
            is_self,
            rsend.at[quarter],
            rland.at[ny, pl.ds(pl.multiple_of(c * half, half), half)],
            r_send.at[quarter],
            r_recv.at[ny, c],
            (quarter, 2 * z + nx),
        )

    def order(i):
        return lax.rem(n + 3 - i, 4)

    def give(i, carry):
        quarter = order(i)
        csend[quarter] = dg(packed[rows_of(quarter, 1 - c), :], own_ref[...], NT).astype(BF16)
        c_copy(quarter).start()
        return carry

    lax.fori_loop(0, 4, give, 0)

    def keep(i, carry):
        quarter = order(i)
        kept[quarter] = dg(packed[rows_of(quarter, c), :], own_ref[...], NT)
        return carry

    lax.fori_loop(0, 4, keep, 0)

    def add(i, carry):
        quarter = order(i)
        wait_bytes(cland.at[quarter], c_recv.at[quarter])
        rsend[quarter] = (kept[quarter] + cland[quarter].astype(F32)).astype(BF16)
        send_or_keep(*r_copy(quarter))
        return carry

    lax.fori_loop(0, 4, add, 0)

    acc_w[...] = jnp.zeros_like(acc_w)

    def weights(i, carry):
        rows = pl.ds(pl.multiple_of(i * local, local), local)
        acc_w[...] += dg(all_ref[rows, :], packed[rows, :], TN)
        return carry

    lax.fori_loop(0, 4, weights, 0)
    gq_ref[...] = acc_w[...].astype(BF16).reshape(gq_ref.shape)

    normed, inv = norm_stats(tokens_ref[...].astype(F32))
    for y in range(2):
        for hh in range(2):
            wait_bytes(rland.at[y, pl.ds(hh * half, half)], r_recv.at[y, hh])
    gfirst = rland[0].astype(F32) + rland[1].astype(F32)
    small_ref[:, 0:D] = sum8(gfirst)
    small_ref[:, D : 2 * D] = sum8(gfirst * normed)
    amp = row_of(gain_ref) * (1.0 + pat_ref[:, D : 2 * D])
    grad = flat8(by8(gfirst) * amp[None])
    mean = jnp.mean(grad, axis=-1, keepdims=True)
    along = jnp.mean(grad * normed, axis=-1, keepdims=True)
    gtok_ref[...] = gmid_ref[...] + (grad - mean - normed * along) * inv

    def drain(quarter, carry):
        c_copy(quarter).wait_send()
        wait_send_unless(*r_copy(quarter))
        return carry

    lax.fori_loop(0, 4, drain, 0)


def call_plain_backward(tokens, pat, gain, gmid, do, q, k, v, everything, own, tab):
    local = tokens.shape[0]
    half = local // 2
    length = 4 * local
    sds = jax.ShapeDtypeStruct
    return pl.pallas_call(
        plain_backward_kernel,
        out_shape=(
            sds((local, D), F32),
            sds((8, 96, WCOLS), BF16),
            sds((8, 2 * D), F32),
        ),
        in_specs=[vm()] * 11,
        out_specs=(vm(),) * 3,
        scratch_shapes=[
            VMEM((length, WCOLS), BF16),
            VMEM((64, length), F32),
            VMEM((64, length), F32),
            VMEM((D, WCOLS), F32),
            VMEM((4, half, D), F32),
            VMEM((4, half, D), BF16),
            VMEM((4, half, D), BF16),
            VMEM((4, half, D), BF16),
            VMEM((2, local, D), BF16),
            dma(4),
            dma(4),
            dma(4),
            dma(2, 2),
        ],
        compiler_params=params(2, 60),
        cost_estimate=pl.CostEstimate(flops=2 * 10**10, bytes_accessed=3 * 10**7, transcendentals=10**7),
    )(tokens, pat, gain, gmid, do, q, k, v, everything, own, tab)


def plain_sums(g, gq, own_ids):
    n, z, c = own_ids
    up = g[:, :, :192].reshape(8, 4, 2, 96, 384).transpose(0, 3, 1, 2, 4).reshape(D, FF)
    down = g[:, :, 192:384].reshape(8, D, 384).transpose(0, 2, 1).reshape(FF, D)
    out = g[:, :, 384:].reshape(8, 2, 2, 48, 384).transpose(0, 1, 3, 2, 4).reshape(D, D)
    flat = gq.reshape(D, WCOLS)
    pieces = []
    for starts in (Q_AT, KV_AT, [at + HEAD_DIM for at in KV_AT]):
        pieces.append(jnp.concatenate([flat[:, at : at + HEAD_DIM] for at in starts], axis=1))
    group = 2 * (n // 2) + c
    whole = jnp.zeros((D, 3, 4, OWN * HEAD_DIM), F32)
    for part in range(3):
        whole = lax.dynamic_update_slice(
            whole, pieces[part].astype(F32)[:, None, None, :], (0, part, group, 0)
        )
    whole = whole.reshape(D, 3 * D)

    def total(values):
        share = lax.psum_scatter(values.astype(F32), "wide", scatter_dimension=0, tiled=True)
        return lax.psum(share, "narrow")

    return total(whole), total(out), total(up), total(down)


def body(
    tokens,
    condition,
    docs_per_row,
    w_ada,
    b_ada,
    gain_one,
    w_qkv,
    w_out,
    gain_two,
    w_up,
    b_up,
    w_down,
    b_down,
    cotangent,
):
    local = tokens.shape[1]
    x = tokens.reshape(local, D)
    cot = cotangent.reshape(local, D)
    cond = condition.reshape(DOCS, -1)
    table = jnp.asarray(rotary_table(4 * local))

    att, everything, q, k, v, pat, own, tab = call_forward(
        docs_per_row, x, cond, w_ada, b_ada, gain_one, w_qkv, table
    )
    if (lax.axis_size("narrow"), lax.axis_size("wide")) == (4, 8):
        output, gtok, blocks, qkv_a, qkv_b, packet, gcond = call_fused(
            docs_per_row, x, cot, att, cond, pat, gain_one, gain_two, b_up,
            b_down, w_ada, w_out, w_up, w_down, q, k, v, everything, own, tab,
        )
        output, gtok, gcond, gqkv, gout, gup, gdown, gada, *vectors = call_finish(
            output, gtok, blocks, qkv_a, qkv_b, packet, gcond
        )
        gvec_ada, gvec_one, gvec_two, gvec_up, gvec_down = vectors
        return (
            output[None],
            gtok[None],
            gcond,
            gada.T,
            gvec_ada,
            gvec_one,
            gqkv,
            gout,
            gvec_two,
            gup,
            gvec_up,
            gdown,
            gvec_down,
        )

    output, gmid, g, small_two, do = call_middle(
        x, cot, att, pat, gain_two, w_out, w_up, b_up, w_down, b_down
    )
    gtok, gq, small_one = call_plain_backward(
        x, pat, gain_one, gmid, do, q, k, v, everything, own, tab
    )
    n, w = lax.axis_index("narrow"), lax.axis_index("wide")
    sum_qkv, sum_out, sum_up, sum_down = plain_sums(g, gq, (n, w // 2, w % 2))

    small = jnp.concatenate([small_one, small_two], axis=1).reshape(4, 2, -1).sum(0)
    small = lax.psum(small, "narrow")
    shift_one, raw_one, gate_one, shift_two, raw_two, gate_two = jnp.split(small[:, : 6 * D], 6, axis=1)
    scales = pat[:2].reshape(2, 6, D)
    sum_gain_one = jnp.sum(raw_one * (1.0 + scales[:, 1]), axis=0)
    sum_gain_two = jnp.sum(raw_two * (1.0 + scales[:, 4]), axis=0)
    grads = jnp.concatenate(
        [
            shift_one,
            raw_one * gain_one.astype(F32),
            gate_one,
            shift_two,
            raw_two * gain_two.astype(F32),
            gate_two,
        ],
        axis=1,
    )
    two = docs_per_row[0] == DOCS
    grad_mods = jnp.stack(
        [jnp.where(two, grads[0], grads[0] + grads[1]), jnp.where(two, grads[1], 0.0)]
    )
    high = lax.Precision.HIGHEST
    grad_condition = jnp.einsum("sm,cm->sc", grad_mods, w_ada.astype(F32), precision=high)[None]
    part_ada = jnp.einsum("sm,sc->mc", grad_mods, cond.astype(F32), precision=high)

    def share(values):
        return lax.psum_scatter(values, "wide", scatter_dimension=0, tiled=True)

    sum_b_up = jnp.sum(small[:, 6 * D : 6 * D + FF], axis=0)
    sum_b_down = jnp.sum(small[:, 6 * D + FF :], axis=0)
    return (
        output[None],
        gtok[None],
        grad_condition,
        share(part_ada).T,
        share(jnp.sum(grad_mods, axis=0)),
        share(sum_gain_one),
        sum_qkv,
        sum_out,
        share(sum_gain_two),
        sum_up,
        share(sum_b_up),
        sum_down,
        share(sum_b_down),
    )


def solution(mesh):
    in_specs = (
        P("wide", "narrow", None),
        P("wide", None, None),
        P("wide"),
        P(),
        P(),
        P(),
        P(),
        P(),
        P(),
        P(),
        P(),
        P(),
        P(),
        P("wide", "narrow", None),
    )
    out_specs = (
        P("wide", "narrow", None),
        P("wide", "narrow", None),
        P("wide", None, None),
        P(None, "wide"),
        P("wide"),
        P("wide"),
        P("wide", None),
        P("wide", None),
        P("wide"),
        P("wide", None),
        P("wide"),
        P("wide", None),
        P("wide"),
    )
    return jax.shard_map(body, mesh=mesh, in_specs=in_specs, out_specs=out_specs, check_vma=False)
```
